32 devices in a mesh: dp: 8 (over y, x, core), fsdp: 4 (over z).
Axes of the slice: x: 2, y: 2, z: 4, core: 2. Of those that a mesh axis runs over, the one named last changes fastest.
Arguments:
- tokens: bfloat16 [38400, 768], P(('dp', 'fsdp')), may hold values from -6 to 6
- image_sides: int32 [64, 3], P(('dp', 'fsdp')), may hold values from 0 to 24, as said below
- out_grad: bfloat16 [38400, 768], P(('dp', 'fsdp')), may hold values from -6 to 6
- attn_norm: bfloat16 [2, 768], P(None, ('dp', 'fsdp'))
- qkv_weight: bfloat16 [768, 2304], P(('dp', 'fsdp')), may hold values from -0.21875 to 0.21875
- qkv_bias: bfloat16 [2304], P(('dp', 'fsdp')), may hold values from -4 to 4
- out_weight: bfloat16 [768, 768], P(('dp', 'fsdp')), may hold values from -1.75 to 1.75
- out_bias: bfloat16 [768], P(('dp', 'fsdp')), may hold values from -4 to 4
- frequencies: bfloat16 [768], P(('dp', 'fsdp')), may hold values from -1 to 1
- mlp_norm: bfloat16 [2, 768], P(None, ('dp', 'fsdp'))
- up_weight: bfloat16 [768, 3072], P(('dp', 'fsdp')), may hold values from -0.21875 to 0.21875
- up_bias: bfloat16 [3072], P(('dp', 'fsdp')), may hold values from -4 to 4
- down_weight: bfloat16 [3072, 768], P(None, ('dp', 'fsdp')), may hold values from -0.15625 to 0.15625
- down_bias: bfloat16 [768], P(('dp', 'fsdp')), may hold values from -4 to 4
Outputs:
- mixed_out: bfloat16 [38400, 768], P(('dp', 'fsdp'))
- token_grad: bfloat16 [38400, 768], P(('dp', 'fsdp'))
- attn_norm_grad: float32 [2, 768], P(None, ('dp', 'fsdp'))
- qkv_weight_grad: float32 [768, 2304], P(('dp', 'fsdp'))
- qkv_bias_grad: float32 [2304], P(('dp', 'fsdp'))
- out_weight_grad: float32 [768, 768], P(('dp', 'fsdp'))
- out_bias_grad: float32 [768], P(('dp', 'fsdp'))
- frequency_grad: float32 [768], P(('dp', 'fsdp'))
- mlp_norm_grad: float32 [2, 768], P(None, ('dp', 'fsdp'))
- up_weight_grad: float32 [768, 3072], P(('dp', 'fsdp'))
- up_bias_grad: float32 [3072], P(('dp', 'fsdp'))
- down_weight_grad: float32 [3072, 768], P(None, ('dp', 'fsdp'))
- down_bias_grad: float32 [768], P(('dp', 'fsdp'))
The draws below stay inside these ranges and needn't reach their ends.
Inputs may be any that keep to these rules, and one draw needn't show every extreme that they name: `image_sides`: each row is one of (24, 0, 0), (20, 14, 0), (14, 20, 0), (14, 14, 14), (20, 0, 0), (14, 14, 0); the first row is (24, 0, 0).
All inputs are finite; a program needn't handle non-finite values.
Results may differ from the reference program's by a relative error of at most 0.012.
Values may be sent and summed in bfloat16 or wider, within the bound.
A program may use at most 256 MiB of HBM per device.

```python
import jax
import jax.numpy as jnp
from jax import lax

D = 768
HEADS = 12
HD = 64
FF = 3072
SIDE_S = 14
SIDE_M = 20
SIDE_L = 24
CAP = 600
SLOTS = 64
TOKENS = 38400


def norm_table(key):
    first_key, second_key = jax.random.split(key)
    gain_row = 1.0 + 0.3 * jax.random.uniform(first_key, (D,), jnp.float32, -1.0, 1.0)
    shift_row = 0.3 * jax.random.normal(second_key, (D,), jnp.float32)
    return jnp.stack([gain_row, shift_row]).astype(jnp.bfloat16)


def draw_attn_norm(key, part):
    key = jax.random.fold_in(key, 11)
    return norm_table(key)


def draw_mlp_norm(key, part):
    key = jax.random.fold_in(key, 23)
    return norm_table(key)


def draw_image_sides(key, part):
    key = jax.random.fold_in(key, 37)
    table = jnp.array([[SIDE_L, 0, 0], [SIDE_M, SIDE_S, 0], [SIDE_S, SIDE_M, 0], [SIDE_S, SIDE_S, SIDE_S], [SIDE_M, 0, 0], [SIDE_S, SIDE_S, 0]], dtype=jnp.int32)
    pattern_ids = jax.random.randint(key, (SLOTS,), 0, 6)
    pattern_ids = pattern_ids.at[0].set(0)
    return table[pattern_ids]


def with_spikes(values, key, source, target, blocks, factor):
    def block_of(position):
        return (jnp.arange(values.shape[position]) // (values.shape[position] // blocks)).reshape((-1,) + (1,) * (values.ndim - 1 - position))

    near = jax.random.permutation(key, blocks)[block_of(target)]
    other_side = (block_of(target) + blocks // 2) % blocks
    return jnp.where((block_of(source) == near) | (block_of(source) == other_side), factor * values, values)


def steps_of(own_key, shape, shards, low, largest):
    loudness = 1.0
    for position, shards_of in shards:
        heights = jax.random.uniform(jax.random.fold_in(jax.random.fold_in(own_key, 6), position), (shards_of,), jnp.float32, low / len(shards), largest / len(shards))
        loudness = loudness * jnp.repeat(jnp.exp(heights), shape[position] // shards_of).reshape((-1,) + (1,) * (len(shape) - 1 - position))
    return loudness


def noise(stream_key, extent, deviation, limit, shards=(), kind=jnp.bfloat16):
    loudness = steps_of(stream_key, extent, shards, -0.22, 0.18) if shards else 1.0
    values = jax.random.normal(stream_key, extent, jnp.float32) * deviation * loudness
    return jnp.minimum(jnp.maximum(values, -limit), limit).astype(kind)


def gaussian_with(own_key, extent, width, most, cuts, heavy, kind=jnp.bfloat16):
    drawn = width * jax.random.normal(own_key, extent, jnp.float32)
    if cuts:
        drawn = drawn * steps_of(own_key, extent, cuts, -0.22, 0.18)
    return jnp.clip(with_spikes(drawn, jax.random.fold_in(own_key, 3), *heavy), -most, most).astype(kind)


def setup_inputs(seed: int = 0) -> dict:
    seeds = jax.random.split(jax.random.key(seed), 15)
    return {
        "tokens": noise(seeds[0], (TOKENS, D), 1.0, 6.0, ((0, 32),)),
        "image_sides": draw_image_sides(jax.random.fold_in(seeds[14], 71), 0),
        "out_grad": gaussian_with(seeds[2], (TOKENS, D), 1.0, 6.0, ((0, 32),), (0, 1, 32, 2.75)),
        "attn_norm": draw_attn_norm(jax.random.fold_in(seeds[14], 71), 0),
        "qkv_weight": noise(seeds[4], (D, 3 * D), D ** -0.5, 0.21875, ((0, 32),)),
        "qkv_bias": noise(seeds[5], (3 * D,), 0.3, 4.0, ((0, 32),)),
        "out_weight": noise(seeds[6], (D, D), (D // 64) ** -0.5, 1.75, ((0, 32),)),
        "out_bias": noise(seeds[7], (D,), 0.3, 4.0, ((0, 32),)),
        "frequencies": jnp.clip(jax.random.uniform(seeds[8], (D,), jnp.float32, -1.0, 1.0) * steps_of(seeds[8], (D,), ((0, 32),), -0.4, 0.0), -1.0, 1.0).astype(jnp.bfloat16),
        "mlp_norm": draw_mlp_norm(jax.random.fold_in(seeds[14], 71), 0),
        "up_weight": noise(seeds[10], (D, FF), D ** -0.5, 0.21875, ((0, 32),)),
        "up_bias": noise(seeds[11], (FF,), 0.3, 4.0, ((0, 32),)),
        "down_weight": noise(seeds[12], (FF, D), (FF // 2) ** -0.5, 0.15625, ((1, 32),)),
        "down_bias": noise(seeds[13], (D,), 0.3, 4.0, ((0, 32),)),
    }


@jax.custom_vjp
def low(v):
    return lax.optimization_barrier(v.astype(jnp.bfloat16)).astype(jnp.float32)

@jax.custom_vjp
def low_back(v):
    return v

def low_keep(v):
    return (low(v), None)

def low_pass(kept, grad):
    return (grad,)

def back_keep(v):
    return (v, None)

def back_low(kept, grad):
    return (low(grad),)
low.defvjp(low_keep, low_pass)
low_back.defvjp(back_keep, back_low)
highest = lax.Precision.HIGHEST
norm_eps = 1e-06
score_scale = 0.125

def layer_norm(values, gain_row, shift_row):
    average = lax.optimization_barrier(jnp.mean(values, axis=-1, keepdims=True))
    centered = values - average
    variance = lax.optimization_barrier(jnp.mean(centered * centered, axis=-1, keepdims=True))
    return centered * lax.rsqrt(variance + norm_eps) * gain_row + shift_row

def grid_places(sides, slot_rows):
    counts = (sides * sides).astype(jnp.int32)
    ends = jnp.cumsum(counts).astype(jnp.int32)
    row_index = jnp.arange(slot_rows, dtype=jnp.int32)
    segment = lax.optimization_barrier(jnp.sum((row_index[:, None] >= ends[None, :]).astype(jnp.int32), axis=1)).astype(jnp.int32)
    starts = jnp.concatenate([jnp.zeros((1,), jnp.int32), ends])
    widths = jnp.concatenate([sides.astype(jnp.int32), jnp.zeros((1,), jnp.int32)])
    picked = segment[:, None] == jnp.arange(4, dtype=jnp.int32)[None, :]
    start_row = lax.optimization_barrier(jnp.sum(jnp.where(picked, starts[None, :], 0), axis=1)).astype(jnp.int32)
    side_row = jnp.maximum(lax.optimization_barrier(jnp.sum(jnp.where(picked, widths[None, :], 0), axis=1)), 1).astype(jnp.int32)
    offset = row_index - start_row
    inside = segment < 3
    height = jnp.where(inside, offset // side_row, 0)
    across = jnp.where(inside, offset % side_row, 0)
    return (segment, height.astype(jnp.float32), across.astype(jnp.float32))

def rotate(query, key_part, frequency_values, height, across):
    table = frequency_values.reshape(2, HEADS, HD // 2)
    angle = height[:, None, None] * table[0][None] + across[:, None, None] * table[1][None]
    cosine = jnp.cos(angle)
    sine = jnp.sin(angle)

    def turn(part):
        part = part.reshape(part.shape[0], HEADS, HD)
        first_half = part[..., :HD // 2]
        second_half = part[..., HD // 2:]
        return jnp.concatenate([first_half * cosine - second_half * sine, first_half * sine + second_half * cosine], axis=-1)
    return (turn(query), turn(key_part))

def slot_forward(slot_block, sides, params):
    norm_one, w_qkv, b_qkv, w_out, b_out, frequency_values, norm_two, w_up, b_up, w_down, b_down = params
    segment, height, across = grid_places(sides, CAP)
    normed = low(layer_norm(slot_block, norm_one[0], norm_one[1]))
    mixed = low_back(jnp.dot(normed, w_qkv, precision=highest) + b_qkv)
    query, key_part = rotate(mixed[:, :D], mixed[:, D:2 * D], frequency_values, height, across)
    query = low(query)
    key_part = low(key_part)
    values = low(mixed[:, 2 * D:].reshape(CAP, HEADS, HD))
    scores = low_back(jnp.einsum('qhd,khd->hqk', query, key_part, precision=highest) * score_scale)
    same_image = segment[:, None] == segment[None, :]
    scores = jnp.where(same_image[None], scores, -1e+30)
    row_peak = lax.optimization_barrier(jnp.max(scores, axis=-1, keepdims=True))
    weights = jnp.exp(scores - row_peak)
    probabilities = low(weights / lax.optimization_barrier(jnp.sum(weights, axis=-1, keepdims=True)))
    attended = jnp.einsum('hqk,khd->qhd', probabilities, values, precision=highest).reshape(CAP, D)
    attended = low_back(low(attended))
    branch = low_back(jnp.dot(attended, w_out, precision=highest) + b_out)
    middle = slot_block + branch
    normed_two = low(layer_norm(middle, norm_two[0], norm_two[1]))
    hidden = low_back(jnp.dot(normed_two, w_up, precision=highest) + b_up)
    activated = low(jax.nn.gelu(hidden))
    result = low_back(jnp.dot(activated, w_down, precision=highest) + b_down)
    return middle + result

def reference(tokens, image_sides, out_grad, attn_norm, qkv_weight, qkv_bias, out_weight, out_bias, frequencies, mlp_norm, up_weight, up_bias, down_weight, down_bias):
    params = tuple((item.astype(jnp.float32) for item in (attn_norm, qkv_weight, qkv_bias, out_weight, out_bias, frequencies, mlp_norm, up_weight, up_bias, down_weight, down_bias)))
    blocks = tokens.astype(jnp.float32).reshape(-1, CAP, D)
    grad_blocks = out_grad.astype(jnp.float32).reshape(-1, CAP, D)
    checked = jax.checkpoint(slot_forward)

    def forward(all_blocks, all_params):

        def one_slot(carry, item):
            return (carry, checked(item[0], item[1], all_params))
        _, results = lax.scan(one_slot, jnp.zeros((), jnp.float32), (all_blocks, image_sides))
        return results
    outputs, pullback = jax.vjp(forward, blocks, params)
    block_grad, param_grads = pullback(grad_blocks)
    return (outputs.reshape(-1, D).astype(jnp.bfloat16), block_grad.reshape(-1, D).astype(jnp.bfloat16), param_grads[0], param_grads[1], param_grads[2], param_grads[3], param_grads[4], param_grads[5], param_grads[6], param_grads[7], param_grads[8], param_grads[9], param_grads[10])
```

```python
import functools
import jax
import jax.numpy as jnp
from jax import lax
from jax.experimental import pallas as pl
from jax.experimental.pallas import tpu as pltpu
from jax.sharding import PartitionSpec as P

HEADS = 12
HD = 64
GROUP = 4
EPS = 1e-06
SCALE = 0.125
GELU_A = 0.7978845608028654
GELU_B = GELU_A * 0.044715
MASKED = -1e30
F32 = jnp.float32
BF16 = jnp.bfloat16


class Grid:
    def __init__(self, dp, fsdp):
        self.P, self.Z = dp // 2, fsdp
        i = lax.axis_index("dp")
        self.core, self.z = i % 2, lax.axis_index("fsdp")
        self.ring = self.turn(i // 2)

    def turn(self, p):
        return p + (p // 2) * (5 - 2 * p) if self.P == 4 else p

    def place(self, d):
        return self.turn((self.ring + d + self.P) % self.P)

    def at(self, d=0, core=None, k=0):
        core = self.core if core is None else core
        return (self.place(d) * 2 + core, (self.z + k + self.Z) % self.Z)

    def block(self, d=0, core=None, k=0):
        a, b = self.at(d, core, k)
        return a * self.Z + b

    def partners(self):
        ring = [1, -1] if self.P > 2 else [1] * (self.P - 1)
        return [self.at(d) for d in ring] + [self.at(core=1 - self.core)] + [self.at(k=k) for k in range(1, self.Z)]


def meet(g):
    barrier = pltpu.get_barrier_semaphore()
    who = g.partners()
    for w in who:
        pl.semaphore_signal(barrier, inc=1, device_id=w, device_id_type=pl.DeviceIdType.MESH)
    pl.semaphore_wait(barrier, len(who))


def remote(src, dst, sems, i, who):
    return pltpu.make_async_remote_copy(src_ref=src, dst_ref=dst, send_sem=sems.at[0, i], recv_sem=sems.at[1, i],
                                        device_id=who, device_id_type=pl.DeviceIdType.MESH)


class Gather:
    def __init__(self, g, mine, full, sems, local):
        self.g, self.full, self.sems, self.mine, self.local = g, full, sems, mine, local
        self.count = 0
        self.sent = []

    @staticmethod
    def copies(dp, fsdp):
        P, Z = dp // 2, fsdp
        return (Z - 1) + Z * (2 * (P // 2)) + Z * (2 * P)

    def send(self, block, who, part=None, src=None):
        dst = self.full.at[block]
        src = dst if src is None else src
        if part is not None:
            src, dst = src.at[:, part], dst.at[:, part]
        c = remote(src, dst, self.sems, self.count, who)
        self.count += 1
        c.start()
        self.sent.append(c)
        return c

    def recv(self, c, block, part=None):
        dst = self.full.at[block]
        if part is not None:
            dst = dst.at[:, part]
        i = c
        pltpu.make_async_remote_copy(src_ref=dst, dst_ref=dst, send_sem=self.sems.at[0, i], recv_sem=self.sems.at[1, i],
                                     device_id=self.g.at(core=1 - self.g.core), device_id_type=pl.DeviceIdType.MESH).wait_recv()

    def steps(self):
        g, P, Z = self.g, self.g.P, self.g.Z
        cols = self.full.shape[2]
        cut = (cols // 256) * 128
        A, B = pl.ds(0, cut), pl.ds(cut, cols - cut)
        sib = g.at(core=1 - g.core)
        other = 1 - g.core
        right, left = g.at(1), g.at(-1)
        inbox = []

        def to_sibling(d, k, part=None):
            n = self.count
            self.send(g.block(d, k=-k), sib, part, self.mine if (d, k) == (0, 0) else None)
            inbox.append((n, g.block(d, other, -k), part))

        def ring_out(k):
            src = self.mine if k == 0 else None
            b = g.block(0, k=-k)
            nr = self.count
            if P == 2:
                self.send(b, right, None, src)
                return {1: (nr, None)}
            self.send(b, right, None, src)
            nl = self.count
            self.send(b, left, None, src)
            return {1: nr, -1: nl}

        def begin():
            own = pltpu.make_async_copy(self.mine, self.full.at[g.block()], self.local)
            own.start()
            self.own = own
            self.rings = [ring_out(0)]
            self.lines = []
            for k in range(1, Z):
                self.lines.append(self.count)
                self.send(g.block(), g.at(k=k), None, self.mine)
            to_sibling(0, 0)
        yield begin

        def line(k):
            def f():
                self.recv(self.lines[k - 1], g.block(0, k=-k))
                self.rings.append(ring_out(k))
                to_sibling(0, k)
            return f

        def ring(k):
            def f():
                r = self.rings[k]
                for d in range(1, P // 2 + 1):
                    last = 2 * d == P
                    nxt = {}
                    for sgn, who in ((1, right), (-1, left)):
                        blk = g.block(-sgn * d, k=-k)
                        part = (A if sgn == 1 else B) if last else None
                        self.recv(r[sgn], blk, part)
                        if not last:
                            nl = 2 * (d + 1) == P
                            nxt[sgn] = self.count
                            self.send(blk, who, (A if sgn == 1 else B) if nl else None)
                    for sgn in (1, -1):
                        to_sibling(-sgn * d, k, (A if sgn == 1 else B) if last else None)
                    r = nxt
            return f

        def ring_near(k):
            def f():
                r = self.rings[k]
                nxt = {}
                for sgn, who in ((1, right), (-1, left)):
                    blk = g.block(-sgn, k=-k)
                    self.recv(r[sgn], blk)
                    nxt[sgn] = self.count
                    self.send(blk, who, A if sgn == 1 else B)
                self.far[k] = nxt
                for sgn in (1, -1):
                    to_sibling(-sgn, k)
            return f

        def ring_far(k):
            def f():
                for sgn in (1, -1):
                    part = A if sgn == 1 else B
                    blk = g.block(-sgn * 2, k=-k)
                    self.recv(self.far[k][sgn], blk, part)
                    to_sibling(-sgn * 2, k, part)
            return f

        self.far = {}
        if P == 4:
            for k in range(Z):
                if k + 1 < Z:
                    yield line(k + 1)
                yield ring_near(k)
                if k > 0:
                    yield ring_far(k - 1)
            yield ring_far(Z - 1)
        else:
            for k in range(Z):
                if k + 1 < Z:
                    yield line(k + 1)
                yield ring(k)

        def finish():
            for n, blk, part in inbox:
                self.recv(n, blk, part)
            self.own.wait()
            for c in self.sent:
                c.wait_send()
        yield finish


def gather_kernel(dp, fsdp, count, *refs):
    mine, full = refs[:count], refs[count:2 * count]
    sems, local = refs[2 * count:3 * count], refs[3 * count]
    g = Grid(dp, fsdp)
    meet(g)
    runs = [list(Gather(g, m, f, s, local.at[i]).steps()) for i, (m, f, s) in enumerate(zip(mine, full, sems))]
    for stage in zip(*runs):
        for step in stage:
            step()


def gather(mesh, arrays, cid):
    dp, fsdp = mesh.shape["dp"], mesh.shape["fsdp"]
    n = dp * fsdp
    count = len(arrays)
    anys = [pl.BlockSpec(memory_space=pl.ANY)] * count

    return pl.pallas_call(
        functools.partial(gather_kernel, dp, fsdp, count),
        in_specs=anys, out_specs=anys,
        out_shape=[jax.ShapeDtypeStruct((n,) + a.shape, a.dtype) for a in arrays],
        scratch_shapes=[pltpu.SemaphoreType.DMA((2, Gather.copies(dp, fsdp)))] * count + [pltpu.SemaphoreType.DMA((count,))],
        compiler_params=pltpu.CompilerParams(collective_id=cid, has_side_effects=True),
        name=f"gather{cid}",
    )(*arrays)


class Scatter:
    FAR, RIGHT, LEFT, OWN = 0, 1, 2, 3
    REL = (2, 1, -1, 0)

    def __init__(self, g, part, out, bufs, sems, local):
        self.g, self.part, self.out, self.sems, self.local = g, part, out, sems, local
        self.own, self.sib, self.ra, self.rb, self.rl, self.rr, self.sum, self.rz = bufs
        cols = part.shape[2]
        cut = (cols // 256) * 128
        self.A, self.B = pl.ds(0, cut), pl.ds(cut, cols - cut)

    @staticmethod
    def buffers(Z, rows, cols, dtype):
        cut = (cols // 256) * 128
        shapes = [(4, Z, rows, cols), (4, Z, rows, cols), (Z, rows, max(cut, 1)), (Z, rows, cols - cut), (Z, rows, cols), (Z, rows, cols),
                  (Z, rows, cols), (max(Z - 1, 1), rows, cols)]
        return [pltpu.VMEM(s, dtype) for s in shapes]

    @staticmethod
    def copies(Z):
        return 4 + 2 + 2 + Z - 1

    def steps(self):
        g, Z = self.g, self.g.Z
        A, B = self.A, self.B
        cut = A.size
        dt = self.own.dtype
        right, left, sibling = g.at(1), g.at(-1), g.at(core=1 - g.core)
        loads = [pltpu.make_async_copy(self.part.at[pl.ds(g.place(d) * 2 * Z + g.core * Z, Z)], self.own.at[i], self.local.at[i])
                 for i, d in enumerate(self.REL)]
        cores = [remote(self.part.at[pl.ds(g.place(d) * 2 * Z + (1 - g.core) * Z, Z)], self.sib.at[i], self.sems, i, sibling)
                 for i, d in enumerate(self.REL)]
        far = [remote(self.own.at[self.FAR, :, :, A], self.ra, self.sems, 4, right)] if cut else []
        far += [remote(self.own.at[self.FAR, :, :, B], self.rb, self.sems, 5, left)]
        near = [remote(self.own.at[self.RIGHT], self.rl, self.sems, 6, right), remote(self.own.at[self.LEFT], self.rr, self.sems, 7, left)]
        lines = [remote(self.sum.at[(g.z + k) % Z], self.rz.at[k - 1], self.sems, 7 + k, g.at(k=k)) for k in range(1, Z)]

        def begin():
            for a, b in zip(loads, cores):
                b.start()
                a.start()

        def take(i):
            loads[i].wait()
            cores[i].wait_recv()

        def do_far():
            take(self.FAR)
            for z in range(Z):
                self.own[self.FAR, z] = (self.own[self.FAR, z].astype(F32) + self.sib[self.FAR, z].astype(F32)).astype(dt)
            for c in far:
                c.start()

        def do_near():
            take(self.RIGHT)
            take(self.LEFT)
            for c in far:
                c.wait_recv()
            for z in range(Z):
                for i, got, has, rest in ((self.RIGHT, self.ra, A, B), (self.LEFT, self.rb, B, A)):
                    if has.size:
                        self.own[i, z, :, has] = (self.own[i, z, :, has].astype(F32) + self.sib[i, z, :, has].astype(F32) + got[z].astype(F32)).astype(dt)
                    if rest.size:
                        self.own[i, z, :, rest] = (self.own[i, z, :, rest].astype(F32) + self.sib[i, z, :, rest].astype(F32)).astype(dt)
            for c in near:
                c.start()

        def do_own():
            take(self.OWN)
            for c in near:
                c.wait_recv()
            for z in range(Z):
                s = self.own[self.OWN, z].astype(F32) + self.sib[self.OWN, z].astype(F32) + self.rl[z].astype(F32) + self.rr[z].astype(F32)
                self.sum[z] = s.astype(dt)
            for c in lines:
                c.start()

        def finish():
            for c in lines:
                c.wait_recv()
            s = self.sum[g.z].astype(F32)
            for k in range(1, Z):
                s += self.rz[k - 1].astype(F32)
            self.out[...] = s
            for c in cores + far + near + lines:
                c.wait_send()

        yield begin
        yield do_far
        yield do_near
        yield do_own
        yield finish


def scatter_kernel(dp, fsdp, layout, *refs):
    parts = [w for out in layout for w in out]
    n = len(parts)
    ins, outs, rest = refs[:n], refs[n:n + len(layout)], refs[n + len(layout):]
    g = Grid(dp, fsdp)
    meet(g)
    runs, at = [], 0
    for o, widths in zip(outs, layout):
        off = 0
        for w in widths:
            bufs, sems, local = rest[:8], rest[8], rest[9]
            rest = rest[10:]
            runs.append(list(Scatter(g, ins[at], o.at[:, pl.ds(off, w)], bufs, sems, local).steps()))
            at, off = at + 1, off + w
    for stage in zip(*runs):
        for step in stage:
            step()


def scatter(mesh, groups, cid):
    dp, fsdp = mesh.shape["dp"], mesh.shape["fsdp"]
    parts = [p for gr in groups for p in gr]
    rows = parts[0].shape[1]
    layout = [[p.shape[2] for p in gr] for gr in groups]
    scratch = []
    for p in parts:
        scratch += Scatter.buffers(fsdp, rows, p.shape[2], p.dtype) + [pltpu.SemaphoreType.DMA((2, Scatter.copies(fsdp))), pltpu.SemaphoreType.DMA((4,))]
    return pl.pallas_call(
        functools.partial(scatter_kernel, dp, fsdp, layout),
        in_specs=[pl.BlockSpec(memory_space=pl.ANY)] * len(parts),
        out_specs=[pl.BlockSpec(memory_space=pltpu.VMEM)] * len(groups),
        out_shape=[jax.ShapeDtypeStruct((rows, sum(ws)), F32) for ws in layout],
        scratch_shapes=scratch,
        compiler_params=pltpu.CompilerParams(collective_id=cid, has_side_effects=True, vmem_limit_bytes=60 * 2**20),
        name=f"scatter{cid}",
    )(*parts)


def dot(a, b, ca, cb):
    return lax.dot_general(a, b, (((ca,), (cb,)), ((), ())), preferred_element_type=F32)


def places(sides_ref, slot, rows):
    a, b, c = sides_ref[slot, 0], sides_ref[slot, 1], sides_ref[slot, 2]
    e1 = a * a
    e2 = e1 + b * b
    e3 = e2 + c * c
    r = lax.broadcasted_iota(jnp.int32, (1, rows), 1)
    in2, in3, out = r >= e1, r >= e2, r >= e3
    seg = in2.astype(jnp.int32) + in3.astype(jnp.int32) + out.astype(jnp.int32)
    start = jnp.where(in3, e2, jnp.where(in2, e1, 0))
    side = jnp.where(in3, c, jnp.where(in2, b, a))
    side = jnp.maximum(side, 1).astype(F32)
    offset = (r - start).astype(F32)
    height = jnp.floor((offset + 0.5) / side)
    across = offset - height * side
    return seg, jnp.where(out, 0.0, height), jnp.where(out, 0.0, across)


def stats(x):
    mean = jnp.mean(x, axis=-1, keepdims=True)
    cen = x - mean
    var = jnp.mean(cen * cen, axis=-1, keepdims=True)
    rstd = lax.rsqrt(var + EPS)
    return cen * rstd, rstd


def ln_back(dn, gain, xhat, rstd):
    e = dn * gain
    m1 = jnp.mean(e, axis=-1, keepdims=True)
    m2 = jnp.mean(e * xhat, axis=-1, keepdims=True)
    return rstd * (e - m1 - xhat * m2)


def attn_fwd_kernel(sides, tok, wq, wk, wv, wo, rows1, bq, bk, bv, freq,
                    mid, qT, kT, vT, eT, linv, oT, cosT, sinT,
                    n1, acc):
    quad, slot = pl.program_id(0), pl.program_id(1)
    rows = tok.shape[1]
    seg, height, across = places(sides, slot, rows)
    j16 = lax.broadcasted_iota(jnp.int32, (16, rows), 0)
    hit = j16 == seg
    k_aug = jnp.where(hit, 1.0, 0.0).astype(BF16)
    q_aug = jnp.where(hit | (j16 > 3), 0.0, MASKED).astype(BF16)

    @pl.when(quad == 0)
    def _():
        x = tok[0].astype(F32)
        xhat, _ = stats(x)
        n1[slot] = (xhat * rows1[0:1, :] + rows1[1:2, :]).astype(BF16)
        acc[slot] = x + rows1[2:3, :]

    half = HD // 2
    angle = freq[0] * height + freq[1] * across
    cos = jnp.cos(angle)
    sin = jnp.sin(angle)
    cosT[0] = cos
    sinT[0] = sin
    n = n1[slot]
    xq = dot(wq[...], n, 0, 1) + bq[...]
    xk = dot(wk[...], n, 0, 1) + bk[...]
    xv = (dot(wv[...], n, 0, 1) + bv[...]).astype(BF16)
    vT[0] = xv
    for h in range(GROUP):
        c, s = cos[h * half:(h + 1) * half], sin[h * half:(h + 1) * half]
        lo, mi, hi = h * HD, h * HD + half, (h + 1) * HD
        q1 = (xq[lo:mi] * c - xq[mi:hi] * s) * SCALE
        q2 = (xq[lo:mi] * s + xq[mi:hi] * c) * SCALE
        k1 = xk[lo:mi] * c - xk[mi:hi] * s
        k2 = xk[lo:mi] * s + xk[mi:hi] * c
        q = jnp.concatenate([q1, q2], axis=0).astype(BF16)
        k = jnp.concatenate([k1, k2], axis=0).astype(BF16)
        qT[0, lo:hi] = q
        kT[0, lo:hi] = k
        sT = dot(jnp.concatenate([k, k_aug], axis=0), jnp.concatenate([q, q_aug], axis=0), 0, 0)
        m = jnp.max(sT, axis=0, keepdims=True)
        e = jnp.exp(sT - m)
        inv = 1.0 / jnp.sum(e, axis=0, keepdims=True)
        e = e.astype(BF16)
        eT[h] = e
        linv[0, h:h + 1] = inv
        o = dot(xv[lo:hi], e, 1, 0) * inv
        oT[0, lo:hi] = o.astype(BF16)
    acc[slot] += dot(oT[0], wo[...], 0, 0)

    @pl.when(quad == pl.num_programs(0) - 1)
    def _():
        mid[slot] = acc[slot]


def attn_fwd(sides, tok, wqkv, wo, rows1, bcol, freq):
    slots, rows, d = tok.shape
    nq = HEADS // GROUP
    gw = GROUP * HD
    sd = jax.ShapeDtypeStruct
    col = lambda off: pl.BlockSpec((d, gw), lambda i, j, off=off: (0, off + i))
    bsp = lambda off: pl.BlockSpec((gw, 1), lambda i, j, off=off: (off + i, 0))
    tr = pl.BlockSpec((1, gw, rows), lambda i, j: (j, i, 0))
    return pl.pallas_call(
        attn_fwd_kernel,
        grid=(nq, slots),
        in_specs=[
            pl.BlockSpec(memory_space=pltpu.SMEM),
            pl.BlockSpec((1, rows, d), lambda i, j: (jnp.where(i == 0, j, slots - 1), 0, 0)),
            col(0), col(nq), col(2 * nq),
            pl.BlockSpec((gw, d), lambda i, j: (i, 0)),
            pl.BlockSpec((8, d), lambda i, j: (0, 0)),
            bsp(0), bsp(nq), bsp(2 * nq),
            pl.BlockSpec((2, gw // 2, 1), lambda i, j: (0, i, 0)),
        ],
        out_specs=[
            pl.BlockSpec((slots, rows, d), lambda i, j: (0, 0, 0)),
            tr, tr, tr,
            pl.BlockSpec((GROUP, rows, rows), lambda i, j: (j * nq + i, 0, 0)),
            pl.BlockSpec((1, 8, rows), lambda i, j: (j * nq + i, 0, 0)),
            tr,
            pl.BlockSpec((1, gw // 2, rows), lambda i, j: (j, i, 0)),
            pl.BlockSpec((1, gw // 2, rows), lambda i, j: (j, i, 0)),
        ],
        out_shape=[
            sd((slots, rows, d), F32),
            sd((slots, d, rows), BF16), sd((slots, d, rows), BF16), sd((slots, d, rows), BF16),
            sd((slots * HEADS, rows, rows), BF16),
            sd((slots * nq, 8, rows), F32),
            sd((slots, d, rows), BF16),
            sd((slots, d // 2, rows), F32), sd((slots, d // 2, rows), F32),
        ],
        scratch_shapes=[pltpu.VMEM((slots, rows, d), BF16), pltpu.VMEM((slots, rows, d), F32)],
        compiler_params=pltpu.CompilerParams(vmem_limit_bytes=60 * 2**20),
        name="attn_fwd",
    )(sides, tok, wqkv, wqkv, wqkv, wo, rows1, bcol, bcol, bcol, freq)


def mlp_kernel(mid, g, up, dnT, rows2, ub,
               out, mgrad, dup, ddT, small, dub,
               n2, n2T, gT, oacc, dacc):
    f, last = pl.program_id(0), pl.num_programs(0) - 1

    @pl.when(f == 0)
    def _():
        xhat, _ = stats(mid[...])
        n = xhat * rows2[0:1, :] + rows2[1:2, :]
        n2[...] = n.astype(BF16)
        n2T[...] = n.T.astype(BF16)
        gT[...] = g[...].astype(F32).T.astype(BF16)

    v = dot(n2[...], up[...], 1, 0) + ub[...]
    ga = dot(g[...], dnT[...], 1, 0)
    v2 = v * v
    t = jnp.tanh(v * (GELU_A + GELU_B * v2))
    p = 0.5 * t + 0.5
    act = (v * p).astype(BF16)
    slope = p + (0.5 * v) * (1.0 - t * t) * (GELU_A + (3.0 * GELU_B) * v2)
    hg = (slope * ga).astype(BF16)
    o = dot(act, dnT[...], 1, 1)
    dn = dot(hg, up[...], 1, 1)
    ddT[...] = dot(gT[...], act, 1, 0).astype(BF16)
    dup[...] = dot(n2T[...], hg, 1, 0).astype(BF16)
    dub[...] = jnp.sum(hg.astype(F32), axis=0, keepdims=True)

    @pl.when(f == 0)
    def _():
        oacc[...] = o
        dacc[...] = dn

    @pl.when(f > 0)
    def _():
        oacc[...] += o
        dacc[...] += dn

    @pl.when(f == last)
    def _():
        x = mid[...]
        out[...] = (x + oacc[...] + rows2[2:3, :]).astype(BF16)
        xhat, rstd = stats(x)
        dn = dacc[...]
        gf = g[...].astype(F32)
        mg = gf + ln_back(dn, rows2[0:1, :], xhat, rstd)
        mgrad[...] = mg
        small[0:1, :] = jnp.sum(dn * xhat, axis=0, keepdims=True)
        small[1:2, :] = jnp.sum(dn, axis=0, keepdims=True)
        small[2:3, :] = jnp.sum(gf, axis=0, keepdims=True)
        small[3:4, :] = jnp.sum(mg.astype(BF16).astype(F32), axis=0, keepdims=True)
        small[4:8, :] = jnp.zeros_like(small[4:8, :])


def mlp(mid, g, up, dnT, rows2, ub, chunk=512):
    rows, d = mid.shape
    ff = up.shape[1]
    sd = jax.ShapeDtypeStruct
    whole = lambda: pl.BlockSpec((rows, d), lambda f: (0, 0))
    wsp = lambda: pl.BlockSpec((d, chunk), lambda f: (0, f))
    return pl.pallas_call(
        mlp_kernel,
        grid=(ff // chunk,),
        in_specs=[whole(), whole(), wsp(), wsp(),
                  pl.BlockSpec((8, d), lambda f: (0, 0)),
                  pl.BlockSpec((1, chunk), lambda f: (0, f))],
        out_specs=[whole(), whole(), wsp(), wsp(),
                   pl.BlockSpec((8, d), lambda f: (0, 0)),
                   pl.BlockSpec((1, chunk), lambda f: (0, f))],
        out_shape=[sd((rows, d), BF16), sd((rows, d), F32), sd((d, ff), BF16), sd((d, ff), BF16),
                   sd((8, d), F32), sd((1, ff), F32)],
        scratch_shapes=[pltpu.VMEM((rows, d), BF16), pltpu.VMEM((d, rows), BF16), pltpu.VMEM((d, rows), BF16),
                        pltpu.VMEM((rows, d), F32), pltpu.VMEM((rows, d), F32)],
        compiler_params=pltpu.CompilerParams(vmem_limit_bytes=60 * 2**20),
        name="mlp",
    )(mid, g, up, dnT, rows2, ub)


def attn_bwd_kernel(sides, tok, mgrad, wq, wk, wv, wo, rows1, qT, kT, vT, eT, linv, oT, cosT, sinT,
                    tgrad, dwq, dwk, dwv, dwo, small, dbq, dbk, dbv, dfr,
                    n1, mlow, dacc, aq, ak, av, ao):
    quad, slot = pl.program_id(0), pl.program_id(1)
    lastq = pl.num_programs(0) - 1
    rows = tok.shape[1]
    half = HD // 2
    _, height, across = places(sides, slot, rows)

    @pl.when(quad == 0)
    def _():
        xhat, _ = stats(tok[slot].astype(F32))
        n1[slot] = (xhat * rows1[0:1, :] + rows1[1:2, :]).astype(BF16)
        mlow[slot] = mgrad[slot].astype(BF16)

    ml = mlow[slot]
    dO = dot(wo[...], ml, 1, 1)
    dqs, dks, dvs, fgs = [], [], [], []
    for h in range(GROUP):
        lo, mi, hi = h * HD, h * HD + half, (h + 1) * HD
        c, s = cosT[0, h * half:(h + 1) * half], sinT[0, h * half:(h + 1) * half]
        dof = dO[lo:hi] * linv[0, h:h + 1]
        do = dof.astype(BF16)
        dd = jnp.sum(dof * oT[0, lo:hi].astype(F32), axis=0, keepdims=True)
        dp = dot(vT[0, lo:hi], do, 0, 0)
        e = eT[h]
        ds = (e.astype(F32) * (dp - dd)).astype(BF16)
        dvs.append(dot(do, e, 1, 1))
        dk = dot(qT[0, lo:hi], ds, 1, 1)
        dq = dot(kT[0, lo:hi], ds, 1, 0)
        k = kT[0, lo:hi].astype(F32)
        q = qT[0, lo:hi].astype(F32)
        ang = dq[half:] * q[:half] - dq[:half] * q[half:] + dk[half:] * k[:half] - dk[:half] * k[half:]
        fgs.append(jnp.concatenate([jnp.sum(ang * height, axis=1, keepdims=True),
                                    jnp.sum(ang * across, axis=1, keepdims=True)], axis=1))
        dq = dq * SCALE
        dqs += [dq[:half] * c + dq[half:] * s, dq[half:] * c - dq[:half] * s]
        dks += [dk[:half] * c + dk[half:] * s, dk[half:] * c - dk[:half] * s]
    dq = jnp.concatenate(dqs, axis=0).astype(BF16)
    dk = jnp.concatenate(dks, axis=0).astype(BF16)
    dv = jnp.concatenate(dvs, axis=0).astype(BF16)
    fg = jnp.concatenate(fgs, axis=0)
    n = n1[slot]
    gq, gk, gv = dot(n, dq, 0, 1), dot(n, dk, 0, 1), dot(n, dv, 0, 1)
    go = dot(oT[0], ml, 1, 0)
    bias = lambda x: jnp.sum(x.astype(F32), axis=1, keepdims=True)
    dn = dot(dq, wq[...], 0, 1) + dot(dk, wk[...], 0, 1) + dot(dv, wv[...], 0, 1)

    weights = ((dwq, aq, gq), (dwk, ak, gk), (dwv, av, gv), (dwo, ao, go))
    sums = ((dbq, bias(dq)), (dbk, bias(dk)), (dbv, bias(dv)), (dfr, fg))

    @pl.when(slot == 0)
    def _():
        for _, ref, val in weights:
            ref[...] = val
        for ref, val in sums:
            ref[...] = val

    @pl.when(slot > 0)
    def _():
        for _, ref, val in weights:
            ref[...] += val
        for ref, val in sums:
            ref[...] += val

    @pl.when(slot == pl.num_programs(1) - 1)
    def _():
        for low, ref, _ in weights:
            low[...] = ref[...].astype(BF16)

    @pl.when(quad == 0)
    def _():
        dacc[slot] = dn

    @pl.when(quad > 0)
    def _():
        dacc[slot] += dn

    @pl.when(quad == lastq)
    def _():
        xhat, rstd = stats(tok[slot].astype(F32))
        d = dacc[slot]
        tgrad[slot] = (mgrad[slot] + ln_back(d, rows1[0:1, :], xhat, rstd)).astype(BF16)
        s0 = jnp.sum(d * xhat, axis=0, keepdims=True)
        s1 = jnp.sum(d, axis=0, keepdims=True)

        @pl.when(slot == 0)
        def _():
            small[...] = jnp.zeros_like(small)
        small[0:1, :] += s0
        small[1:2, :] += s1


def attn_bwd(sides, tok, mgrad, wqkv, wo, rows1, saved):
    slots, rows, d = tok.shape
    nq = HEADS // GROUP
    gw = GROUP * HD
    sd = jax.ShapeDtypeStruct
    col = lambda off: pl.BlockSpec((d, gw), lambda i, j, off=off: (0, off + i))
    whole = lambda: pl.BlockSpec((slots, rows, d), lambda i, j: (0, 0, 0))
    tr = pl.BlockSpec((1, gw, rows), lambda i, j: (j, i, 0))
    trh = pl.BlockSpec((1, gw // 2, rows), lambda i, j: (j, i, 0))
    gcol = lambda: pl.BlockSpec((d, gw), lambda i, j: (0, i))
    bcol = lambda: pl.BlockSpec((gw, 1), lambda i, j: (i, 0))
    return pl.pallas_call(
        attn_bwd_kernel,
        grid=(nq, slots),
        in_specs=[
            pl.BlockSpec(memory_space=pltpu.SMEM), whole(), whole(),
            col(0), col(nq), col(2 * nq),
            pl.BlockSpec((gw, d), lambda i, j: (i, 0)),
            pl.BlockSpec((8, d), lambda i, j: (0, 0)),
            tr, tr, tr,
            pl.BlockSpec((GROUP, rows, rows), lambda i, j: (j * nq + i, 0, 0)),
            pl.BlockSpec((1, 8, rows), lambda i, j: (j * nq + i, 0, 0)),
            tr, trh, trh,
        ],
        out_specs=[
            whole(), gcol(), gcol(), gcol(),
            pl.BlockSpec((gw, d), lambda i, j: (i, 0)),
            pl.BlockSpec((8, d), lambda i, j: (0, 0)),
            bcol(), bcol(), bcol(),
            pl.BlockSpec((gw // 2, 2), lambda i, j: (i, 0)),
        ],
        out_shape=[
            sd((slots, rows, d), BF16), sd((d, d), BF16), sd((d, d), BF16), sd((d, d), BF16), sd((d, d), BF16),
            sd((8, d), F32), sd((d, 1), F32), sd((d, 1), F32), sd((d, 1), F32), sd((d // 2, 2), F32),
        ],
        scratch_shapes=[pltpu.VMEM((slots, rows, d), BF16), pltpu.VMEM((slots, rows, d), BF16), pltpu.VMEM((slots, rows, d), F32),
                        pltpu.VMEM((d, gw), F32), pltpu.VMEM((d, gw), F32), pltpu.VMEM((d, gw), F32), pltpu.VMEM((gw, d), F32)],
        compiler_params=pltpu.CompilerParams(vmem_limit_bytes=62 * 2**20),
        name="attn_bwd",
    )(sides, tok, mgrad, wqkv, wqkv, wqkv, wo, rows1, *saved)


LANES = 128
BOTH = ("dp", "fsdp")


def pack(columns):
    have = jnp.concatenate(columns, axis=-1)
    pad = [(0, 0)] * (have.ndim - 1) + [(0, LANES - have.shape[-1])]
    return jnp.pad(have, pad)


def on_device(mesh, tok, sides, g, attn_norm, wqkv, bqkv, wo, bo, freq, mlp_norm, up, ub, down, db):
    n = mesh.shape["dp"] * mesh.shape["fsdp"]
    slots = sides.shape[0]
    d = tok.shape[1]
    rows = tok.shape[0] // slots
    r = wqkv.shape[0]
    nb, nu = bqkv.shape[0] // r, ub.shape[0] // r
    hand = mesh.shape["dp"] == 8 and r % 8 == 0
    mine = [wqkv, wo, pack([attn_norm.T, bo[:, None], freq[:, None], mlp_norm.T, db[:, None], bqkv.reshape(nb, r).T, ub.reshape(nu, r).T]),
            up, down.T]
    if hand:
        full = gather(mesh, mine, 0)
    else:
        full = [lax.all_gather(x, BOTH, axis=0) for x in mine]
    wqkv, wo, small, up, dnT = full
    wqkv, wo, up, dnT = (x.reshape(d, -1) for x in (wqkv, wo, up, dnT))
    small = small.astype(F32)
    lanes = small.reshape(d, LANES).T
    rows1 = jnp.concatenate([lanes[:3], jnp.zeros((5, d), F32)], axis=0)
    rows2 = jnp.concatenate([lanes[4:7], jnp.zeros((5, d), F32)], axis=0)
    freq = small[:, :, 3].reshape(2, d // 2, 1)
    bcol = small[:, :, 7:7 + nb].transpose(0, 2, 1).reshape(nb * d, 1)
    urow = small[:, :, 7 + nb:7 + nb + nu].transpose(0, 2, 1).reshape(1, nu * d)

    t3 = tok.reshape(slots, rows, d)
    mid, *saved = attn_fwd(sides, t3, wqkv, wo, rows1, bcol, freq)
    out, mgrad, dup, ddT, small2, dub = mlp(mid.reshape(-1, d), g, up, dnT, rows2, urow)
    tg, dwq, dwk, dwv, dwo, small1, dbq, dbk, dbv, dfr = attn_bwd(sides, t3, mgrad.reshape(slots, rows, d), wqkv, wo, rows1, saved)

    cut = lambda x: x.reshape(n, r, -1)
    small = pack([cut(small1[:2].T), cut(small2[3]), cut(dfr.T), cut(small2[:2].T), cut(small2[2]),
                  jnp.concatenate([dbq, dbk, dbv], axis=0).reshape(n, nb, r).transpose(0, 2, 1),
                  dub.reshape(n, nu, r).transpose(0, 2, 1)])
    parts = [[cut(dwq), cut(dwk), cut(dwv)], [cut(dwo)], [small], [cut(dup)], [cut(ddT)]]
    if hand:
        sums = scatter(mesh, parts, 1)
    else:
        sums = [jnp.concatenate([lax.psum_scatter(x.astype(F32), BOTH, scatter_dimension=0) for x in p], axis=-1) for p in parts]
    gqkv, go, gs, gup, gdT = sums
    return (out, tg.reshape(-1, d), gs[:, :2].T, gqkv, gs[:, 7:7 + nb].T.reshape(-1), go, gs[:, 2], gs[:, 3], gs[:, 4:6].T, gup,
            gs[:, 7 + nb:7 + nb + nu].T.reshape(-1), gdT.T, gs[:, 6])


def solution(mesh):
    row, col, flat = P(BOTH, None), P(None, BOTH), P(BOTH)
    return jax.shard_map(
        functools.partial(on_device, mesh), mesh=mesh,
        in_specs=(row, row, row, col, row, flat, row, flat, flat, col, row, flat, col, flat),
        out_specs=(row, row, col, row, flat, row, flat, flat, col, row, flat, col, flat),
        check_vma=False,
    )
```

```python
import functools
import jax
import jax.numpy as jnp
from jax import lax
from jax.experimental import pallas as pl
from jax.experimental.pallas import tpu as pltpu
from jax.sharding import PartitionSpec as P

HEADS = 12
HD = 64
GROUP = 4
EPS = 1e-06
SCALE = 0.125
GELU_A = 0.7978845608028654
GELU_B = GELU_A * 0.044715
MASKED = -1e30
F32 = jnp.float32
BF16 = jnp.bfloat16


class Grid:
    def __init__(self, dp, fsdp):
        self.P, self.Z = dp // 2, fsdp
        i = lax.axis_index("dp")
        self.core, self.z = i % 2, lax.axis_index("fsdp")
        self.ring = self.turn(i // 2)

    def turn(self, p):
        return p + (p // 2) * (5 - 2 * p) if self.P == 4 else p

    def place(self, d):
        return self.turn((self.ring + d + self.P) % self.P)

    def at(self, d=0, core=None, k=0):
        core = self.core if core is None else core
        return (self.place(d) * 2 + core, (self.z + k + self.Z) % self.Z)

    def block(self, d=0, core=None, k=0):
        a, b = self.at(d, core, k)
        return a * self.Z + b

    def partners(self):
        ring = [1, -1] if self.P > 2 else [1] * (self.P - 1)
        return [self.at(d) for d in ring] + [self.at(core=1 - self.core)] + [self.at(k=k) for k in range(1, self.Z)]


def meet(g):
    barrier = pltpu.get_barrier_semaphore()
    who = g.partners()
    for w in who:
        pl.semaphore_signal(barrier, inc=1, device_id=w, device_id_type=pl.DeviceIdType.MESH)
    pl.semaphore_wait(barrier, len(who))


def remote(src, dst, sems, i, who):
    return pltpu.make_async_remote_copy(src_ref=src, dst_ref=dst, send_sem=sems.at[0, i], recv_sem=sems.at[1, i],
                                        device_id=who, device_id_type=pl.DeviceIdType.MESH)


class Gather:
    def __init__(self, g, mine, full, sems, local):
        self.g, self.full, self.sems, self.mine, self.local = g, full, sems, mine, local
        cols = full.shape[2]
        cut = (cols // 256) * 128
        self.parts = (pl.ds(0, cut), pl.ds(cut, cols - cut))
        self.numbers = {}

    @staticmethod
    def copies(Z):
        return (Z - 1) + Z * 4 + Z * 5

    def copy(self, kind, d, k, part=None):
        g = self.g
        n = self.numbers.setdefault((kind, d, k, part), len(self.numbers))
        dst = self.full.at[g.block(d, k=-k) if kind != "line" else g.block()]
        src = self.mine if (d, k) == (0, 0) or kind == "line" else dst
        if part is not None:
            src, dst = src.at[:, self.parts[part]], dst.at[:, self.parts[part]]
        who = {"line": lambda: g.at(k=k), "right": lambda: g.at(1), "left": lambda: g.at(-1), "core": lambda: g.at(core=1 - g.core)}[kind]()
        return remote(src, dst, self.sems, n, who)

    def land(self, kind, d, k, part=None):
        g = self.g
        n = self.numbers[kind, d, k, part]
        block = {"line": lambda: g.block(0, k=-k), "right": lambda: g.block(d - 1, k=-k), "left": lambda: g.block(d + 1, k=-k),
                 "core": lambda: g.block(d, 1 - g.core, -k)}[kind]()
        dst = self.full.at[block]
        if part is not None:
            dst = dst.at[:, self.parts[part]]
        remote(dst, dst, self.sems, n, g.at(core=1 - g.core)).wait_recv()

    def steps(self):
        Z = self.g.Z

        def send(*what):
            self.copy(*what).start()

        def around(k):
            send("right", 0, k)
            send("left", 0, k)
            send("core", 0, k)

        def keep():
            return pltpu.make_async_copy(self.mine, self.full.at[self.g.block()], self.local)

        def own():
            keep().start()
            around(0)

        def lines():
            for k in range(1, Z):
                send("line", 0, k)

        def line(k):
            self.land("line", 0, k)
            around(k)

        def near(k):
            self.land("right", 0, k)
            send("right", -1, k, 0)
            self.land("left", 0, k)
            send("left", 1, k, 1)
            send("core", -1, k)
            send("core", 1, k)

        def far(k):
            self.land("right", -1, k, 0)
            send("core", -2, k, 0)
            self.land("left", 1, k, 1)
            send("core", 2, k, 1)

        def finish():
            for what in list(self.numbers):
                if what[0] == "core":
                    self.land(*what)
            keep().wait()
            for what in list(self.numbers):
                self.copy(*what).wait_send()

        steps = {"own": own, "lines": lines, "finish": finish}
        for k in range(Z):
            steps["line", k] = functools.partial(line, k)
            steps["near", k] = functools.partial(near, k)
            steps["far", k] = functools.partial(far, k)
        return steps

    @staticmethod
    def order(Z):
        names = ["lines", "own"]
        for k in range(Z):
            names += [("line", k + 1)] * (k + 1 < Z) + [("near", k)] + [("far", k - 1)] * (k > 0)
        return names + [("far", Z - 1), "finish"]


def run(plans, names):
    for name in names:
        for plan in plans:
            plan[name]()


def gather_kernel(dp, fsdp, count, *refs):
    mine, full = refs[:count], refs[count:2 * count]
    sems, local = refs[2 * count:3 * count], refs[3 * count]
    g = Grid(dp, fsdp)
    meet(g)
    run([Gather(g, m, f, s, local.at[i]).steps() for i, (m, f, s) in enumerate(zip(mine, full, sems))], Gather.order(fsdp))


def gather_scratch(fsdp, count):
    return [pltpu.SemaphoreType.DMA((2, Gather.copies(fsdp)))] * count + [pltpu.SemaphoreType.DMA((count,))]


def gathered(n, arrays):
    return [jax.ShapeDtypeStruct((n,) + a.shape, a.dtype) for a in arrays]


def gather(mesh, arrays, cid):
    dp, fsdp = mesh.shape["dp"], mesh.shape["fsdp"]
    count = len(arrays)
    anys = [pl.BlockSpec(memory_space=pl.ANY)] * count
    return pl.pallas_call(
        functools.partial(gather_kernel, dp, fsdp, count),
        in_specs=anys, out_specs=anys, out_shape=gathered(dp * fsdp, arrays),
        scratch_shapes=gather_scratch(fsdp, count),
        compiler_params=pltpu.CompilerParams(collective_id=cid, has_side_effects=True),
        name=f"gather{cid}",
    )(*arrays)


class Scatter:
    FAR, RIGHT, LEFT, OWN = 0, 1, 2, 3
    REL = (2, 1, -1, 0)

    def __init__(self, g, part, out, bufs, sems, local):
        self.g, self.part, self.out, self.sems, self.local = g, part, out, sems, local
        self.own, self.sib, self.ra, self.rb, self.rl, self.rr, self.sum, self.rz = bufs
        cols = part.shape[2]
        cut = (cols // 256) * 128
        self.A, self.B = pl.ds(0, cut), pl.ds(cut, cols - cut)

    @staticmethod
    def buffers(Z, rows, cols, dtype):
        cut = (cols // 256) * 128
        shapes = [(4, Z, rows, cols), (4, Z, rows, cols), (Z, rows, max(cut, 1)), (Z, rows, cols - cut), (Z, rows, cols), (Z, rows, cols),
                  (Z, rows, cols), (max(Z - 1, 1), rows, cols)]
        return [pltpu.VMEM(s, dtype) for s in shapes]

    @staticmethod
    def scratch(Z, rows, cols, dtype):
        return Scatter.buffers(Z, rows, cols, dtype) + [pltpu.SemaphoreType.DMA((2, 4 + 2 + 2 + Z - 1)), pltpu.SemaphoreType.DMA((4,))]

    def steps(self):
        g, Z = self.g, self.g.Z
        A, B = self.A, self.B
        cut = A.size
        dt = self.own.dtype
        right, left, sibling = g.at(1), g.at(-1), g.at(core=1 - g.core)
        loads = [pltpu.make_async_copy(self.part.at[pl.ds(g.place(d) * 2 * Z + g.core * Z, Z)], self.own.at[i], self.local.at[i])
                 for i, d in enumerate(self.REL)]
        cores = [remote(self.part.at[pl.ds(g.place(d) * 2 * Z + (1 - g.core) * Z, Z)], self.sib.at[i], self.sems, i, sibling)
                 for i, d in enumerate(self.REL)]
        far = [remote(self.own.at[self.FAR, :, :, A], self.ra, self.sems, 4, right)] if cut else []
        far += [remote(self.own.at[self.FAR, :, :, B], self.rb, self.sems, 5, left)]
        near = [remote(self.own.at[self.RIGHT], self.rl, self.sems, 6, right), remote(self.own.at[self.LEFT], self.rr, self.sems, 7, left)]
        lines = [remote(self.sum.at[(g.z + k) % Z], self.rz.at[k - 1], self.sems, 7 + k, g.at(k=k)) for k in range(1, Z)]

        def begin():
            for a, b in zip(loads, cores):
                b.start()
                a.start()

        def take(i):
            loads[i].wait()
            cores[i].wait_recv()

        def do_far():
            take(self.FAR)
            for z in range(Z):
                self.own[self.FAR, z] = (self.own[self.FAR, z].astype(F32) + self.sib[self.FAR, z].astype(F32)).astype(dt)
            for c in far:
                c.start()

        def do_near():
            take(self.RIGHT)
            take(self.LEFT)
            for c in far:
                c.wait_recv()
            for z in range(Z):
                for i, got, has, rest in ((self.RIGHT, self.ra, A, B), (self.LEFT, self.rb, B, A)):
                    if has.size:
                        self.own[i, z, :, has] = (self.own[i, z, :, has].astype(F32) + self.sib[i, z, :, has].astype(F32) + got[z].astype(F32)).astype(dt)
                    if rest.size:
                        self.own[i, z, :, rest] = (self.own[i, z, :, rest].astype(F32) + self.sib[i, z, :, rest].astype(F32)).astype(dt)
            for c in near:
                c.start()

        def do_own():
            take(self.OWN)
            for c in near:
                c.wait_recv()
            for z in range(Z):
                s = self.own[self.OWN, z].astype(F32) + self.sib[self.OWN, z].astype(F32) + self.rl[z].astype(F32) + self.rr[z].astype(F32)
                self.sum[z] = s.astype(dt)
            for c in lines:
                c.start()

        def finish():
            for c in lines:
                c.wait_recv()
            s = self.sum[g.z].astype(F32)
            for k in range(1, Z):
                s += self.rz[k - 1].astype(F32)
            self.out[...] = s
            for c in cores + far + near + lines:
                c.wait_send()

        return {"begin": begin, "far": do_far, "near": do_near, "own": do_own, "finish": finish}

    ORDER = ("begin", "far", "near", "own", "finish")


def scatter_kernel(dp, fsdp, layout, *refs):
    parts = [w for out in layout for w in out]
    n = len(parts)
    ins, outs, rest = refs[:n], refs[n:n + len(layout)], refs[n + len(layout):]
    g = Grid(dp, fsdp)
    meet(g)
    runs, at = [], 0
    for o, widths in zip(outs, layout):
        off = 0
        for w in widths:
            bufs, sems, local = rest[:8], rest[8], rest[9]
            rest = rest[10:]
            runs.append(Scatter(g, ins[at], o.at[:, pl.ds(off, w)], bufs, sems, local).steps())
            at, off = at + 1, off + w
    run(runs, Scatter.ORDER)


def scatter(mesh, groups, cid):
    dp, fsdp = mesh.shape["dp"], mesh.shape["fsdp"]
    parts = [p for gr in groups for p in gr]
    rows = parts[0].shape[1]
    layout = [[p.shape[2] for p in gr] for gr in groups]
    scratch = [x for p in parts for x in Scatter.scratch(fsdp, rows, p.shape[2], p.dtype)]
    return pl.pallas_call(
        functools.partial(scatter_kernel, dp, fsdp, layout),
        in_specs=[pl.BlockSpec(memory_space=pl.ANY)] * len(parts),
        out_specs=[pl.BlockSpec(memory_space=pltpu.VMEM)] * len(groups),
        out_shape=[jax.ShapeDtypeStruct((rows, sum(ws)), F32) for ws in layout],
        scratch_shapes=scratch,
        compiler_params=pltpu.CompilerParams(collective_id=cid, has_side_effects=True, vmem_limit_bytes=60 * 2**20),
        name=f"scatter{cid}",
    )(*parts)


def dot(a, b, ca, cb):
    return lax.dot_general(a, b, (((ca,), (cb,)), ((), ())), preferred_element_type=F32)


def places(sides_ref, slot, rows):
    a, b, c = sides_ref[slot, 0], sides_ref[slot, 1], sides_ref[slot, 2]
    e1 = a * a
    e2 = e1 + b * b
    e3 = e2 + c * c
    r = lax.broadcasted_iota(jnp.int32, (1, rows), 1)
    in2, in3, out = r >= e1, r >= e2, r >= e3
    seg = in2.astype(jnp.int32) + in3.astype(jnp.int32) + out.astype(jnp.int32)
    start = jnp.where(in3, e2, jnp.where(in2, e1, 0))
    side = jnp.where(in3, c, jnp.where(in2, b, a))
    side = jnp.maximum(side, 1).astype(F32)
    offset = (r - start).astype(F32)
    height = jnp.floor((offset + 0.5) / side)
    across = offset - height * side
    return seg, jnp.where(out, 0.0, height), jnp.where(out, 0.0, across)


def stats(x):
    mean = jnp.mean(x, axis=-1, keepdims=True)
    cen = x - mean
    var = jnp.mean(cen * cen, axis=-1, keepdims=True)
    rstd = lax.rsqrt(var + EPS)
    return cen * rstd, rstd


def ln_back(dn, gain, xhat, rstd):
    e = dn * gain
    m1 = jnp.mean(e, axis=-1, keepdims=True)
    m2 = jnp.mean(e * xhat, axis=-1, keepdims=True)
    return rstd * (e - m1 - xhat * m2)


def attn_fwd_kernel(plan, *refs):
    (sides, tok, wq, wk, wv, rows1, bq, bk, bv, freq), refs = refs[:10], refs[10:]
    step = pl.program_id(0) * pl.num_programs(1) + pl.program_id(1)
    talk = None
    if plan:
        (dp, fsdp, count), schedule = plan
        mine, refs = refs[:count], refs[count:]
    (qT, kT, vT, eT, linv, oT, cosT, sinT), refs = refs[:8], refs[8:]
    if plan:
        full, refs = refs[:count], refs[count:]
        sems, local, refs = refs[:count], refs[count], refs[count + 1:]
        g = Grid(dp, fsdp)
        talk = [Gather(g, m, f, s, local.at[i]).steps() for i, (m, f, s) in enumerate(zip(mine, full, sems))]
    n1, = refs

    def talk_at(point):
        @pl.when(step == min(point, len(schedule) - 2))
        def _():
            if point == 0:
                meet(g)
            for i, name in schedule[point]:
                talk[i][name]()

    if plan:
        for point in range(len(schedule) - 1):
            talk_at(point)
    slot = pl.program_id(1)
    rows = tok.shape[1]
    seg, height, across = places(sides, slot, rows)
    j16 = lax.broadcasted_iota(jnp.int32, (16, rows), 0)
    hit = j16 == seg
    k_aug = jnp.where(hit, 1.0, 0.0).astype(BF16)
    q_aug = jnp.where(hit | (j16 > 3), 0.0, MASKED).astype(BF16)

    @pl.when(pl.program_id(0) == 0)
    def _():
        xhat, _ = stats(tok[0].astype(F32))
        n1[slot] = (xhat * rows1[0:1, :] + rows1[1:2, :]).astype(BF16)

    half = HD // 2
    angle = freq[0] * height + freq[1] * across
    cos = jnp.cos(angle)
    sin = jnp.sin(angle)
    cosT[0] = cos
    sinT[0] = sin
    n = n1[slot]
    xq = dot(wq[...], n, 0, 1) + bq[...]
    xk = dot(wk[...], n, 0, 1) + bk[...]
    xv = (dot(wv[...], n, 0, 1) + bv[...]).astype(BF16)
    vT[0] = xv
    for h in range(GROUP):
        c, s = cos[h * half:(h + 1) * half], sin[h * half:(h + 1) * half]
        lo, mi, hi = h * HD, h * HD + half, (h + 1) * HD
        q1 = (xq[lo:mi] * c - xq[mi:hi] * s) * SCALE
        q2 = (xq[lo:mi] * s + xq[mi:hi] * c) * SCALE
        k1 = xk[lo:mi] * c - xk[mi:hi] * s
        k2 = xk[lo:mi] * s + xk[mi:hi] * c
        q = jnp.concatenate([q1, q2], axis=0).astype(BF16)
        k = jnp.concatenate([k1, k2], axis=0).astype(BF16)
        qT[0, lo:hi] = q
        kT[0, lo:hi] = k
        sT = dot(jnp.concatenate([k, k_aug], axis=0), jnp.concatenate([q, q_aug], axis=0), 0, 0)
        m = jnp.max(sT, axis=0, keepdims=True)
        e = jnp.exp(sT - m)
        inv = 1.0 / jnp.sum(e, axis=0, keepdims=True)
        e = e.astype(BF16)
        eT[h] = e
        linv[0, h:h + 1] = inv
        o = dot(xv[lo:hi], e, 1, 0) * inv
        oT[0, lo:hi] = o.astype(BF16)
    linv[0, GROUP:] = jnp.zeros_like(linv[0, GROUP:])
    if plan:
        talk_at(len(schedule) - 1)


GATHERS = (
    (("own", 1), ("lines", 1), ("own", 0), ("lines", 0), ("own", 2)),
    (("line", 1, 1), ("line", 1, 0), ("near", 0, 1), ("near", 0, 0), ("near", 0, 2), ("lines", 2)),
    (("line", 2, 1), ("line", 2, 0), ("near", 1, 1), ("near", 1, 0), ("far", 0, 1), ("far", 0, 0), ("far", 0, 2), ("line", 3, 1), ("line", 3, 0)),
    (("line", 1, 2), ("near", 2, 1), ("near", 2, 0), ("far", 1, 1), ("far", 1, 0), ("near", 3, 1), ("near", 3, 0)),
    (("line", 2, 2), ("near", 1, 2), ("far", 2, 1), ("far", 2, 0), ("far", 3, 1), ("far", 3, 0), ("line", 3, 2)),
    (("near", 2, 2), ("far", 1, 2), ("near", 3, 2), ("finish", 0)),
    (("far", 2, 2), ("far", 3, 2), ("finish", 1), ("finish", 2)),
)


def schedule_of(Z, table):
    if Z == 4:
        return tuple(tuple((t[-1], t[0] if len(t) == 2 else t[:2]) for t in point) for point in table)
    return ((),) * (len(table) - 1) + (tuple((i, name) for name in Gather.order(Z) for i in range(3)),)


def attn_fwd(mesh, sides, tok, wqkv, rows1, bcol, freq, mine, cid):
    slots, rows, d = tok.shape
    nq = HEADS // GROUP
    gw = GROUP * HD
    sd = jax.ShapeDtypeStruct
    col = lambda off: pl.BlockSpec((d, gw), lambda i, j, off=off: (0, off + i))
    bsp = lambda off: pl.BlockSpec((gw, 1), lambda i, j, off=off: (off + i, 0))
    tr = pl.BlockSpec((1, gw, rows), lambda i, j: (j, i, 0))
    anys, plan, shapes, scratch, params = [], None, [], [], {}
    if mine:
        dp, fsdp = mesh.shape["dp"], mesh.shape["fsdp"]
        anys = [pl.BlockSpec(memory_space=pl.ANY)] * len(mine)
        plan = (dp, fsdp, len(mine)), schedule_of(fsdp, GATHERS)
        shapes, scratch = gathered(dp * fsdp, mine), gather_scratch(fsdp, len(mine))
        params = dict(collective_id=cid, has_side_effects=True)
    return pl.pallas_call(
        functools.partial(attn_fwd_kernel, plan),
        grid=(nq, slots),
        in_specs=[
            pl.BlockSpec(memory_space=pltpu.SMEM),
            pl.BlockSpec((1, rows, d), lambda i, j: (jnp.where(i == 0, j, slots - 1), 0, 0)),
            col(0), col(nq), col(2 * nq),
            pl.BlockSpec((8, d), lambda i, j: (0, 0)),
            bsp(0), bsp(nq), bsp(2 * nq),
            pl.BlockSpec((2, gw // 2, 1), lambda i, j: (0, i, 0)),
            *anys,
        ],
        out_specs=[
            tr, tr, tr,
            pl.BlockSpec((GROUP, rows, rows), lambda i, j: (j * nq + i, 0, 0)),
            pl.BlockSpec((1, 8, rows), lambda i, j: (j * nq + i, 0, 0)),
            tr,
            pl.BlockSpec((1, gw // 2, rows), lambda i, j: (j, i, 0)),
            pl.BlockSpec((1, gw // 2, rows), lambda i, j: (j, i, 0)),
            *anys,
        ],
        out_shape=[
            sd((slots, d, rows), BF16), sd((slots, d, rows), BF16), sd((slots, d, rows), BF16),
            sd((slots * HEADS, rows, rows), BF16),
            sd((slots * nq, 8, rows), F32),
            sd((slots, d, rows), BF16),
            sd((slots, d // 2, rows), F32), sd((slots, d // 2, rows), F32),
            *shapes,
        ],
        scratch_shapes=[*scratch, pltpu.VMEM((slots, rows, d), BF16)],
        compiler_params=pltpu.CompilerParams(vmem_limit_bytes=56 * 2**20, **params),
        name="attn_fwd",
    )(sides, tok, wqkv, wqkv, wqkv, rows1, bcol, bcol, bcol, freq, *(mine or ()))


def mlp_kernel(tok, oT, wo, g, up, dnT, rows2, ub,
               out, mgrad, dup, ddT, small, dub,
               mid, n2, n2T, gT, oacc, dacc):
    f, last = pl.program_id(0), pl.num_programs(0) - 1

    @pl.when(f == 0)
    def _():
        branch = jnp.concatenate([dot(oT[i], wo[...], 0, 0) for i in range(oT.shape[0])], axis=0)
        x = tok[...].astype(F32) + branch + rows2[3:4, :]
        mid[...] = x
        xhat, _ = stats(x)
        n = xhat * rows2[0:1, :] + rows2[1:2, :]
        n2[...] = n.astype(BF16)
        n2T[...] = n.T.astype(BF16)
        gT[...] = g[...].astype(F32).T.astype(BF16)

    v = dot(n2[...], up[...], 1, 0) + ub[...]
    ga = dot(g[...], dnT[...], 1, 0)
    v2 = v * v
    t = jnp.tanh(v * (GELU_A + GELU_B * v2))
    p = 0.5 * t + 0.5
    act = (v * p).astype(BF16)
    slope = p + (0.5 * v) * (1.0 - t * t) * (GELU_A + (3.0 * GELU_B) * v2)
    hg = (slope * ga).astype(BF16)
    o = dot(act, dnT[...], 1, 1)
    dn = dot(hg, up[...], 1, 1)
    ddT[...] = dot(gT[...], act, 1, 0).astype(BF16)
    dup[...] = dot(n2T[...], hg, 1, 0).astype(BF16)
    dub[...] = jnp.sum(hg.astype(F32), axis=0, keepdims=True)

    @pl.when(f == 0)
    def _():
        oacc[...] = o
        dacc[...] = dn

    @pl.when(f > 0)
    def _():
        oacc[...] += o
        dacc[...] += dn

    @pl.when(f == last)
    def _():
        x = mid[...]
        out[...] = (x + oacc[...] + rows2[2:3, :]).astype(BF16)
        xhat, rstd = stats(x)
        dn = dacc[...]
        gf = g[...].astype(F32)
        mg = gf + ln_back(dn, rows2[0:1, :], xhat, rstd)
        mgrad[...] = mg
        small[0:1, :] = jnp.sum(dn * xhat, axis=0, keepdims=True)
        small[1:2, :] = jnp.sum(dn, axis=0, keepdims=True)
        small[2:3, :] = jnp.sum(gf, axis=0, keepdims=True)
        small[3:4, :] = jnp.sum(mg.astype(BF16).astype(F32), axis=0, keepdims=True)
        small[4:8, :] = jnp.zeros_like(small[4:8, :])


def mlp(tok, oT, wo, g, up, dnT, rows2, ub, chunk=512):
    rows, d = tok.shape
    ff = up.shape[1]
    sd = jax.ShapeDtypeStruct
    whole = lambda: pl.BlockSpec((rows, d), lambda f: (0, 0))
    wsp = lambda: pl.BlockSpec((d, chunk), lambda f: (0, f))
    return pl.pallas_call(
        mlp_kernel,
        grid=(ff // chunk,),
        in_specs=[whole(), pl.BlockSpec(oT.shape, lambda f: (0, 0, 0)), pl.BlockSpec(wo.shape, lambda f: (0, 0)), whole(), wsp(), wsp(),
                  pl.BlockSpec((8, d), lambda f: (0, 0)),
                  pl.BlockSpec((1, chunk), lambda f: (0, f))],
        out_specs=[whole(), whole(), wsp(), wsp(),
                   pl.BlockSpec((8, d), lambda f: (0, 0)),
                   pl.BlockSpec((1, chunk), lambda f: (0, f))],
        out_shape=[sd((rows, d), BF16), sd((rows, d), F32), sd((d, ff), BF16), sd((d, ff), BF16),
                   sd((8, d), F32), sd((1, ff), F32)],
        scratch_shapes=[pltpu.VMEM((rows, d), F32), pltpu.VMEM((rows, d), BF16), pltpu.VMEM((d, rows), BF16), pltpu.VMEM((d, rows), BF16),
                        pltpu.VMEM((rows, d), F32), pltpu.VMEM((rows, d), F32)],
        compiler_params=pltpu.CompilerParams(vmem_limit_bytes=60 * 2**20),
        name="mlp",
    )(tok, oT, wo, g, up, dnT, rows2, ub)


def attn_bwd_kernel(plan, *refs):
    (sides, tok, mgrad, wq, wk, wv, wo, rows1, qT, kT, vT, eT, linv, oT, cosT, sinT), refs = refs[:16], refs[16:]
    step = pl.program_id(0) * pl.num_programs(1) + pl.program_id(1)
    if plan:
        (dp, fsdp, count), schedule = plan
        parts, refs = refs[:count], refs[count:]
    (tgrad, dwq, dwk, dwv, dwo, small, dbq, dbk, dbv, dfr), refs = refs[:10], refs[10:]
    if plan:
        sums, refs = refs[:count], refs[count:]
        g, talk = Grid(dp, fsdp), []
        for part, total in zip(parts, sums):
            talk.append(Scatter(g, part, total, refs[:8], refs[8], refs[9]).steps())
            refs = refs[10:]
    n1, mlow, dacc, aq, ak, av, ao = refs

    def talk_at(point):
        @pl.when(step == min(point, len(schedule) - 2))
        def _():
            if point == 0:
                meet(g)
            for i, name in schedule[point]:
                talk[i][name]()

    if plan:
        for point in range(len(schedule) - 1):
            talk_at(point)
    quad, slot = pl.program_id(0), pl.program_id(1)
    lastq = pl.num_programs(0) - 1
    rows = tok.shape[1]
    half = HD // 2
    _, height, across = places(sides, slot, rows)

    @pl.when(quad == 0)
    def _():
        xhat, _ = stats(tok[slot].astype(F32))
        n1[slot] = (xhat * rows1[0:1, :] + rows1[1:2, :]).astype(BF16)
        mlow[slot] = mgrad[slot].astype(BF16)

    ml = mlow[slot]
    dO = dot(wo[...], ml, 1, 1)
    dqs, dks, dvs, fgs = [], [], [], []
    for h in range(GROUP):
        lo, mi, hi = h * HD, h * HD + half, (h + 1) * HD
        c, s = cosT[0, h * half:(h + 1) * half], sinT[0, h * half:(h + 1) * half]
        dof = dO[lo:hi] * linv[0, h:h + 1]
        do = dof.astype(BF16)
        dd = jnp.sum(dof * oT[0, lo:hi].astype(F32), axis=0, keepdims=True)
        dp = dot(vT[0, lo:hi], do, 0, 0)
        e = eT[h]
        ds = (e.astype(F32) * (dp - dd)).astype(BF16)
        dvs.append(dot(do, e, 1, 1))
        dk = dot(qT[0, lo:hi], ds, 1, 1)
        dq = dot(kT[0, lo:hi], ds, 1, 0)
        k = kT[0, lo:hi].astype(F32)
        q = qT[0, lo:hi].astype(F32)
        ang = dq[half:] * q[:half] - dq[:half] * q[half:] + dk[half:] * k[:half] - dk[:half] * k[half:]
        fgs.append(jnp.concatenate([jnp.sum(ang * height, axis=1, keepdims=True),
                                    jnp.sum(ang * across, axis=1, keepdims=True)], axis=1))
        dq = dq * SCALE
        dqs += [dq[:half] * c + dq[half:] * s, dq[half:] * c - dq[:half] * s]
        dks += [dk[:half] * c + dk[half:] * s, dk[half:] * c - dk[:half] * s]
    dq = jnp.concatenate(dqs, axis=0).astype(BF16)
    dk = jnp.concatenate(dks, axis=0).astype(BF16)
    dv = jnp.concatenate(dvs, axis=0).astype(BF16)
    fg = jnp.concatenate(fgs, axis=0)
    n = n1[slot]
    gq, gk, gv = dot(n, dq, 0, 1), dot(n, dk, 0, 1), dot(n, dv, 0, 1)
    go = dot(oT[0], ml, 1, 0)
    bias = lambda x: jnp.sum(x.astype(F32), axis=1, keepdims=True)
    dn = dot(dq, wq[...], 0, 1) + dot(dk, wk[...], 0, 1) + dot(dv, wv[...], 0, 1)

    weights = ((dwq, aq, gq), (dwk, ak, gk), (dwv, av, gv), (dwo, ao, go))
    sums = ((dbq, bias(dq)), (dbk, bias(dk)), (dbv, bias(dv)), (dfr, fg))

    @pl.when(slot == 0)
    def _():
        for _, ref, val in weights:
            ref[...] = val
        for ref, val in sums:
            ref[...] = val

    @pl.when(slot > 0)
    def _():
        for _, ref, val in weights:
            ref[...] += val
        for ref, val in sums:
            ref[...] += val

    @pl.when(slot == pl.num_programs(1) - 1)
    def _():
        for low, ref, _ in weights:
            low[...] = ref[...].astype(BF16)

    @pl.when(quad == 0)
    def _():
        dacc[slot] = dn

    @pl.when(quad > 0)
    def _():
        dacc[slot] += dn

    @pl.when(quad == lastq)
    def _():
        xhat, rstd = stats(tok[slot].astype(F32))
        d = dacc[slot]
        tgrad[slot] = (mgrad[slot] + ln_back(d, rows1[0:1, :], xhat, rstd)).astype(BF16)
        s0 = jnp.sum(d * xhat, axis=0, keepdims=True)
        s1 = jnp.sum(d, axis=0, keepdims=True)

        @pl.when(slot == 0)
        def _():
            small[...] = jnp.zeros_like(small)
        small[0:1, :] += s0
        small[1:2, :] += s1

    if plan:
        talk_at(len(schedule) - 1)


SCATTERS = (
    ((0, "begin"), (1, "begin")),
    ((0, "far"), (1, "far")),
    ((0, "near"),),
    ((1, "near"),),
    ((0, "own"),),
    ((1, "own"),),
    ((0, "finish"), (1, "finish")),
)


def attn_bwd(mesh, sides, tok, mgrad, wqkv, wo, rows1, saved, parts, cid):
    slots, rows, d = tok.shape
    nq = HEADS // GROUP
    gw = GROUP * HD
    sd = jax.ShapeDtypeStruct
    col = lambda off: pl.BlockSpec((d, gw), lambda i, j, off=off: (0, off + i))
    whole = lambda: pl.BlockSpec((slots, rows, d), lambda i, j: (0, 0, 0), pipeline_mode=pl.Buffered(1))
    tr = pl.BlockSpec((1, gw, rows), lambda i, j: (j, i, 0))
    trh = pl.BlockSpec((1, gw // 2, rows), lambda i, j: (j, i, 0))
    gcol = lambda: pl.BlockSpec((d, gw), lambda i, j: (0, i))
    bcol = lambda: pl.BlockSpec((gw, 1), lambda i, j: (i, 0))
    anys, plan, shapes, scratch, params = [], None, [], [], {}
    if parts:
        dp, fsdp = mesh.shape["dp"], mesh.shape["fsdp"]
        anys = [pl.BlockSpec(memory_space=pl.ANY)] * len(parts)
        plan = (dp, fsdp, len(parts)), SCATTERS
        shapes = [sd(x.shape[1:], F32) for x in parts]
        scratch = [y for x in parts for y in Scatter.scratch(fsdp, x.shape[1], x.shape[2], x.dtype)]
        params = dict(collective_id=cid, has_side_effects=True)
    return pl.pallas_call(
        functools.partial(attn_bwd_kernel, plan),
        grid=(nq, slots),
        in_specs=[
            pl.BlockSpec(memory_space=pltpu.SMEM), whole(), whole(),
            col(0), col(nq), col(2 * nq),
            pl.BlockSpec((gw, d), lambda i, j: (i, 0)),
            pl.BlockSpec((8, d), lambda i, j: (0, 0)),
            tr, tr, tr,
            pl.BlockSpec((GROUP, rows, rows), lambda i, j: (j * nq + i, 0, 0)),
            pl.BlockSpec((1, 8, rows), lambda i, j: (j * nq + i, 0, 0)),
            tr, trh, trh, *anys,
        ],
        out_specs=[
            whole(), gcol(), gcol(), gcol(),
            pl.BlockSpec((gw, d), lambda i, j: (i, 0)),
            pl.BlockSpec((8, d), lambda i, j: (0, 0)),
            bcol(), bcol(), bcol(),
            pl.BlockSpec((gw // 2, 2), lambda i, j: (i, 0)),
            *[pl.BlockSpec(x.shape, lambda i, j: (0, 0)) for x in shapes],
        ],
        out_shape=[
            sd((slots, rows, d), BF16), sd((d, d), BF16), sd((d, d), BF16), sd((d, d), BF16), sd((d, d), BF16),
            sd((8, d), F32), sd((d, 1), F32), sd((d, 1), F32), sd((d, 1), F32), sd((d // 2, 2), F32), *shapes,
        ],
        scratch_shapes=[*scratch, pltpu.VMEM((slots, rows, d), BF16), pltpu.VMEM((slots, rows, d), BF16), pltpu.VMEM((slots, rows, d), F32),
                        pltpu.VMEM((d, gw), F32), pltpu.VMEM((d, gw), F32), pltpu.VMEM((d, gw), F32), pltpu.VMEM((gw, d), F32)],
        compiler_params=pltpu.CompilerParams(vmem_limit_bytes=62 * 2**20, **params),
        name="attn_bwd",
    )(sides, tok, mgrad, wqkv, wqkv, wqkv, wo, rows1, *saved, *(parts or ()))


LANES = 128
BOTH = ("dp", "fsdp")


def pack(columns):
    have = jnp.concatenate(columns, axis=-1)
    pad = [(0, 0)] * (have.ndim - 1) + [(0, LANES - have.shape[-1])]
    return jnp.pad(have, pad)


def on_device(mesh, tok, sides, g, attn_norm, wqkv, bqkv, wo, bo, freq, mlp_norm, up, ub, down, db):
    n = mesh.shape["dp"] * mesh.shape["fsdp"]
    slots = sides.shape[0]
    d = tok.shape[1]
    rows = tok.shape[0] // slots
    r = wqkv.shape[0]
    nb, nu = bqkv.shape[0] // r, ub.shape[0] // r
    hand = mesh.shape["dp"] == 8 and r % 8 == 0
    mine = [wqkv, wo, pack([attn_norm.T, bo[:, None], freq[:, None], mlp_norm.T, db[:, None], bqkv.reshape(nb, r).T, ub.reshape(nu, r).T]),
            up, down.T]
    if hand:
        wqkv, small = gather(mesh, [mine[0], mine[2]], 0)
    else:
        wqkv, wo, small, up, dnT = [lax.all_gather(x, BOTH, axis=0) for x in mine]
    small = small.astype(F32)
    lanes = small.reshape(d, LANES).T
    rows1 = jnp.concatenate([lanes[:3], jnp.zeros((5, d), F32)], axis=0)
    rows2 = jnp.concatenate([lanes[4:7], lanes[2:3], jnp.zeros((4, d), F32)], axis=0)
    freq = small[:, :, 3].reshape(2, d // 2, 1)
    bcol = small[:, :, 7:7 + nb].transpose(0, 2, 1).reshape(nb * d, 1)
    urow = small[:, :, 7 + nb:7 + nb + nu].transpose(0, 2, 1).reshape(1, nu * d)

    t3 = tok.reshape(slots, rows, d)
    whole = lambda x: x.reshape(d, -1)
    *saved, = attn_fwd(mesh, sides, t3, whole(wqkv), rows1, bcol, freq, [mine[1], mine[3], mine[4]] if hand else None, 1)
    if hand:
        *saved, wo, up, dnT = saved
    out, mgrad, dup, ddT, small2, dub = mlp(tok, saved[5], whole(wo), g, whole(up), whole(dnT), rows2, urow)
    cut = lambda x: x.reshape(n, r, -1)
    back = attn_bwd(mesh, sides, t3, mgrad.reshape(slots, rows, d), whole(wqkv), whole(wo), rows1, saved, [cut(dup), cut(ddT)] if hand else None, 2)
    tg, dwq, dwk, dwv, dwo, small1, dbq, dbk, dbv, dfr, *sums = back

    small = pack([cut(small1[:2].T), cut(small2[3]), cut(dfr.T), cut(small2[:2].T), cut(small2[2]),
                  jnp.concatenate([dbq, dbk, dbv], axis=0).reshape(n, nb, r).transpose(0, 2, 1),
                  dub.reshape(n, nu, r).transpose(0, 2, 1)])
    parts = [[cut(dwq), cut(dwk), cut(dwv)], [cut(dwo)], [small]]
    if hand:
        sums = [*scatter(mesh, parts, 3), *sums]
    else:
        sums = [jnp.concatenate([lax.psum_scatter(x.astype(F32), BOTH, scatter_dimension=0) for x in p], axis=-1)
                for p in [*parts, [cut(dup)], [cut(ddT)]]]
    gqkv, go, gs, gup, gdT = sums
    return (out, tg.reshape(-1, d), gs[:, :2].T, gqkv, gs[:, 7:7 + nb].T.reshape(-1), go, gs[:, 2], gs[:, 3], gs[:, 4:6].T, gup,
            gs[:, 7 + nb:7 + nb + nu].T.reshape(-1), gdT.T, gs[:, 6])


def solution(mesh):
    row, col, flat = P(BOTH, None), P(None, BOTH), P(BOTH)
    return jax.shard_map(
        functools.partial(on_device, mesh), mesh=mesh,
        in_specs=(row, row, row, col, row, flat, row, flat, flat, col, row, flat, col, flat),
        out_specs=(row, row, col, row, flat, row, flat, flat, col, row, flat, col, flat),
        check_vma=False,
    )
```

```python
import functools
import jax
import jax.numpy as jnp
from jax import lax
from jax.experimental import pallas as pl
from jax.experimental.pallas import tpu as pltpu
from jax.sharding import PartitionSpec as P

HEADS = 12
HD = 64
HALF = HD // 2
GROUP = 4
GROUPS = HEADS // GROUP
GW = GROUP * HD
CHUNK = 512
FIRST = 3
EARLY = 3
PLACES = 32
EPS = 1e-06
SCALE = 0.125
GELU_A = 0.7978845608028654
GELU_B = GELU_A * 0.044715
MASKED = -1e30
LANES = 128
BOTH = ("dp", "fsdp")
F32 = jnp.float32
BF16 = jnp.bfloat16
ANY = pl.BlockSpec(memory_space=pl.ANY)
SD = jax.ShapeDtypeStruct


def dot(a, b, ca, cb):
    return lax.dot_general(a, b, (((ca,), (cb,)), ((), ())), preferred_element_type=F32)


class Grid:
    def __init__(self, dp, fsdp):
        self.P, self.Z = dp // 2, fsdp
        i = lax.axis_index("dp")
        self.core, self.z = i % 2, lax.axis_index("fsdp")
        self.ring = self.turn(i // 2)

    def turn(self, p):
        return p + (p // 2) * (5 - 2 * p)

    def place(self, d):
        return self.turn((self.ring + d + self.P) % self.P)

    def at(self, d=0, core=None, k=0):
        core = self.core if core is None else core
        return (self.place(d) * 2 + core, (self.z + k + self.Z) % self.Z)

    def block(self, d=0, k=0):
        a, b = self.at(d, None, k)
        return self.place(d), self.core, b

    def line(self, d=0):
        return self.place(d), self.core

    def sibling(self):
        return self.at(core=1 - self.core)


def greet(g):
    barrier = pltpu.get_barrier_semaphore()
    for w in [g.at(1), g.at(-1), g.sibling()] + [g.at(k=k) for k in range(1, g.Z)]:
        pl.semaphore_signal(barrier, inc=1, device_id=w, device_id_type=pl.DeviceIdType.MESH)


def met(g):
    pl.semaphore_wait(pltpu.get_barrier_semaphore(), 2 + g.Z)


def remote(src, dst, sems, i, who):
    return pltpu.make_async_remote_copy(src_ref=src, dst_ref=dst, send_sem=sems.at[0, i], recv_sem=sems.at[1, i],
                                        device_id=who, device_id_type=pl.DeviceIdType.MESH)


def halves(cols):
    cut = max(cols // 256, 1) * 128
    return pl.ds(0, cut), pl.ds(cut, cols - cut)


class Gather:
    def __init__(self, g, full, sems):
        self.g, self.full, self.sems = g, full, sems
        cols = full.shape[4]
        self.A, self.B = halves(cols)
        self.whole = cols < 256

    @staticmethod
    def scratch(Z):
        return [pltpu.SemaphoreType.DMA((2, Z - 1 + 5))]

    def lined(self, k):
        own = self.full.at[self.g.block()]
        return remote(own, own, self.sems, k - 1, self.g.at(k=k))

    def col(self, d, part=None):
        ref = self.full.at[self.g.line(d)]
        return ref if part is None else ref.at[:, :, part]

    def far_parts(self):
        return ((-1, 1, self.A), ) if self.whole else ((-1, 1, self.A), (1, -1, self.B))

    def copies(self):
        g = self.g

        def copy(i, ref, who):
            return remote(ref, ref, self.sems, g.Z - 1 + i, who)
        out = {0: copy(0, self.col(0), g.at(1)), 1: copy(1, self.col(0), g.at(-1)), 4: copy(4, self.full.at[:, g.core], g.sibling())}
        for i, (d, to, part) in enumerate(self.far_parts()):
            out[2 + i] = copy(2 + i, self.col(d, part), g.at(to))
        return out

    def arrive(self, i, ref):
        remote(ref, ref, self.sems, i, self.g.sibling()).wait_recv()

    def L(self):
        for k in range(1, self.g.Z):
            self.lined(k).start()

    def N(self):
        g = self.g
        for k in range(1, g.Z):
            self.arrive(k - 1, self.full.at[g.block(k=-k)])
        c = self.copies()
        c[0].start()
        c[1].start()

    def F(self):
        c, n = self.copies(), self.g.Z - 1
        self.arrive(n, self.col(-1))
        c[2].start()
        self.arrive(n + 1, self.col(1))
        if not self.whole:
            c[3].start()

    def T(self):
        n = self.g.Z - 1
        for i, (d, to, part) in enumerate(self.far_parts()):
            self.arrive(n + 2 + i, self.col(2 * d, part))
        self.copies()[4].start()

    def E(self):
        g = self.g
        self.arrive(g.Z - 1 + 4, self.full.at[:, 1 - g.core])
        for k in range(1, g.Z):
            self.lined(k).wait_send()
        for c in self.copies().values():
            c.wait_send()


class Scatter:
    def __init__(self, g, part, write, bufs, sems):
        self.g, self.part, self.write, self.sems = g, part, write, sems
        self.sib, self.ra, self.rb, self.rl, self.rr, self.rz = bufs
        cols = part.shape[4]
        self.A, self.B = halves(cols)
        self.whole = cols < 256

    @staticmethod
    def scratch(Z, rows, cols, dtype):
        a, b = halves(cols)
        shapes = [(4, Z, rows, cols), (Z, rows, a.size), (Z, rows, max(b.size, LANES)), (Z, rows, cols), (Z, rows, cols), (max(Z - 1, 1), rows, cols)]
        return [pltpu.VMEM(s, dtype) for s in shapes] + [pltpu.SemaphoreType.DMA((2, 5 + Z - 1))]

    def cores(self):
        g = self.g
        return remote(self.part.at[:, 1 - g.core], self.sib, self.sems, 0, g.sibling())

    def far(self):
        g = self.g
        src = self.part.at[g.line(2)]
        a = [remote(src.at[:, :, self.A], self.ra, self.sems, 1, g.at(1))]
        return a if self.whole else a + [remote(src.at[:, :, self.B], self.rb, self.sems, 2, g.at(-1))]

    def near(self):
        g = self.g
        return [remote(self.part.at[g.line(1)], self.rl, self.sems, 3, g.at(1)), remote(self.part.at[g.line(-1)], self.rr, self.sems, 4, g.at(-1))]

    def lines(self):
        g = self.g
        return [remote(self.part.at[g.block(k=k)], self.rz.at[k - 1], self.sems, 4 + k, g.at(k=k)) for k in range(1, g.Z)]

    def add(self, d, got=(), part=slice(None)):
        place, core = self.g.line(d)
        s = self.part[place, core, :, :, part].astype(F32) + self.sib[place, :, :, part].astype(F32)
        for t in got:
            s += t[...].astype(F32)
        self.part[place, core, :, :, part] = s.astype(self.part.dtype)

    def B_(self):
        self.cores().start()

    def F(self):
        self.cores().wait_recv()
        self.add(2)
        for c in self.far():
            c.start()

    def N(self):
        for c in self.far():
            c.wait_recv()
        if self.whole:
            self.add(1, [self.ra])
            self.add(-1)
        else:
            self.add(1, [self.ra], self.A)
            self.add(1, (), self.B)
            self.add(-1, [self.rb], self.B)
            self.add(-1, (), self.A)
        for c in self.near():
            c.start()

    def O(self):
        for c in self.near():
            c.wait_recv()
        self.add(0, [self.rl, self.rr])
        for c in self.lines():
            c.start()

    def E(self):
        for c in self.lines():
            c.wait_recv()
        s = self.part[self.g.block()].astype(F32)
        for k in range(1, self.g.Z):
            s += self.rz[k - 1].astype(F32)
        self.write(s)
        for c in [self.cores()] + self.far() + self.near() + self.lines():
            c.wait_send()


def talk(schedule, step, point, points):
    for at, calls in schedule.items():
        if at % points == point:
            @pl.when(step == at // points)
            def _():
                for call in calls:
                    call()


def places(sides_ref, slot, rows):
    a, b, c = sides_ref[slot, 0], sides_ref[slot, 1], sides_ref[slot, 2]
    e1 = a * a
    e2 = e1 + b * b
    e3 = e2 + c * c
    r = lax.broadcasted_iota(jnp.int32, (1, rows), 1)
    in2, in3, out = r >= e1, r >= e2, r >= e3
    seg = in2.astype(jnp.int32) + in3.astype(jnp.int32) + out.astype(jnp.int32)
    start = jnp.where(in3, e2, jnp.where(in2, e1, 0))
    side = jnp.where(in3, c, jnp.where(in2, b, a))
    side = jnp.maximum(side, 1).astype(F32)
    offset = (r - start).astype(F32)
    height = jnp.floor((offset + 0.5) / side)
    across = offset - height * side
    return seg, jnp.where(out, 0.0, height), jnp.where(out, 0.0, across)


def stats(x):
    mean = jnp.mean(x, axis=-1, keepdims=True)
    cen = x - mean
    var = jnp.mean(cen * cen, axis=-1, keepdims=True)
    rstd = lax.rsqrt(var + EPS)
    return cen * rstd, rstd


def ln_back(dn, gain, xhat, rstd):
    e = dn * gain
    m1 = jnp.mean(e, axis=-1, keepdims=True)
    m2 = jnp.mean(e * xhat, axis=-1, keepdims=True)
    return rstd * (e - m1 - xhat * m2)


def flat(w):
    return w.reshape(-1, w.shape[-1])


def unflat(w, like):
    return w.reshape(*like, -1, w.shape[1])


ROWS = ("gain", "shift", "out_bias", "freq", "gain_two", "shift_two", "down_bias", "qkv_bias", "up_bias")


def vectors(small, r, nb, nu):
    n = small.shape[0]
    rows = jnp.concatenate([small[i, 0:8, :r] for i in range(n)], axis=1)
    qkv = jnp.concatenate([small[i, 0:8, :nb * r] for i in range(n)], axis=1)
    up = jnp.concatenate([small[i, 8:16, :nu * r] for i in range(n)], axis=1)
    return rows, qkv, up


def spread(rows, qkv, up, n, store):
    r, rq, ru = rows.shape[1] // n, qkv.shape[1] // n, up.shape[1] // n
    wide = lambda x: jnp.concatenate([x, jnp.zeros((x.shape[0], LANES - x.shape[1]), F32)], axis=1)
    for i in range(n):
        store(i, jnp.concatenate([wide(rows[0:7, i * r:(i + 1) * r]), wide(qkv[:, i * rq:(i + 1) * rq]), wide(up[:, i * ru:(i + 1) * ru]),
                                  jnp.zeros((7, LANES), F32)], axis=0))


def attn_fwd_kernel(plan, *refs):
    sides, tok, *refs = refs
    quad, slot = pl.program_id(0), pl.program_id(1)
    step = quad * pl.num_programs(1) + slot
    schedule = {}
    if plan:
        dp, fsdp, r, nb, nu = plan
        wqkv, wo, up, dnT, small, *refs = refs
        qT, kT, vT, eT, linv, oT, cosT, sinT, rows, urow, wqkv_all, wo_all, chunks, *refs = refs
        n1, trig, w, bcol, fcol, small_all, local, *sems = refs
        g = Grid(dp, fsdp)
        own = g.block()
        mines = []

        def mine(src, dst):
            mines.append(pltpu.make_async_copy(src, dst, local.at[len(mines)]))
        mine(small, small_all.at[own])
        mine(wo, wo_all.at[own])
        for i in range(GROUPS):
            for j in range(3):
                mine(wqkv.at[:, pl.ds((j * GROUPS + i) * GW, GW)], w.at[(i, *own)].at[:, pl.ds(j * GW, GW)])
        for f in range(FIRST):
            for j, src in enumerate((up, dnT)):
                mine(src.at[:, pl.ds(f * CHUNK, CHUNK)], chunks.at[(f, *own)].at[:, pl.ds(j * CHUNK, CHUNK)])
        saves = [pltpu.make_async_copy(w.at[i], wqkv_all.at[i], local.at[len(mines) + i]) for i in range(GROUPS)]
        wholes = [small_all, *(w.at[i] for i in range(GROUPS)), wo_all, *(chunks.at[f] for f in range(FIRST))]
        s, *rest = [Gather(g, a, b) for a, b in zip(wholes, sems)]
        q, o, c = rest[:GROUPS], rest[GROUPS], rest[GROUPS + 1:]

        def ready(a, b):
            for m in mines[a:b]:
                m.wait()

        def begin():
            for m in mines:
                m.start()
            greet(g)

        def then():
            ready(0, 1)
            ready(2, 5)
            met(g)
            s.L()
            q[0].L()
            ready(5, 2 + 3 * GROUPS)
            for call in (s.N, q[0].N, q[1].L, s.F, q[0].F, s.T, q[0].T, q[1].N, q[2].L, s.E, q[0].E, saves[0].start):
                call()
            sm = small_all[...].astype(F32).reshape(-1, 16, LANES)
            vec, qkv, upb = vectors(sm, r, nb, nu)
            rows[...] = vec
            urow[...] = upb
            bcol[...] = qkv.T[:, 7:8]
            fcol[...] = vec.T[:, 3:4]

        chunk = lambda f: functools.partial(ready, 2 + 3 * GROUPS + 2 * f, 4 + 3 * GROUPS + 2 * f)
        schedule = {
            0: [chunk(0), c[0].L],
            1: [chunk(2), c[2].L, q[2].N],
            2: [q[1].F, chunk(1), c[1].L, c[0].N, functools.partial(ready, 1, 2), o.L],
            3: [q[2].F, q[1].T],
            4: [q[1].E, saves[1].start, c[2].N],
            5: [c[1].N],
            6: [c[0].F, o.N, q[2].T],
            7: [q[2].E, saves[2].start],
            8: [c[1].F],
            9: [c[0].T, c[2].F],
            10: [o.F],
            11: [c[1].T, c[2].T, c[0].E, o.T],
        }
        finish = [c[1].E, c[2].E, o.E, *(x.wait for x in saves)]
        weight = lambda: flat(w[quad])
    else:
        w, rows, bcol, fcol, qT, kT, vT, eT, linv, oT, cosT, sinT, n1, trig = refs
        weight = lambda: flat(w[0])
    t = tok.shape[1]

    @pl.when(step == 0)
    def _():
        if plan:
            begin()
        for i in range(tok.shape[0]):
            n1[i] = stats(tok[i].astype(F32))[0]
        if plan:
            then()
        for i in range(tok.shape[0]):
            n1[i] = n1[i] * rows[0:1, :] + rows[1:2, :]

    talk(schedule, step, 0, 2)
    seg, height, across = places(sides, slot, t)

    @pl.when(slot == 0)
    def _():
        lane = lax.broadcasted_iota(jnp.int32, (GW // 2, LANES), 1).astype(F32)
        low = pl.ds(pl.multiple_of(quad * (GW // 2), GW // 2), GW // 2)
        high = pl.ds(pl.multiple_of(fcol.shape[0] // 2 + quad * (GW // 2), GW // 2), GW // 2)
        angle = jnp.where(lane < PLACES, fcol[low] * lane, fcol[high] * (lane - PLACES))
        rest = jnp.concatenate([jnp.cos(angle), jnp.sin(angle)], axis=0)[:, :2 * PLACES]
        parts = []
        for _ in range(3):
            parts.append(rest.astype(BF16))
            rest = rest - parts[-1].astype(F32)
        trig[...] = jnp.concatenate(parts + [jnp.zeros_like(parts[0])], axis=1)

    k256 = lax.broadcasted_iota(jnp.int32, (8 * PLACES, t), 0) % (2 * PLACES)
    pick = lambda v: jnp.where(k256 == v, 1.0, 0.0).astype(BF16)
    by_height = dot(trig[...], pick(height.astype(jnp.int32)), 1, 0)
    by_across = dot(trig[...], pick(across.astype(jnp.int32) + PLACES), 1, 0)
    ch, sh, ca, sa = by_height[:GW // 2], by_height[GW // 2:], by_across[:GW // 2], by_across[GW // 2:]
    cos = ch * ca - sh * sa
    sin = sh * ca + ch * sa
    cosT[0] = cos
    sinT[0] = sin
    j16 = lax.broadcasted_iota(jnp.int32, (16, t), 0)
    hit = j16 == seg
    k_aug = jnp.where(hit, 1.0, 0.0).astype(BF16)
    q_aug = jnp.where(hit | (j16 > 3), 0.0, MASKED).astype(BF16)
    n = n1[slot].astype(BF16)
    x = dot(weight(), n, 0, 1)
    nd = bcol.shape[0] // 3
    bias = jnp.concatenate([bcol[pl.ds(pl.multiple_of(j * nd + quad * GW, GW), GW)] for j in range(3)], axis=0)
    x = x + bias
    xq, xk, xv = x[:GW], x[GW:2 * GW], x[2 * GW:].astype(BF16)
    vT[0] = xv
    qs, ks = [], []
    for h in range(GROUP):
        c_, s_ = cos[h * HALF:(h + 1) * HALF], sin[h * HALF:(h + 1) * HALF]
        lo, mi, hi = h * HD, h * HD + HALF, (h + 1) * HD
        q_ = jnp.concatenate([(xq[lo:mi] * c_ - xq[mi:hi] * s_) * SCALE, (xq[lo:mi] * s_ + xq[mi:hi] * c_) * SCALE], axis=0).astype(BF16)
        k_ = jnp.concatenate([xk[lo:mi] * c_ - xk[mi:hi] * s_, xk[lo:mi] * s_ + xk[mi:hi] * c_], axis=0).astype(BF16)
        qT[0, lo:hi] = q_
        kT[0, lo:hi] = k_
        qs.append(jnp.concatenate([q_, q_aug], axis=0))
        ks.append(jnp.concatenate([k_, k_aug], axis=0))
    sT = dot(ks[0], qs[0], 0, 0)
    for h in range(GROUP):
        if h == GROUP // 2:
            talk(schedule, step, 1, 2)
        now = sT
        if h + 1 < GROUP:
            sT = dot(ks[h + 1], qs[h + 1], 0, 0)
        lo, hi = h * HD, (h + 1) * HD
        m = jnp.max(now, axis=0, keepdims=True)
        e = jnp.exp(now - m)
        inv = 1.0 / jnp.sum(e, axis=0, keepdims=True)
        e = e.astype(BF16)
        eT[h] = e
        linv[0, h:h + 1] = inv
        oT[0, lo:hi] = (dot(xv[lo:hi], e, 1, 0) * inv).astype(BF16)
    linv[0, GROUP:] = jnp.zeros_like(linv[0, GROUP:])
    if plan:
        talk({0: finish}, step - 2 * GROUPS + 1, 0, 1)


def attn_fwd(mesh, sides, tok, args, hand):
    slots, t, d = tok.shape
    fixed = lambda s: pl.BlockSpec(s, lambda i, j: (0,) * len(s))
    tr = pl.BlockSpec((1, GW, t), lambda i, j: (j, i, 0))
    trh = pl.BlockSpec((1, GW // 2, t), lambda i, j: (j, i, 0))
    specs = [tr, tr, tr, pl.BlockSpec((GROUP, t, t), lambda i, j: (j * GROUPS + i, 0, 0)),
             pl.BlockSpec((1, 8, t), lambda i, j: (j * GROUPS + i, 0, 0)), tr, trh, trh]
    shapes = [SD((slots, d, t), BF16)] * 3 + [SD((slots * HEADS, t, t), BF16), SD((slots * GROUPS, 8, t), F32), SD((slots, d, t), BF16)]
    shapes += [SD((slots, d // 2, t), F32)] * 2
    scratch = [pltpu.VMEM((slots, t, d), F32), pltpu.VMEM((GW, 8 * PLACES), BF16)]
    plan, params = None, {}
    if hand:
        dp, fsdp = mesh.shape["dp"], mesh.shape["fsdp"]
        wqkv, wo, up, dnT, small = args
        r = wqkv.shape[0]
        nb, nu = wqkv.shape[1] // d, up.shape[1] // d
        plan = dp, fsdp, r, nb, nu
        in_specs = [ANY] * 5
        specs += [fixed((8, d)), fixed((8, up.shape[1])), ANY, ANY, ANY]
        n = dp // 2, 2, fsdp
        shapes += [SD((8, d), F32), SD((8, up.shape[1]), F32), SD((GROUPS, *n, r, 3 * GW), BF16), SD((*n, r, d), BF16), SD((FIRST, *n, r, 2 * CHUNK), BF16)]
        scratch += [pltpu.VMEM((GROUPS, *n, r, 3 * GW), BF16), pltpu.VMEM((nb * d, 1), F32), pltpu.VMEM((d, 1), F32), pltpu.VMEM((*n, 16, LANES), BF16),
                    pltpu.SemaphoreType.DMA((2 + 4 * GROUPS + 2 * FIRST,))]
        scratch += Gather.scratch(fsdp) * (2 + GROUPS + FIRST)
        params = dict(collective_id=0, has_side_effects=True)
    else:
        w, rows, bcol, fcol = args
        in_specs = [pl.BlockSpec((1, d, 3 * GW), lambda i, j: (i, 0, 0)), fixed(rows.shape), fixed(bcol.shape), fixed(fcol.shape)]
    return pl.pallas_call(
        functools.partial(attn_fwd_kernel, plan),
        grid=(GROUPS, slots),
        in_specs=[pl.BlockSpec(memory_space=pltpu.SMEM), fixed(tok.shape), *in_specs],
        out_specs=specs, out_shape=shapes, scratch_shapes=scratch,
        compiler_params=pltpu.CompilerParams(vmem_limit_bytes=60 * 2**20, **params),
        name="attn_fwd",
    )(sides, tok, *args)


def mlp_kernel(plan, *refs):
    tok, oT, wo, g_, rows, ub, *refs = refs
    f, last = pl.program_id(0), pl.num_programs(0) - 1
    schedule = {}
    if plan:
        dp, fsdp, count = plan
        chunks, up, dnT, out, mgrad, small, dub, dwo, late, early, *refs = refs
        w, local, n2, act, hg, oacc, dacc, *refs = refs
        g = Grid(dp, fsdp)
        mines = [pltpu.make_async_copy(src.at[:, pl.ds((FIRST + i) * CHUNK, CHUNK)], w.at[(FIRST + i, *g.block())].at[:, pl.ds(j * CHUNK, CHUNK)],
                                       local.at[2 * i + j])
                 for i in range(count - FIRST) for j, src in enumerate((up, dnT))]
        loads = [pltpu.make_async_copy(chunks.at[i], w.at[i], local.at[len(mines) + i]) for i in range(FIRST)]
        outs = [pltpu.make_async_copy(w.at[i], late.at[i - EARLY], local.at[len(mines) + i]) for i in range(EARLY, count)]
        c = {FIRST + i: Gather(g, w.at[FIRST + i], refs[i]) for i in range(count - FIRST)}
        refs = refs[count - FIRST:]

        def keep(i):
            def write(s):
                early[i] = s
            return write
        rs = [Scatter(g, w.at[i], keep(i), refs[7 * i:7 * i + 6], refs[7 * i + 6]) for i in range(EARLY)]

        def begin():
            for m in loads + mines:
                m.start()
            greet(g)

        def then():
            for m in mines:
                m.wait()
            met(g)
            c[3].L()
            loads[0].wait()
        schedule = {
            0: [c[4].L],
            4: [loads[1].wait, c[3].N, c[5].L],
            5: [rs[0].B_, c[4].N],
            7: [rs[0].F],
            8: [loads[2].wait, c[3].F],
            9: [rs[1].B_, c[4].F, c[5].N],
            10: [c[3].T, rs[1].F, rs[0].N],
            11: [c[4].T],
            12: [c[3].E, rs[2].B_],
            13: [c[4].E, rs[2].F],
            14: [c[5].F],
            16: [rs[1].N, rs[0].O, outs[0].start],
            17: [c[5].T, rs[2].N],
            19: [c[5].E],
            20: [rs[1].O, outs[1].start],
            21: [rs[2].O],
            22: [rs[0].E],
        }
        finish = [outs[2].start], [rs[2].E, rs[1].E, *(x.wait for x in outs)]
        weight = lambda: w[f]
    else:
        w, out, mgrad, small, dub, dwo, dw, n2, act, hg, oacc, dacc = refs
        weight = lambda: w[0]
    mid = mgrad

    @pl.when(f == 0)
    def _():
        if plan:
            begin()
        slots = oT.shape[0]
        branch = jnp.concatenate([dot(oT[i], flat(wo[...]), 0, 0) for i in range(slots)], axis=0)
        x = tok[...].astype(F32) + branch + rows[2:3, :]
        mid[...] = x
        xhat, _ = stats(x)
        n2[...] = (xhat * rows[4:5, :] + rows[5:6, :]).astype(BF16)
        oacc[...] = x + rows[6:7, :]
        if plan:
            then()

    talk(schedule, f, 0, 4)
    v = dot(n2[...], flat(weight()[..., :CHUNK]), 1, 0) + ub[0:1, :]
    ga = dot(g_[...], flat(weight()[..., CHUNK:]), 1, 0)
    v2 = v * v
    t = jnp.tanh(v * (GELU_A + GELU_B * v2))
    p = 0.5 * t + 0.5
    act[...] = (v * p).astype(BF16)
    slope = p + (0.5 * v) * (1.0 - t * t) * (GELU_A + (3.0 * GELU_B) * v2)
    low = (slope * ga).astype(BF16)
    hg[...] = low
    dub[...] = jnp.sum(low.astype(F32), axis=0, keepdims=True)
    talk(schedule, f, 1, 4)
    oacc[...] += dot(act[...], flat(weight()[..., CHUNK:]), 1, 1)
    dn = dot(hg[...], flat(weight()[..., :CHUNK]), 1, 1)

    @pl.when(f == 0)
    def _():
        dacc[...] = dn

    @pl.when(f > 0)
    def _():
        dacc[...] += dn

    talk(schedule, f, 2, 4)
    for point, cols, a, b in ((3, slice(0, CHUNK), n2, hg), (None, slice(CHUNK, None), g_, act)):
        grad = dot(a[...], b[...], 0, 0)
        if plan:
            w[f, :, :, :, :, cols] = unflat(grad, w.shape[1:4]).astype(BF16)
        else:
            dw[0, :, cols] = grad.astype(BF16)
        if point:
            talk(schedule, f, point, 4)

    @pl.when(f == last)
    def _():
        if plan:
            for call in finish[0]:
                call()
        out[...] = oacc[...].astype(BF16)
        xhat, rstd = stats(mid[...])
        dn = dacc[...]
        gf = g_[...].astype(F32)
        mg = gf + ln_back(dn, rows[4:5, :], xhat, rstd)
        mgrad[...] = mg
        low = mg.astype(BF16)
        small[4:5, :] = jnp.sum(dn * xhat, axis=0, keepdims=True)
        small[5:6, :] = jnp.sum(dn, axis=0, keepdims=True)
        small[6:7, :] = jnp.sum(gf, axis=0, keepdims=True)
        small[2:3, :] = jnp.sum(low.astype(F32), axis=0, keepdims=True)
        small[0:2, :] = jnp.zeros_like(small[0:2, :])
        small[3:4, :] = jnp.zeros_like(small[3:4, :])
        small[7:8, :] = jnp.zeros_like(small[7:8, :])
        slots, t = oT.shape[0], oT.shape[2]
        go = dot(oT[0], mg[:t].astype(BF16), 1, 0)
        for i in range(1, slots):
            go += dot(oT[i], mg[i * t:(i + 1) * t].astype(BF16), 1, 0)
        dwo[...] = (unflat(go, dwo.shape[:3]) if plan else go).astype(BF16)
        if plan:
            for call in finish[1]:
                call()


def mlp(mesh, tok, oT, wo, g, rows, urow, args, hand):
    t, d = tok.shape
    ff = urow.shape[1]
    count = ff // CHUNK
    fixed = lambda s: pl.BlockSpec(s, lambda f: (0,) * len(s), pipeline_mode=pl.Buffered(1))
    col = lambda h: pl.BlockSpec((h, CHUNK), lambda f: (0, f))
    specs = [fixed((t, d)), fixed((t, d)), fixed((8, d)), col(1), fixed(wo.shape)]
    shapes = [SD((t, d), BF16), SD((t, d), F32), SD((8, d), F32), SD((1, ff), F32), SD(wo.shape, BF16)]
    scratch = [pltpu.VMEM((t, d), BF16), pltpu.VMEM((t, CHUNK), BF16), pltpu.VMEM((t, CHUNK), BF16), pltpu.VMEM((t, d), F32), pltpu.VMEM((t, d), F32)]
    plan, params = None, {}
    if hand:
        dp, fsdp = mesh.shape["dp"], mesh.shape["fsdp"]
        chunks, up, dnT = args
        *n, r, w2 = chunks.shape[1:]
        plan = dp, fsdp, count
        in_specs = [ANY] * 3
        specs += [ANY, fixed((EARLY, r, w2))]
        shapes += [SD((count - EARLY, *n, r, w2), BF16), SD((EARLY, r, w2), F32)]
        scratch = [pltpu.VMEM((count, *n, r, w2), BF16), pltpu.SemaphoreType.DMA((2 * (count - FIRST) + count,)), *scratch]
        scratch += Gather.scratch(fsdp) * (count - FIRST) + Scatter.scratch(fsdp, r, w2, BF16) * EARLY
        params = dict(collective_id=1, has_side_effects=True)
    else:
        wide = pl.BlockSpec((1, d, 2 * CHUNK), lambda f: (f, 0, 0))
        in_specs = [wide]
        specs += [wide]
        shapes += [SD((count, d, 2 * CHUNK), BF16)]
    return pl.pallas_call(
        functools.partial(mlp_kernel, plan),
        grid=(count,),
        in_specs=[fixed((t, d)), fixed(oT.shape), fixed(wo.shape), fixed((t, d)), fixed((8, d)), col(8), *in_specs],
        out_specs=specs, out_shape=shapes, scratch_shapes=scratch,
        compiler_params=pltpu.CompilerParams(vmem_limit_bytes=62 * 2**20, **params),
        name="mlp",
    )(tok, oT, wo, g, rows, urow, *args)


def attn_bwd_kernel(plan, *refs):
    sides, tok, mgrad, w, wo, rows, qT, kT, vT, eT, linv, oT, cosT, sinT, *refs = refs
    quad, slot = pl.program_id(0), pl.program_id(1)
    lastq, lasts = pl.num_programs(0) - 1, pl.num_programs(1) - 1
    step = quad * pl.num_programs(1) + slot
    schedule = {}
    tail = [[]] * 3
    if plan:
        dp, fsdp = plan
        small2, dub, dwo, late, tgrad, gqkv, go, gs, gl, *refs = refs
        n1, dacc, mg, vec, qb, px, po, pq, ps, local, *refs = refs
        g = Grid(dp, fsdp)
        count = late.shape[0]
        loads = [pltpu.make_async_copy(late.at[i], px.at[i], local.at[i]) for i in range(count)] + [pltpu.make_async_copy(dwo, po, local.at[count])]
        units = []

        def unit(part, write):
            nonlocal refs
            units.append(Scatter(g, part, write, refs[:6], refs[6]))
            refs = refs[7:]
            return units[-1]

        def into(ref, i=None):
            def write(s):
                if i is None:
                    ref[...] = s
                else:
                    ref[i] = s
            return write
        x = [unit(px.at[i], into(gl, i)) for i in range(count)]
        o = unit(po, into(go))

        def quads(i):
            def write(s):
                for j in range(3):
                    gqkv[:, (j * GROUPS + i) * GW:(j * GROUPS + i + 1) * GW] = s[:, j * GW:(j + 1) * GW]
            return write
        q = [unit(pq.at[i], quads(i)) for i in range(GROUPS)]
        sm = unit(ps, into(gs))

        def begin():
            for m in loads:
                m.start()
            greet(g)

        def then():
            met(g)
            loads[-1].wait()
            o.B_()

        schedule = {
            1: [loads[0].wait, x[0].B_, loads[1].wait, x[1].B_],
            3: [o.F, x[0].F, loads[2].wait, x[2].B_],
            4: [x[1].F],
            5: [x[2].F, o.N],
            6: [q[0].B_, x[0].N],
            7: [x[2].N, q[0].F],
            9: [x[0].O, x[1].N],
            12: [q[1].B_, o.O],
            13: [q[1].F, x[2].O, x[1].O, q[0].N],
            14: [q[1].N],
            15: [q[0].O],
            16: [x[0].E, q[1].O, x[2].E],
            17: [o.E],
        }
        tail = [[q[2].B_], [sm.B_, q[2].F, sm.F, q[0].E, x[1].E, q[2].N, sm.N, q[1].E, q[2].O, sm.O, q[2].E, sm.E]]
        weight = lambda: flat(w[0])
    else:
        tgrad, dwqkv, vec, qb, n1, dacc, mg = refs
        weight = lambda: flat(w[0])
    t = tok.shape[1]

    @pl.when(step == 0)
    def _():
        if plan:
            begin()
        for i in range(tok.shape[0]):
            xhat, _ = stats(tok[i].astype(F32))
            n1[i] = (xhat * rows[0:1, :] + rows[1:2, :]).astype(BF16)
        vec[...] = small2[...] if plan else jnp.zeros_like(vec)
        qb[...] = jnp.zeros_like(qb)
        if plan:
            then()

    talk(schedule, step, 0, 3)
    _, height, across = places(sides, slot, t)
    ml = mgrad[slot].astype(BF16)
    wo_q = pl.ds(pl.multiple_of(quad * GW, GW), GW)
    dO = dot(wo[wo_q], ml, 1, 1)
    dqs, dks, dvs, angs = [], [], [], []
    for h in range(GROUP):
        if h == GROUP // 2:
            talk(schedule, step, 1, 3)
        lo, mi, hi = h * HD, h * HD + HALF, (h + 1) * HD
        c_, s_ = cosT[0, h * HALF:(h + 1) * HALF], sinT[0, h * HALF:(h + 1) * HALF]
        dof = dO[lo:hi] * linv[0, h:h + 1]
        do = dof.astype(BF16)
        dd = jnp.sum(dof * oT[0, lo:hi].astype(F32), axis=0, keepdims=True)
        dp_ = dot(vT[0, lo:hi], do, 0, 0)
        e = eT[h]
        ds = (e.astype(F32) * (dp_ - dd)).astype(BF16)
        dvs.append(dot(do, e, 1, 1))
        dk = dot(qT[0, lo:hi], ds, 1, 1)
        dq = dot(kT[0, lo:hi], ds, 1, 0)
        k = kT[0, lo:hi].astype(F32)
        q_ = qT[0, lo:hi].astype(F32)
        angs.append(dq[HALF:] * q_[:HALF] - dq[:HALF] * q_[HALF:] + dk[HALF:] * k[:HALF] - dk[:HALF] * k[HALF:])
        dq = dq * SCALE
        dqs += [dq[:HALF] * c_ + dq[HALF:] * s_, dq[HALF:] * c_ - dq[:HALF] * s_]
        dks += [dk[:HALF] * c_ + dk[HALF:] * s_, dk[HALF:] * c_ - dk[:HALF] * s_]
    m = jnp.concatenate(dqs + dks + dvs, axis=0).astype(BF16)
    mg[slot] = m
    ang = jnp.concatenate(angs, axis=0)
    j8 = lax.broadcasted_iota(jnp.int32, (8, t), 0)
    where = jnp.where(j8 == 0, height, jnp.where(j8 == 1, across, 0.0)).astype(BF16)
    big = ang.astype(BF16)
    fr = dot(where, big, 1, 1) + dot(where, (ang - big.astype(F32)).astype(BF16), 1, 1)
    d = vec.shape[1]
    for a in range(2):
        at = pl.ds(pl.multiple_of(a * (d // 2) + quad * (GW // 2), GW // 2), GW // 2)
        vec[3:4, at] += fr[a:a + 1]
    bias = dot(jnp.ones((8, t), BF16), m, 1, 1)[0:1]
    for j in range(3):
        at = pl.ds(pl.multiple_of(j * d + quad * GW, GW), GW)
        qb[0:1, at] += bias[:, j * GW:(j + 1) * GW]
    talk(schedule, step, 2, 3)

    @pl.when(slot == lasts)
    def _():
        gw = dot(n1[0], mg[0], 0, 1)
        for i in range(1, n1.shape[0]):
            gw += dot(n1[i], mg[i], 0, 1)
        if plan:
            pq[quad] = unflat(gw, pq.shape[1:4]).astype(BF16)
        else:
            dwqkv[0] = gw.astype(BF16)

    if plan:
        @pl.when((quad == lastq) & (slot == lasts))
        def _():
            for call in tail[0]:
                call()

    dn = dot(m, weight(), 0, 1)

    @pl.when(quad == 0)
    def _():
        dacc[slot] = dn

    @pl.when(quad > 0)
    def _():
        dacc[slot] += dn

    @pl.when(quad == lastq)
    def _():
        xhat, rstd = stats(tok[slot].astype(F32))
        dn = dacc[slot]
        tgrad[slot] = (mgrad[slot] + ln_back(dn, rows[0:1, :], xhat, rstd)).astype(BF16)
        vec[0:1, :] += jnp.sum(dn * xhat, axis=0, keepdims=True)
        vec[1:2, :] += jnp.sum(dn, axis=0, keepdims=True)

    if plan:
        @pl.when((quad == lastq) & (slot == lasts))
        def _():
            cs, zs = ps.shape[1:3]

            def store(i, x):
                ps[i // (cs * zs), i // zs % cs, i % zs] = x
            spread(vec[...], qb[0:1, :], dub[...], dp * fsdp, store)
            for call in tail[1]:
                call()


def attn_bwd(mesh, sides, tok, mgrad, w, wo, rows, saved, args, hand):
    slots, t, d = tok.shape
    fixed = lambda s: pl.BlockSpec(s, lambda i, j: (0,) * len(s), pipeline_mode=pl.Buffered(1))
    tr = pl.BlockSpec((1, GW, t), lambda i, j: (j, i, 0))
    trh = pl.BlockSpec((1, GW // 2, t), lambda i, j: (j, i, 0))
    block = lambda s: pl.BlockSpec((1, *s[1:]), lambda i, j: (i,) + (0,) * (len(s) - 1))
    specs = [fixed(tok.shape)]
    shapes = [SD(tok.shape, BF16)]
    scratch = [pltpu.VMEM((slots, t, d), BF16), pltpu.VMEM((slots, t, d), F32), pltpu.VMEM((slots, 3 * GW, t), BF16)]
    vec, qb = (8, d), (8, 3 * d)
    plan, params = None, {}
    if hand:
        dp, fsdp = mesh.shape["dp"], mesh.shape["fsdp"]
        small2, dub, dwo, late = args
        *n, r, _ = dwo.shape
        plan = dp, fsdp
        in_specs = [fixed(small2.shape), fixed(dub.shape), ANY, ANY]
        outs = [(r, 3 * d), (r, d), (16, LANES), (late.shape[0], *late.shape[4:])]
        specs += [fixed(s) for s in outs]
        shapes += [SD(s, F32) for s in outs]
        parts = [*[late.shape[1:]] * late.shape[0], dwo.shape, *[(*n, r, 3 * GW)] * GROUPS]
        scratch += [pltpu.VMEM(vec, F32), pltpu.VMEM(qb, F32), pltpu.VMEM(late.shape, BF16), pltpu.VMEM(dwo.shape, BF16),
                    pltpu.VMEM((GROUPS, *n, r, 3 * GW), BF16), pltpu.VMEM((*n, 16, LANES), F32), pltpu.SemaphoreType.DMA((late.shape[0] + 1,))]
        scratch += [y for s in parts for y in Scatter.scratch(fsdp, s[3], s[4], BF16)] + Scatter.scratch(fsdp, 16, LANES, F32)
        params = dict(collective_id=2, has_side_effects=True)
    else:
        in_specs = []
        specs += [block((GROUPS, d, 3 * GW)), fixed(vec), fixed(qb)]
        shapes += [SD((GROUPS, d, 3 * GW), BF16), SD(vec, F32), SD(qb, F32)]
    return pl.pallas_call(
        functools.partial(attn_bwd_kernel, plan),
        grid=(GROUPS, slots),
        in_specs=[pl.BlockSpec(memory_space=pltpu.SMEM), fixed(tok.shape), fixed(tok.shape), block(w.shape), fixed((d, d)), fixed((8, d)),
                  tr, tr, tr, pl.BlockSpec((GROUP, t, t), lambda i, j: (j * GROUPS + i, 0, 0)), pl.BlockSpec((1, 8, t), lambda i, j: (j * GROUPS + i, 0, 0)),
                  tr, trh, trh, *in_specs],
        out_specs=specs, out_shape=shapes, scratch_shapes=scratch,
        compiler_params=pltpu.CompilerParams(vmem_limit_bytes=62 * 2**20, **params),
        name="attn_bwd",
    )(sides, tok, mgrad, w, wo, rows, *saved, *args)


def lay_out_kernel(r, widths, gqkv, go, gs, early, late, an_o, qkv_o, bq_o, o_o, bo_o, f_o, mn_o, up_o, bu_o, dT_o, bd_o):
    qkv_o[...] = gqkv[...]
    o_o[...] = go[...]
    for f, ref in enumerate([early.at[i] for i in range(early.shape[0])] + [late.at[i] for i in range(late.shape[0])]):
        up_o[:, f * CHUNK:(f + 1) * CHUNK] = ref[:, :CHUNK]
        dT_o[:, f * CHUNK:(f + 1) * CHUNK] = ref[:, CHUNK:]
    nb, nu = widths
    an_o[...] = gs[0:2, :r]
    bo_o[...] = gs[2:3, :r]
    f_o[...] = gs[3:4, :r]
    mn_o[...] = gs[4:6, :r]
    bd_o[...] = gs[6:7, :r]
    bq_o[...] = gs[7:8, :nb]
    bu_o[...] = gs[8:9, :nu]


def lay_out(gqkv, go, gs, early, late, nb, nu):
    r, d = go.shape
    ff = (early.shape[0] + late.shape[0]) * CHUNK
    one = lambda w: SD((1, w), F32)
    vm = pl.BlockSpec(memory_space=pltpu.VMEM)
    shapes = [SD((2, r), F32), SD(gqkv.shape, F32), one(nb), SD(go.shape, F32), one(r), one(r), SD((2, r), F32),
              SD((r, ff), F32), one(nu), SD((r, ff), F32), one(r)]
    res = pl.pallas_call(
        functools.partial(lay_out_kernel, r, (nb, nu)),
        in_specs=[vm] * 5, out_specs=[vm] * 11, out_shape=shapes, name="lay_out",
    )(gqkv, go, gs, early, late)
    res = list(res)
    res[9] = res[9].T
    return tuple(x.reshape(-1) if x.shape[0] == 1 else x for x in res)


def on_device(mesh, tok, sides, g, attn_norm, wqkv, bqkv, wo, bo, freq, mlp_norm, up, ub, down, db):
    n = mesh.shape["dp"] * mesh.shape["fsdp"]
    slots = sides.shape[0]
    d = tok.shape[1]
    t = tok.shape[0] // slots
    r = wqkv.shape[0]
    ff = up.shape[1]
    nb, nu = bqkv.shape[0] // r, ub.shape[0] // r
    count = ff // CHUNK
    hand = mesh.shape["dp"] == 8 and r % 8 == 0 and count == 6
    dnT = down.T
    small, at = jnp.zeros((16, LANES), BF16), 0
    for x in (attn_norm, bo, freq, mlp_norm, db, bqkv, ub):
        x = x.reshape(-1, x.shape[-1])
        small += jnp.pad(x, ((at, 16 - at - x.shape[0]), (0, LANES - x.shape[1])))
        at += x.shape[0]
    t3 = tok.reshape(slots, t, d)
    if hand:
        *saved, rows, urow, wqkv, wo, chunks = attn_fwd(mesh, sides, t3, (wqkv, wo, up, dnT, small), True)
        out, mgrad, small2, dub, dwo, late, early = mlp(mesh, tok, saved[5], wo, g, rows, urow, (chunks, up, dnT), True)
        tg, gqkv, go, gs, gl = attn_bwd(mesh, sides, t3, mgrad.reshape(t3.shape), wqkv, wo.reshape(d, d), rows, saved, (small2, dub, dwo, late), True)
        return (out, tg.reshape(-1, d)) + lay_out(gqkv, go, gs, early, gl, nb * r, nu * r)
    else:
        whole = lambda x: lax.all_gather(x, BOTH, axis=0, tiled=True)
        wqkv, wo, up, dnT = (whole(x) for x in (wqkv, wo, up, dnT))
        small = lax.all_gather(small, BOTH, axis=0).astype(F32)
        wide = lambda i, k: small[:, i, :k * r].reshape(1, k * d)
        rows = small[:, :8, :r].transpose(1, 0, 2).reshape(8, d)
        urow = jnp.broadcast_to(wide(8, nu), (8, nu * d))
        w = wqkv.reshape(d, 3, GROUPS, GW).transpose(2, 0, 1, 3).reshape(GROUPS, d, 3 * GW)
        saved = attn_fwd(mesh, sides, t3, (w, rows, wide(7, nb).T, rows[3:4].T), False)
        chunks = jnp.stack([up.reshape(d, count, CHUNK), dnT.reshape(d, count, CHUNK)], axis=2).transpose(1, 0, 2, 3).reshape(count, d, 2 * CHUNK)
        out, mgrad, small2, dub, dwo, dw = mlp(mesh, tok, saved[5], wo, g, rows, urow, (chunks,), False)
        tg, dwqkv, vec, qb = attn_bwd(mesh, sides, t3, mgrad.reshape(t3.shape), w, wo, rows, saved, (), False)
        total = lambda x, ax: lax.psum_scatter(x.astype(F32), BOTH, scatter_dimension=ax, tiled=True)
        gqkv = total(dwqkv.reshape(GROUPS, d, 3, GW).transpose(1, 2, 0, 3).reshape(d, 3 * d), 0)
        go = total(dwo, 0)
        both = total(dw, 1)
        cut = lambda x: jnp.pad(x.reshape(x.shape[0], n, -1).transpose(1, 0, 2), ((0, 0), (0, 0), (0, LANES - x.shape[1] // n)))
        gs = total(jnp.concatenate([cut((vec + small2)[:7]), cut(qb[:1]), cut(dub), jnp.zeros((n, 7, LANES), F32)], axis=1), 0)[0]
    gup = both[:, :, :CHUNK].transpose(1, 0, 2).reshape(r, ff)
    gdT = both[:, :, CHUNK:].transpose(1, 0, 2).reshape(r, ff)
    return (out, tg.reshape(-1, d), gs[0:2, :r], gqkv, gs[7, :nb * r], go, gs[2, :r], gs[3, :r], gs[4:6, :r], gup, gs[8, :nu * r], gdT.T, gs[6, :r])


def solution(mesh):
    row, col, one = P(BOTH, None), P(None, BOTH), P(BOTH)
    return jax.shard_map(
        functools.partial(on_device, mesh), mesh=mesh,
        in_specs=(row, row, row, col, row, one, row, one, one, col, row, one, col, one),
        out_specs=(row, row, col, row, one, row, one, one, col, row, one, col, one),
        check_vma=False,
    )
```

```python
import functools
import jax
import jax.numpy as jnp
from jax import lax
from jax.experimental import pallas as pl
from jax.experimental.pallas import tpu as pltpu
from jax.sharding import PartitionSpec as P

HEADS = 12
HD = 64
HALF = HD // 2
GROUP = 4
GROUPS = HEADS // GROUP
GW = GROUP * HD
CHUNK = 512
FIRST = 3
EARLY = 4
ENDS = ((0,), (1, 2))
PLACES = 32
EPS = 1e-06
SCALE = 0.125
GELU_A = 0.7978845608028654
GELU_B = GELU_A * 0.044715
MASKED = -1e30
LANES = 128
BOTH = ("dp", "fsdp")
F32 = jnp.float32
BF16 = jnp.bfloat16
ANY = pl.BlockSpec(memory_space=pl.ANY)
SD = jax.ShapeDtypeStruct


def dot(a, b, ca, cb):
    return lax.dot_general(a, b, (((ca,), (cb,)), ((), ())), preferred_element_type=F32)


class Grid:
    def __init__(self, dp, fsdp):
        self.P, self.Z = dp // 2, fsdp
        i = lax.axis_index("dp")
        self.core, z = i % 2, lax.axis_index("fsdp")
        ring = self.turn(i // 2)
        self.places = {d: self.turn((ring + d + self.P) % self.P) for d in (-1, 0, 1, 2)}
        self.zs = {k: (z + k + fsdp) % fsdp for k in range(1 - fsdp, fsdp)}

    def turn(self, p):
        return p + (p // 2) * (5 - 2 * p)

    def place(self, d):
        return self.places[2 if d == -2 else d]

    def at(self, d=0, core=None, k=0):
        core = self.core if core is None else core
        return (self.place(d) * 2 + core, self.zs[k])

    def block(self, d=0, k=0):
        return self.place(d), self.core, self.zs[k]

    def line(self, d=0):
        return self.place(d), self.core

    def sibling(self):
        return self.at(core=1 - self.core)


def partners(g, wide):
    if wide:
        return [g.sibling()] + [g.at(d, k=k) for d, k in others(g)]
    return [g.at(1), g.at(-1), g.sibling()] + [g.at(k=k) for k in range(1, g.Z)]


def others(g):
    return [(d, k) for d in (0, 1, -1, 2) for k in range(g.Z) if (d, k) != (0, 0)]


def greet(g, wide=False):
    barrier = pltpu.get_barrier_semaphore()
    for w in partners(g, wide):
        pl.semaphore_signal(barrier, inc=1, device_id=w, device_id_type=pl.DeviceIdType.MESH)


def met(g, wide=False):
    pl.semaphore_wait(pltpu.get_barrier_semaphore(), len(partners(g, wide)))


def remote(src, dst, sems, i, who):
    return pltpu.make_async_remote_copy(src_ref=src, dst_ref=dst, send_sem=sems.at[0, i], recv_sem=sems.at[1, i],
                                        device_id=who, device_id_type=pl.DeviceIdType.MESH)


def halves(cols):
    cut = max(cols // 256, 1) * 128
    return pl.ds(0, cut), pl.ds(cut, cols - cut)


class Gather:
    def __init__(self, g, full, sems):
        self.g, self.full, self.sems = g, full, sems
        cols = full.shape[4]
        self.A, self.B = halves(cols)
        self.whole = cols < 256

    @staticmethod
    def scratch(Z):
        return [pltpu.SemaphoreType.DMA((2, Z - 1 + 5))]

    def lined(self, k):
        own = self.full.at[self.g.block()]
        return remote(own, own, self.sems, k - 1, self.g.at(k=k))

    def col(self, d, part=None):
        ref = self.full.at[self.g.line(d)]
        return ref if part is None else ref.at[:, :, part]

    def far_parts(self):
        return ((-1, 1, self.A), ) if self.whole else ((-1, 1, self.A), (1, -1, self.B))

    def copies(self):
        g = self.g

        def copy(i, ref, who):
            return remote(ref, ref, self.sems, g.Z - 1 + i, who)
        out = {0: copy(0, self.col(0), g.at(1)), 1: copy(1, self.col(0), g.at(-1)), 4: copy(4, self.full.at[:, g.core], g.sibling())}
        for i, (d, to, part) in enumerate(self.far_parts()):
            out[2 + i] = copy(2 + i, self.col(d, part), g.at(to))
        return out

    def arrive(self, i, ref):
        remote(ref, ref, self.sems, i, self.g.sibling()).wait_recv()

    def L(self):
        for k in range(1, self.g.Z):
            self.lined(k).start()

    def N(self):
        g = self.g
        for k in range(1, g.Z):
            self.arrive(k - 1, self.full.at[g.block(k=-k)])
        c = self.copies()
        c[0].start()
        c[1].start()

    def F(self):
        c, n = self.copies(), self.g.Z - 1
        self.arrive(n, self.col(-1))
        c[2].start()
        self.arrive(n + 1, self.col(1))
        if not self.whole:
            c[3].start()

    def T(self):
        n = self.g.Z - 1
        for i, (d, to, part) in enumerate(self.far_parts()):
            self.arrive(n + 2 + i, self.col(2 * d, part))
        self.copies()[4].start()

    def E(self):
        g = self.g
        self.arrive(g.Z - 1 + 4, self.full.at[:, 1 - g.core])
        for k in range(1, g.Z):
            self.lined(k).wait_send()
        for c in self.copies().values():
            c.wait_send()


class Scatter:
    def __init__(self, g, part, write, bufs, sems):
        self.g, self.part, self.write, self.sems = g, part, write, sems
        self.sib, self.ra, self.rb, self.rl, self.rr, self.rz = bufs
        cols = part.shape[4]
        self.A, self.B = halves(cols)
        self.whole = cols < 256

    @staticmethod
    def scratch(Z, rows, cols, dtype):
        a, b = halves(cols)
        shapes = [(4, Z, rows, cols), (Z, rows, a.size), (Z, rows, max(b.size, LANES)), (Z, rows, cols), (Z, rows, cols), (max(Z - 1, 1), rows, cols)]
        return [pltpu.VMEM(s, dtype) for s in shapes] + [pltpu.SemaphoreType.DMA((2, 5 + Z - 1))]

    def cores(self):
        g = self.g
        return remote(self.part.at[:, 1 - g.core], self.sib, self.sems, 0, g.sibling())

    def far(self):
        g = self.g
        src = self.part.at[g.line(2)]
        a = [remote(src.at[:, :, self.A], self.ra, self.sems, 1, g.at(1))]
        return a if self.whole else a + [remote(src.at[:, :, self.B], self.rb, self.sems, 2, g.at(-1))]

    def near(self):
        g = self.g
        return [remote(self.part.at[g.line(1)], self.rl, self.sems, 3, g.at(1)), remote(self.part.at[g.line(-1)], self.rr, self.sems, 4, g.at(-1))]

    def lines(self):
        g = self.g
        return [remote(self.part.at[g.block(k=k)], self.rz.at[k - 1], self.sems, 4 + k, g.at(k=k)) for k in range(1, g.Z)]

    def add(self, d, got=(), part=slice(None)):
        place, core = self.g.line(d)
        s = self.part[place, core, :, :, part].astype(F32) + self.sib[place, :, :, part].astype(F32)
        for t in got:
            s += t[...].astype(F32)
        self.part[place, core, :, :, part] = s.astype(self.part.dtype)

    def B_(self):
        self.cores().start()

    def F(self):
        self.cores().wait_recv()
        self.add(2)
        for c in self.far():
            c.start()

    def N(self):
        for c in self.far():
            c.wait_recv()
        if self.whole:
            self.add(1, [self.ra])
            self.add(-1)
        else:
            self.add(1, [self.ra], self.A)
            self.add(1, (), self.B)
            self.add(-1, [self.rb], self.B)
            self.add(-1, (), self.A)
        for c in self.near():
            c.start()

    def O(self):
        for c in self.near():
            c.wait_recv()
        self.add(0, [self.rl, self.rr])
        for c in self.lines():
            c.start()

    def E(self):
        for c in self.lines():
            c.wait_recv()
        s = self.part[self.g.block()].astype(F32)
        for k in range(1, self.g.Z):
            s += self.rz[k - 1].astype(F32)
        self.write(s)
        for c in [self.cores()] + self.far() + self.near() + self.lines():
            c.wait_send()


class Direct:
    def __init__(self, g, part, out, bufs, sems):
        self.g, self.part, self.out, self.sems = g, part, out, sems
        self.sib, self.got = bufs

    @staticmethod
    def scratch(Z, rows, cols, dtype):
        return [pltpu.VMEM((4, Z, rows, cols), dtype), pltpu.VMEM((4 * Z - 1, rows, cols), dtype), pltpu.SemaphoreType.DMA((2, 4 * Z))]

    def cores(self):
        g = self.g
        return remote(self.part.at[:, 1 - g.core], self.sib, self.sems, 0, g.sibling())

    def sends(self):
        g = self.g
        return [remote(self.part.at[g.block(d, k)], self.got.at[i], self.sems, 1 + i, g.at(d, k=k)) for i, (d, k) in enumerate(others(g))]

    def B_(self):
        self.cores().start()

    def O(self):
        self.cores().wait_recv()
        self.part[:, self.g.core] = self.part[:, self.g.core] + self.sib[...]
        for c in self.sends():
            c.start()

    def E(self):
        s = self.part[self.g.block()]
        for i, c in enumerate(self.sends()):
            c.wait_recv()
            s += self.got[i]
        self.out[...] = s
        for c in [self.cores()] + self.sends():
            c.wait_send()


def talk(schedule, step, point, points):
    for at, calls in schedule.items():
        if at % points == point:
            @pl.when(step == at // points)
            def _():
                for call in calls:
                    call()


def places(sides_ref, slot, rows):
    a, b, c = sides_ref[slot, 0], sides_ref[slot, 1], sides_ref[slot, 2]
    e1 = a * a
    e2 = e1 + b * b
    e3 = e2 + c * c
    r = lax.broadcasted_iota(jnp.int32, (1, rows), 1)
    in2, in3, out = r >= e1, r >= e2, r >= e3
    seg = in2.astype(jnp.int32) + in3.astype(jnp.int32) + out.astype(jnp.int32)
    start = jnp.where(in3, e2, jnp.where(in2, e1, 0))
    side = jnp.where(in3, c, jnp.where(in2, b, a))
    side = jnp.maximum(side, 1).astype(F32)
    offset = (r - start).astype(F32)
    height = jnp.floor((offset + 0.5) / side)
    across = offset - height * side
    return seg, jnp.where(out, 0.0, height), jnp.where(out, 0.0, across)


def stats(x):
    mean = jnp.mean(x, axis=-1, keepdims=True)
    cen = x - mean
    var = jnp.mean(cen * cen, axis=-1, keepdims=True)
    rstd = lax.rsqrt(var + EPS)
    return cen * rstd, rstd


def ln_back(dn, gain, xhat, rstd):
    e = dn * gain
    m1 = jnp.mean(e, axis=-1, keepdims=True)
    m2 = jnp.mean(e * xhat, axis=-1, keepdims=True)
    return rstd * (e - m1 - xhat * m2)


def flat(w):
    return w.reshape(-1, w.shape[-1])


def unflat(w, like):
    return w.reshape(*like, -1, w.shape[1])


VECTORS = ("attn_norm", "out_bias", "frequencies", "mlp_norm", "down_bias", "qkv_bias", "up_bias")


def vectors(small, r, nb, nu):
    n = small.shape[0]
    rows = jnp.concatenate([small[i, 0:8, :r] for i in range(n)], axis=1)
    qkv = jnp.concatenate([small[i, 0:8, :nb * r] for i in range(n)], axis=1)
    up = jnp.concatenate([small[i, 8:16, :nu * r] for i in range(n)], axis=1)
    return rows, qkv, up


def spread(rows, qkv, up, n, store):
    r, rq, ru = rows.shape[1] // n, qkv.shape[1] // n, up.shape[1] // n
    wide = lambda x: jnp.concatenate([x, jnp.zeros((x.shape[0], LANES - x.shape[1]), F32)], axis=1)
    for i in range(n):
        store(i, jnp.concatenate([wide(rows[0:7, i * r:(i + 1) * r]), wide(qkv[:, i * rq:(i + 1) * rq]), wide(up[:, i * ru:(i + 1) * ru]),
                                  jnp.zeros((7, LANES), F32)], axis=0))


def attn_fwd_kernel(plan, *refs):
    sides, tok, *refs = refs
    quad, slot = pl.program_id(0), pl.program_id(1)
    step = quad * pl.num_programs(1) + slot
    schedule = {}
    if plan:
        dp, fsdp, r, nb, nu = plan
        wqkv, wo, up, dnT, *refs = refs
        small, refs = refs[:len(VECTORS)], refs[len(VECTORS):]
        qT, kT, vT, eT, linv, oT, cosT, sinT, rows, urow, wqkv_all, wo_all, chunks, *refs = refs
        n1, trig, w, bcol, fcol, small_all, local, *sems = refs
        g = Grid(dp, fsdp)
        own = g.block()
        mines = []

        def mine(src, dst):
            mines.append(pltpu.make_async_copy(src, dst, local.at[len(mines)]))
        mine(wo, wo_all.at[own])
        for i in range(GROUPS):
            for j in range(3):
                mine(wqkv.at[:, pl.ds((j * GROUPS + i) * GW, GW)], w.at[(i, *own)].at[:, pl.ds(j * GW, GW)])
        for f in range(FIRST):
            for j, src in enumerate((up, dnT)):
                mine(src.at[:, pl.ds(f * CHUNK, CHUNK)], chunks.at[(f, *own)].at[:, pl.ds(j * CHUNK, CHUNK)])
        saves = [pltpu.make_async_copy(w.at[i], wqkv_all.at[i], local.at[len(mines) + i]) for i in range(GROUPS)]
        wholes = [small_all, *(w.at[0, :, :, :, :, pl.ds(js[0] * GW, len(js) * GW)] for js in ENDS), *(w.at[i] for i in range(1, GROUPS)), wo_all,
                  *(chunks.at[f] for f in range(FIRST))]
        s, qa, *rest = [Gather(g, a, b) for a, b in zip(wholes, sems)]
        q, o, c = rest[:GROUPS], rest[GROUPS], rest[GROUPS + 1:]

        def ready(a, b):
            for m in mines[a:b]:
                m.wait()

        def begin():
            for m in mines:
                m.start()
            greet(g)
            wide = [jnp.concatenate([x[...].astype(F32), jnp.zeros((x.shape[0], LANES - x.shape[1]), F32)], axis=1) for x in small]
            small_all[own] = jnp.concatenate(wide + [jnp.zeros((7, LANES), F32)], axis=0).astype(BF16)

        def then():
            ready(1, 4)
            met(g)
            s.L()
            qa.L()
            q[0].L()
            ready(4, 1 + 3 * GROUPS)
            for call in (s.N, qa.N, q[0].N, q[1].L, s.F, qa.F, q[0].F, s.T, qa.T, q[0].T, q[1].N, q[2].L, s.E, qa.E, q[0].E, saves[0].start):
                call()
            sm = small_all[...].astype(F32).reshape(-1, 16, LANES)
            vec, qkv, upb = vectors(sm, r, nb, nu)
            rows[...] = vec
            urow[...] = upb
            bcol[...] = qkv.T[:, 7:8]
            fcol[...] = vec.T[:, 3:4]

        chunk = lambda f: functools.partial(ready, 1 + 3 * GROUPS + 2 * f, 3 + 3 * GROUPS + 2 * f)
        schedule = {
            0: [chunk(0), c[0].L],
            1: [chunk(2), c[2].L, q[2].N],
            2: [q[1].F, chunk(1), c[1].L, c[0].N, functools.partial(ready, 0, 1), o.L],
            3: [q[2].F, q[1].T],
            4: [q[1].E, saves[1].start, c[2].N],
            5: [c[1].N],
            6: [c[0].F, o.N, q[2].T],
            7: [q[2].E, saves[2].start],
            8: [c[1].F],
            9: [c[0].T, c[2].F],
            10: [o.F],
            11: [c[1].T, c[2].T, c[0].E, o.T],
        }
        finish = [c[1].E, c[2].E, o.E, *(x.wait for x in saves)]
        weight = lambda: flat(w[quad])
    else:
        w, rows, bcol, fcol, qT, kT, vT, eT, linv, oT, cosT, sinT, n1, trig = refs
        weight = lambda: flat(w[0])
    t = tok.shape[1]

    @pl.when(step == 0)
    def _():
        if plan:
            begin()
        for i in range(tok.shape[0]):
            n1[i] = stats(tok[i].astype(F32))[0]
        if plan:
            then()
        for i in range(tok.shape[0]):
            n1[i] = n1[i] * rows[0:1, :] + rows[1:2, :]

    talk(schedule, step, 0, 2)
    seg, height, across = places(sides, slot, t)

    @pl.when(slot == 0)
    def _():
        lane = lax.broadcasted_iota(jnp.int32, (GW // 2, LANES), 1).astype(F32)
        low = pl.ds(pl.multiple_of(quad * (GW // 2), GW // 2), GW // 2)
        high = pl.ds(pl.multiple_of(fcol.shape[0] // 2 + quad * (GW // 2), GW // 2), GW // 2)
        angle = jnp.where(lane < PLACES, fcol[low] * lane, fcol[high] * (lane - PLACES))
        rest = jnp.concatenate([jnp.cos(angle), jnp.sin(angle)], axis=0)[:, :2 * PLACES]
        parts = []
        for _ in range(3):
            parts.append(rest.astype(BF16))
            rest = rest - parts[-1].astype(F32)
        trig[...] = jnp.concatenate(parts + [jnp.zeros_like(parts[0])], axis=1)

    k256 = lax.broadcasted_iota(jnp.int32, (8 * PLACES, t), 0) % (2 * PLACES)
    pick = lambda v: jnp.where(k256 == v, 1.0, 0.0).astype(BF16)
    by_height = dot(trig[...], pick(height.astype(jnp.int32)), 1, 0)
    by_across = dot(trig[...], pick(across.astype(jnp.int32) + PLACES), 1, 0)
    ch, sh, ca, sa = by_height[:GW // 2], by_height[GW // 2:], by_across[:GW // 2], by_across[GW // 2:]
    cos = ch * ca - sh * sa
    sin = sh * ca + ch * sa
    cosT[0] = cos
    sinT[0] = sin
    j16 = lax.broadcasted_iota(jnp.int32, (16, t), 0)
    hit = j16 == seg
    k_aug = jnp.where(hit, 1.0, 0.0).astype(BF16)
    q_aug = jnp.where(hit | (j16 > 3), 0.0, MASKED).astype(BF16)
    n = n1[slot].astype(BF16)
    x = dot(weight(), n, 0, 1)
    nd = bcol.shape[0] // 3
    bias = jnp.concatenate([bcol[pl.ds(pl.multiple_of(j * nd + quad * GW, GW), GW)] for j in range(3)], axis=0)
    x = x + bias
    xq, xk, xv = x[:GW], x[GW:2 * GW], x[2 * GW:].astype(BF16)
    vT[0] = xv
    qs, ks = [], []
    for h in range(GROUP):
        c_, s_ = cos[h * HALF:(h + 1) * HALF], sin[h * HALF:(h + 1) * HALF]
        lo, mi, hi = h * HD, h * HD + HALF, (h + 1) * HD
        q_ = jnp.concatenate([(xq[lo:mi] * c_ - xq[mi:hi] * s_) * SCALE, (xq[lo:mi] * s_ + xq[mi:hi] * c_) * SCALE], axis=0).astype(BF16)
        k_ = jnp.concatenate([xk[lo:mi] * c_ - xk[mi:hi] * s_, xk[lo:mi] * s_ + xk[mi:hi] * c_], axis=0).astype(BF16)
        qT[0, lo:hi] = q_
        kT[0, lo:hi] = k_
        qs.append(jnp.concatenate([q_, q_aug], axis=0))
        ks.append(jnp.concatenate([k_, k_aug], axis=0))
    sT = dot(ks[0], qs[0], 0, 0)
    for h in range(GROUP):
        if h == GROUP // 2:
            talk(schedule, step, 1, 2)
        now = sT
        if h + 1 < GROUP:
            sT = dot(ks[h + 1], qs[h + 1], 0, 0)
        lo, hi = h * HD, (h + 1) * HD
        m = jnp.max(now, axis=0, keepdims=True)
        e = jnp.exp(now - m)
        inv = 1.0 / jnp.sum(e, axis=0, keepdims=True)
        e = e.astype(BF16)
        eT[h] = e
        linv[0, h:h + 1] = inv
        oT[0, lo:hi] = (dot(xv[lo:hi], e, 1, 0) * inv).astype(BF16)
    linv[0, GROUP:] = jnp.zeros_like(linv[0, GROUP:])
    if plan:
        talk({0: finish}, step - 2 * GROUPS + 1, 0, 1)


def attn_fwd(mesh, sides, tok, args, hand):
    slots, t, d = tok.shape
    fixed = lambda s: pl.BlockSpec(s, lambda i, j: (0,) * len(s))
    tr = pl.BlockSpec((1, GW, t), lambda i, j: (j, i, 0))
    trh = pl.BlockSpec((1, GW // 2, t), lambda i, j: (j, i, 0))
    specs = [tr, tr, tr, pl.BlockSpec((GROUP, t, t), lambda i, j: (j * GROUPS + i, 0, 0)),
             pl.BlockSpec((1, 8, t), lambda i, j: (j * GROUPS + i, 0, 0)), tr, trh, trh]
    shapes = [SD((slots, d, t), BF16)] * 3 + [SD((slots * HEADS, t, t), BF16), SD((slots * GROUPS, 8, t), F32), SD((slots, d, t), BF16)]
    shapes += [SD((slots, d // 2, t), F32)] * 2
    scratch = [pltpu.VMEM((slots, t, d), F32), pltpu.VMEM((GW, 8 * PLACES), BF16)]
    plan, params = None, {}
    if hand:
        dp, fsdp = mesh.shape["dp"], mesh.shape["fsdp"]
        wqkv, wo, up, dnT, *small = args
        r = wqkv.shape[0]
        nb, nu = wqkv.shape[1] // d, up.shape[1] // d
        plan = dp, fsdp, r, nb, nu
        in_specs = [ANY] * 4 + [fixed(x.shape) for x in small]
        specs += [fixed((8, d)), fixed((8, up.shape[1])), ANY, ANY, ANY]
        n = dp // 2, 2, fsdp
        shapes += [SD((8, d), F32), SD((8, up.shape[1]), F32), SD((GROUPS, *n, r, 3 * GW), BF16), SD((*n, r, d), BF16), SD((FIRST, *n, r, 2 * CHUNK), BF16)]
        scratch += [pltpu.VMEM((GROUPS, *n, r, 3 * GW), BF16), pltpu.VMEM((nb * d, 1), F32), pltpu.VMEM((d, 1), F32), pltpu.VMEM((*n, 16, LANES), BF16),
                    pltpu.SemaphoreType.DMA((1 + 4 * GROUPS + 2 * FIRST,))]
        scratch += Gather.scratch(fsdp) * (3 + GROUPS + FIRST)
        params = dict(collective_id=0, has_side_effects=True)
    else:
        w, rows, bcol, fcol = args
        in_specs = [pl.BlockSpec((1, d, 3 * GW), lambda i, j: (i, 0, 0)), fixed(rows.shape), fixed(bcol.shape), fixed(fcol.shape)]
    return pl.pallas_call(
        functools.partial(attn_fwd_kernel, plan),
        grid=(GROUPS, slots),
        in_specs=[pl.BlockSpec(memory_space=pltpu.SMEM), fixed(tok.shape), *in_specs],
        out_specs=specs, out_shape=shapes, scratch_shapes=scratch,
        compiler_params=pltpu.CompilerParams(vmem_limit_bytes=60 * 2**20, **params),
        name="attn_fwd",
    )(sides, tok, *args)


def mlp_kernel(plan, *refs):
    tok, oT, wo, g_, rows, ub, *refs = refs
    f, last = pl.program_id(0), pl.num_programs(0) - 1
    schedule = {}
    if plan:
        dp, fsdp, count = plan
        chunks, up, dnT, out, mgrad, small, dub, dwo, late, early, *refs = refs
        w, local, n2, act, hg, oacc, dacc, *refs = refs
        g = Grid(dp, fsdp)
        mines = [pltpu.make_async_copy(src.at[:, pl.ds((FIRST + i) * CHUNK, CHUNK)], w.at[(FIRST + i, *g.block())].at[:, pl.ds(j * CHUNK, CHUNK)],
                                       local.at[2 * i + j])
                 for i in range(count - FIRST) for j, src in enumerate((up, dnT))]
        loads = [pltpu.make_async_copy(chunks.at[i], w.at[i], local.at[len(mines) + i]) for i in range(FIRST)]
        outs = [pltpu.make_async_copy(w.at[i], late.at[i - EARLY], local.at[len(mines) + i]) for i in range(EARLY, count)]
        c = {FIRST + i: Gather(g, w.at[FIRST + i], refs[i]) for i in range(count - FIRST)}
        refs = refs[count - FIRST:]

        def keep(i):
            def write(s):
                early[i] = s
            return write
        rs = [Scatter(g, w.at[i], keep(i), refs[7 * i:7 * i + 6], refs[7 * i + 6]) for i in range(EARLY)]

        def begin():
            for m in loads + mines:
                m.start()
            greet(g)

        def then():
            for m in mines:
                m.wait()
            met(g)
            c[3].L()
            loads[0].wait()
        schedule = {
            0: [c[4].L],
            2: [c[5].L],
            4: [loads[1].wait, rs[0].B_, c[3].N],
            5: [c[4].N],
            6: [rs[0].F],
            7: [c[3].F],
            8: [loads[2].wait, rs[1].B_, c[5].N],
            9: [rs[1].F],
            10: [c[3].T, c[4].F],
            12: [c[3].E, rs[2].B_, c[5].F],
            13: [c[4].T, rs[2].F, rs[0].N],
            14: [c[5].T],
            15: [rs[1].N],
            16: [c[4].E, rs[3].B_],
            17: [rs[0].O, rs[3].F],
            18: [rs[2].N],
            19: [rs[1].O],
            20: [c[5].E, rs[3].N, outs[0].start],
            21: [rs[2].O, rs[0].E],
            23: [rs[3].O, rs[1].E],
        }
        finish = [outs[1].start], [rs[2].E, rs[3].E, *(x.wait for x in outs)]
        weight = lambda: w[f]
    else:
        w, out, mgrad, small, dub, dwo, dw, n2, act, hg, oacc, dacc = refs
        weight = lambda: w[0]
    mid = mgrad

    @pl.when(f == 0)
    def _():
        if plan:
            begin()
        slots = oT.shape[0]
        branch = jnp.concatenate([dot(oT[i], flat(wo[...]), 0, 0) for i in range(slots)], axis=0)
        x = tok[...].astype(F32) + branch + rows[2:3, :]
        mid[...] = x
        xhat, _ = stats(x)
        n2[...] = (xhat * rows[4:5, :] + rows[5:6, :]).astype(BF16)
        oacc[...] = x + rows[6:7, :]
        if plan:
            then()

    talk(schedule, f, 0, 4)
    v = dot(n2[...], flat(weight()[..., :CHUNK]), 1, 0) + ub[0:1, :]
    ga = dot(g_[...], flat(weight()[..., CHUNK:]), 1, 0)
    v2 = v * v
    t = jnp.tanh(v * (GELU_A + GELU_B * v2))
    p = 0.5 * t + 0.5
    act[...] = (v * p).astype(BF16)
    slope = p + (0.5 * v) * (1.0 - t * t) * (GELU_A + (3.0 * GELU_B) * v2)
    low = (slope * ga).astype(BF16)
    hg[...] = low
    dub[...] = jnp.sum(low.astype(F32), axis=0, keepdims=True)
    talk(schedule, f, 1, 4)
    oacc[...] += dot(act[...], flat(weight()[..., CHUNK:]), 1, 1)
    dn = dot(hg[...], flat(weight()[..., :CHUNK]), 1, 1)

    @pl.when(f == 0)
    def _():
        dacc[...] = dn

    @pl.when(f > 0)
    def _():
        dacc[...] += dn

    talk(schedule, f, 2, 4)
    for point, cols, a, b in ((3, slice(0, CHUNK), n2, hg), (None, slice(CHUNK, None), g_, act)):
        grad = dot(a[...], b[...], 0, 0)
        if plan:
            w[f, :, :, :, :, cols] = unflat(grad, w.shape[1:4]).astype(BF16)
        else:
            dw[0, :, cols] = grad.astype(BF16)
        if point:
            talk(schedule, f, point, 4)

    @pl.when(f == last)
    def _():
        if plan:
            for call in finish[0]:
                call()
        out[...] = oacc[...].astype(BF16)
        xhat, rstd = stats(mid[...])
        dn = dacc[...]
        gf = g_[...].astype(F32)
        mg = gf + ln_back(dn, rows[4:5, :], xhat, rstd)
        mgrad[...] = mg
        low = mg.astype(BF16)
        small[4:5, :] = jnp.sum(dn * xhat, axis=0, keepdims=True)
        small[5:6, :] = jnp.sum(dn, axis=0, keepdims=True)
        small[6:7, :] = jnp.sum(gf, axis=0, keepdims=True)
        small[2:3, :] = jnp.sum(low.astype(F32), axis=0, keepdims=True)
        small[0:2, :] = jnp.zeros_like(small[0:2, :])
        small[3:4, :] = jnp.zeros_like(small[3:4, :])
        small[7:8, :] = jnp.zeros_like(small[7:8, :])
        slots, t = oT.shape[0], oT.shape[2]
        go = dot(oT[0], mg[:t].astype(BF16), 1, 0)
        for i in range(1, slots):
            go += dot(oT[i], mg[i * t:(i + 1) * t].astype(BF16), 1, 0)
        dwo[...] = (unflat(go, dwo.shape[:3]) if plan else go).astype(BF16)
        if plan:
            for call in finish[1]:
                call()


def mlp(mesh, tok, oT, wo, g, rows, urow, args, hand):
    t, d = tok.shape
    ff = urow.shape[1]
    count = ff // CHUNK
    fixed = lambda s: pl.BlockSpec(s, lambda f: (0,) * len(s), pipeline_mode=pl.Buffered(1))
    col = lambda h: pl.BlockSpec((h, CHUNK), lambda f: (0, f))
    specs = [fixed((t, d)), fixed((t, d)), fixed((8, d)), col(1), fixed(wo.shape)]
    shapes = [SD((t, d), BF16), SD((t, d), F32), SD((8, d), F32), SD((1, ff), F32), SD(wo.shape, BF16)]
    scratch = [pltpu.VMEM((t, d), BF16), pltpu.VMEM((t, CHUNK), BF16), pltpu.VMEM((t, CHUNK), BF16), pltpu.VMEM((t, d), F32), pltpu.VMEM((t, d), F32)]
    plan, params = None, {}
    if hand:
        dp, fsdp = mesh.shape["dp"], mesh.shape["fsdp"]
        chunks, up, dnT = args
        *n, r, w2 = chunks.shape[1:]
        plan = dp, fsdp, count
        in_specs = [ANY] * 3
        specs += [ANY, fixed((EARLY, r, w2))]
        shapes += [SD((count - EARLY, *n, r, w2), BF16), SD((EARLY, r, w2), F32)]
        scratch = [pltpu.VMEM((count, *n, r, w2), BF16), pltpu.SemaphoreType.DMA((2 * (count - FIRST) + count,)), *scratch]
        scratch += Gather.scratch(fsdp) * (count - FIRST) + Scatter.scratch(fsdp, r, w2, BF16) * EARLY
        params = dict(collective_id=1, has_side_effects=True)
    else:
        wide = pl.BlockSpec((1, d, 2 * CHUNK), lambda f: (f, 0, 0))
        in_specs = [wide]
        specs += [wide]
        shapes += [SD((count, d, 2 * CHUNK), BF16)]
    return pl.pallas_call(
        functools.partial(mlp_kernel, plan),
        grid=(count,),
        in_specs=[fixed((t, d)), fixed(oT.shape), fixed(wo.shape), fixed((t, d)), fixed((8, d)), col(8), *in_specs],
        out_specs=specs, out_shape=shapes, scratch_shapes=scratch,
        compiler_params=pltpu.CompilerParams(vmem_limit_bytes=62 * 2**20, **params),
        name="mlp",
    )(tok, oT, wo, g, rows, urow, *args)


def attn_bwd_kernel(plan, *refs):
    sides, tok, mgrad, w, wo, rows, qT, kT, vT, eT, linv, oT, cosT, sinT, *refs = refs
    quad, slot = pl.program_id(0), pl.program_id(1)
    lastq, lasts = pl.num_programs(0) - 1, pl.num_programs(1) - 1
    step = quad * pl.num_programs(1) + slot
    schedule = {}
    tail = [[]] * 3
    if plan:
        dp, fsdp = plan
        small2, dub, dwo, late, tgrad, gqkv, go, gs, gl, *refs = refs
        n1, dacc, mg, vec, qb, px, po, pq, ps, local, *refs = refs
        g = Grid(dp, fsdp)
        count = late.shape[0]
        loads = [pltpu.make_async_copy(late.at[i], px.at[i], local.at[i]) for i in range(count)] + [pltpu.make_async_copy(dwo, po, local.at[count])]
        units = []

        def unit(part, write):
            nonlocal refs
            units.append(Scatter(g, part, write, refs[:6], refs[6]))
            refs = refs[7:]
            return units[-1]

        def into(ref, i=None):
            def write(s):
                if i is None:
                    ref[...] = s
                else:
                    ref[i] = s
            return write
        x = [unit(px.at[i], into(gl, i)) for i in range(count)]
        o = unit(po, into(go))

        def quads(i, js):
            def write(s):
                for j in js:
                    gqkv[:, (j * GROUPS + i) * GW:(j * GROUPS + i + 1) * GW] = s[:, (j - js[0]) * GW:(j - js[0] + 1) * GW]
            return write
        q = [unit(pq.at[i], quads(i, (0, 1, 2))) for i in range(GROUPS - 1)]
        q += [unit(pq.at[GROUPS - 1, :, :, :, :, pl.ds(js[0] * GW, len(js) * GW)], quads(GROUPS - 1, js)) for js in ENDS]
        sm = Direct(g, ps, gs, refs[:2], refs[2])

        def begin():
            for m in loads:
                m.start()
            greet(g, True)

        def then():
            met(g, True)
            loads[-1].wait()
            o.B_()

        schedule = {
            0: [loads[0].wait, x[0].B_],
            2: [loads[1].wait, x[1].B_],
            3: [x[0].F, o.F],
            6: [q[0].B_],
            7: [x[0].N],
            8: [q[0].F, o.N],
            9: [x[1].F],
            12: [q[1].B_, o.O],
            13: [x[1].N],
            14: [q[1].F],
            15: [q[0].N, x[0].O],
            16: [q[1].N],
            17: [x[1].O, q[0].O],
        }
        tail = [[q[2].B_, q[3].B_], [q[2].F, q[3].F, q[1].O, o.E],
                [sm.B_, q[2].N, q[3].N, x[0].E, sm.O, x[1].E, q[0].E, q[1].E, q[2].O, q[3].O, sm.E, q[2].E, q[3].E]]
        weight = lambda: flat(w[0])
    else:
        tgrad, dwqkv, vec, qb, n1, dacc, mg = refs
        weight = lambda: flat(w[0])
    t = tok.shape[1]

    @pl.when(step == 0)
    def _():
        if plan:
            begin()
        for i in range(tok.shape[0]):
            xhat, _ = stats(tok[i].astype(F32))
            n1[i] = (xhat * rows[0:1, :] + rows[1:2, :]).astype(BF16)
        vec[...] = small2[...] if plan else jnp.zeros_like(vec)
        qb[...] = jnp.zeros_like(qb)
        if plan:
            then()

    talk(schedule, step, 0, 3)
    _, height, across = places(sides, slot, t)
    ml = mgrad[slot].astype(BF16)
    wo_q = pl.ds(pl.multiple_of(quad * GW, GW), GW)
    dO = dot(wo[wo_q], ml, 1, 1)
    dqs, dks, dvs, angs = [], [], [], []
    for h in range(GROUP):
        if h == GROUP // 2:
            talk(schedule, step, 1, 3)
        lo, mi, hi = h * HD, h * HD + HALF, (h + 1) * HD
        c_, s_ = cosT[0, h * HALF:(h + 1) * HALF], sinT[0, h * HALF:(h + 1) * HALF]
        dof = dO[lo:hi] * linv[0, h:h + 1]
        do = dof.astype(BF16)
        dd = jnp.sum(dof * oT[0, lo:hi].astype(F32), axis=0, keepdims=True)
        dp_ = dot(vT[0, lo:hi], do, 0, 0)
        e = eT[h]
        ds = (e.astype(F32) * (dp_ - dd)).astype(BF16)
        dvs.append(dot(do, e, 1, 1))
        dk = dot(qT[0, lo:hi], ds, 1, 1)
        dq = dot(kT[0, lo:hi], ds, 1, 0)
        k = kT[0, lo:hi].astype(F32)
        q_ = qT[0, lo:hi].astype(F32)
        angs.append(dq[HALF:] * q_[:HALF] - dq[:HALF] * q_[HALF:] + dk[HALF:] * k[:HALF] - dk[:HALF] * k[HALF:])
        dq = dq * SCALE
        dqs += [dq[:HALF] * c_ + dq[HALF:] * s_, dq[HALF:] * c_ - dq[:HALF] * s_]
        dks += [dk[:HALF] * c_ + dk[HALF:] * s_, dk[HALF:] * c_ - dk[:HALF] * s_]
    m = jnp.concatenate(dqs + dks + dvs, axis=0).astype(BF16)
    mg[slot] = m
    ang = jnp.concatenate(angs, axis=0)
    j8 = lax.broadcasted_iota(jnp.int32, (8, t), 0)
    where = jnp.where(j8 == 0, height, jnp.where(j8 == 1, across, 0.0)).astype(BF16)
    big = ang.astype(BF16)
    fr = dot(where, big, 1, 1) + dot(where, (ang - big.astype(F32)).astype(BF16), 1, 1)
    d = vec.shape[1]
    for a in range(2):
        at = pl.ds(pl.multiple_of(a * (d // 2) + quad * (GW // 2), GW // 2), GW // 2)
        vec[3:4, at] += fr[a:a + 1]
    bias = dot(jnp.ones((8, t), BF16), m, 1, 1)[0:1]
    for j in range(3):
        at = pl.ds(pl.multiple_of(j * d + quad * GW, GW), GW)
        qb[0:1, at] += bias[:, j * GW:(j + 1) * GW]
    talk(schedule, step, 2, 3)

    @pl.when(slot == lasts)
    def _():
        gw = dot(n1[0], mg[0], 0, 1)
        for i in range(1, n1.shape[0]):
            gw += dot(n1[i], mg[i], 0, 1)
        if plan:
            pq[quad] = unflat(gw, pq.shape[1:4]).astype(BF16)
        else:
            dwqkv[0] = gw.astype(BF16)

    if plan:
        @pl.when((quad == lastq) & (slot == lasts))
        def _():
            for call in tail[0]:
                call()

    def gradient(i):
        return dot(mg[i], weight(), 0, 1)

    @pl.when(quad == 0)
    def _():
        dacc[slot] = gradient(slot)

    @pl.when((quad > 0) & (quad < lastq))
    def _():
        dacc[slot] += gradient(slot)

    @pl.when((quad == lastq) & (slot == lasts))
    def _():
        def end(i, carry):
            xhat, rstd = stats(tok[i].astype(F32))
            dn = dacc[i] + gradient(i)
            tgrad[i] = (mgrad[i] + ln_back(dn, rows[0:1, :], xhat, rstd)).astype(BF16)
            vec[0:1, :] += jnp.sum(dn * xhat, axis=0, keepdims=True)
            vec[1:2, :] += jnp.sum(dn, axis=0, keepdims=True)

            @pl.when(i == 0)
            def _():
                for call in tail[1]:
                    call()
            return carry
        lax.fori_loop(0, tok.shape[0], end, 0)
        if plan:
            cs, zs = ps.shape[1:3]

            def store(i, x):
                ps[i // (cs * zs), i // zs % cs, i % zs] = x
            spread(vec[...], qb[0:1, :], dub[...], dp * fsdp, store)
        for call in tail[2]:
            call()


def attn_bwd(mesh, sides, tok, mgrad, w, wo, rows, saved, args, hand):
    slots, t, d = tok.shape
    fixed = lambda s: pl.BlockSpec(s, lambda i, j: (0,) * len(s), pipeline_mode=pl.Buffered(1))
    tr = pl.BlockSpec((1, GW, t), lambda i, j: (j, i, 0))
    trh = pl.BlockSpec((1, GW // 2, t), lambda i, j: (j, i, 0))
    block = lambda s: pl.BlockSpec((1, *s[1:]), lambda i, j: (i,) + (0,) * (len(s) - 1))
    specs = [fixed(tok.shape)]
    shapes = [SD(tok.shape, BF16)]
    scratch = [pltpu.VMEM((slots, t, d), BF16), pltpu.VMEM((slots, t, d), F32), pltpu.VMEM((slots, 3 * GW, t), BF16)]
    vec, qb = (8, d), (8, 3 * d)
    plan, params = None, {}
    if hand:
        dp, fsdp = mesh.shape["dp"], mesh.shape["fsdp"]
        small2, dub, dwo, late = args
        *n, r, _ = dwo.shape
        plan = dp, fsdp
        in_specs = [fixed(small2.shape), fixed(dub.shape), ANY, ANY]
        outs = [(r, 3 * d), (r, d), (16, LANES), (late.shape[0], *late.shape[4:])]
        specs += [fixed(s) for s in outs]
        shapes += [SD(s, F32) for s in outs]
        parts = [*[late.shape[1:]] * late.shape[0], dwo.shape, *[(*n, r, 3 * GW)] * (GROUPS - 1), *[(*n, r, len(js) * GW) for js in ENDS]]
        scratch += [pltpu.VMEM(vec, F32), pltpu.VMEM(qb, F32), pltpu.VMEM(late.shape, BF16), pltpu.VMEM(dwo.shape, BF16),
                    pltpu.VMEM((GROUPS, *n, r, 3 * GW), BF16), pltpu.VMEM((*n, 16, LANES), F32), pltpu.SemaphoreType.DMA((late.shape[0] + 1,))]
        scratch += [y for s in parts for y in Scatter.scratch(fsdp, s[3], s[4], BF16)] + Direct.scratch(fsdp, 16, LANES, F32)
        params = dict(collective_id=2, has_side_effects=True)
    else:
        in_specs = []
        specs += [block((GROUPS, d, 3 * GW)), fixed(vec), fixed(qb)]
        shapes += [SD((GROUPS, d, 3 * GW), BF16), SD(vec, F32), SD(qb, F32)]
    return pl.pallas_call(
        functools.partial(attn_bwd_kernel, plan),
        grid=(GROUPS, slots),
        in_specs=[pl.BlockSpec(memory_space=pltpu.SMEM), fixed(tok.shape), fixed(tok.shape), block(w.shape), fixed((d, d)), fixed((8, d)),
                  tr, tr, tr, pl.BlockSpec((GROUP, t, t), lambda i, j: (j * GROUPS + i, 0, 0)), pl.BlockSpec((1, 8, t), lambda i, j: (j * GROUPS + i, 0, 0)),
                  tr, trh, trh, *in_specs],
        out_specs=specs, out_shape=shapes, scratch_shapes=scratch,
        compiler_params=pltpu.CompilerParams(vmem_limit_bytes=62 * 2**20, **params),
        name="attn_bwd",
    )(sides, tok, mgrad, w, wo, rows, *saved, *args)


def lay_out_kernel(r, widths, gqkv, go, gs, early, late, an_o, qkv_o, bq_o, o_o, bo_o, f_o, mn_o, up_o, bu_o, dT_o, bd_o):
    qkv_o[...] = gqkv[...]
    o_o[...] = go[...]
    for f, ref in enumerate([early.at[i] for i in range(early.shape[0])] + [late.at[i] for i in range(late.shape[0])]):
        up_o[:, f * CHUNK:(f + 1) * CHUNK] = ref[:, :CHUNK]
        dT_o[:, f * CHUNK:(f + 1) * CHUNK] = ref[:, CHUNK:]
    nb, nu = widths
    an_o[...] = gs[0:2, :r]
    bo_o[...] = gs[2:3, :r]
    f_o[...] = gs[3:4, :r]
    mn_o[...] = gs[4:6, :r]
    bd_o[...] = gs[6:7, :r]
    bq_o[...] = gs[7:8, :nb]
    bu_o[...] = gs[8:9, :nu]


def lay_out(gqkv, go, gs, early, late, nb, nu):
    r, d = go.shape
    ff = (early.shape[0] + late.shape[0]) * CHUNK
    one = lambda w: SD((1, w), F32)
    vm = pl.BlockSpec(memory_space=pltpu.VMEM)
    shapes = [SD((2, r), F32), SD(gqkv.shape, F32), one(nb), SD(go.shape, F32), one(r), one(r), SD((2, r), F32),
              SD((r, ff), F32), one(nu), SD((r, ff), F32), one(r)]
    res = pl.pallas_call(
        functools.partial(lay_out_kernel, r, (nb, nu)),
        in_specs=[vm] * 5, out_specs=[vm] * 11, out_shape=shapes, name="lay_out",
    )(gqkv, go, gs, early, late)
    res = list(res)
    res[9] = res[9].T
    return tuple(x.reshape(-1) if x.shape[0] == 1 else x for x in res)


def on_device(mesh, tok, sides, g, attn_norm, wqkv, bqkv, wo, bo, freq, mlp_norm, up, ub, down, db):
    n = mesh.shape["dp"] * mesh.shape["fsdp"]
    slots = sides.shape[0]
    d = tok.shape[1]
    t = tok.shape[0] // slots
    r = wqkv.shape[0]
    ff = up.shape[1]
    nb, nu = bqkv.shape[0] // r, ub.shape[0] // r
    count = ff // CHUNK
    hand = mesh.shape["dp"] == 8 and r % 8 == 0 and count == 6
    dnT = down.T
    small = [x.reshape(-1, x.shape[-1]) for x in (attn_norm, bo, freq, mlp_norm, db, bqkv, ub)]
    t3 = tok.reshape(slots, t, d)
    if hand:
        *saved, rows, urow, wqkv, wo, chunks = attn_fwd(mesh, sides, t3, (wqkv, wo, up, dnT, *small), True)
        out, mgrad, small2, dub, dwo, late, early = mlp(mesh, tok, saved[5], wo, g, rows, urow, (chunks, up, dnT), True)
        tg, gqkv, go, gs, gl = attn_bwd(mesh, sides, t3, mgrad.reshape(t3.shape), wqkv, wo.reshape(d, d), rows, saved, (small2, dub, dwo, late), True)
        return (out, tg.reshape(-1, d)) + lay_out(gqkv, go, gs, early, gl, nb * r, nu * r)
    else:
        whole = lambda x: lax.all_gather(x, BOTH, axis=0, tiled=True)
        wqkv, wo, up, dnT = (whole(x) for x in (wqkv, wo, up, dnT))
        small = jnp.concatenate([jnp.pad(x, ((0, 0), (0, LANES - x.shape[1]))) for x in small] + [jnp.zeros((7, LANES), BF16)], axis=0)
        small = lax.all_gather(small, BOTH, axis=0).astype(F32)
        wide = lambda i, k: small[:, i, :k * r].reshape(1, k * d)
        rows = small[:, :8, :r].transpose(1, 0, 2).reshape(8, d)
        urow = jnp.broadcast_to(wide(8, nu), (8, nu * d))
        w = wqkv.reshape(d, 3, GROUPS, GW).transpose(2, 0, 1, 3).reshape(GROUPS, d, 3 * GW)
        saved = attn_fwd(mesh, sides, t3, (w, rows, wide(7, nb).T, rows[3:4].T), False)
        chunks = jnp.stack([up.reshape(d, count, CHUNK), dnT.reshape(d, count, CHUNK)], axis=2).transpose(1, 0, 2, 3).reshape(count, d, 2 * CHUNK)
        out, mgrad, small2, dub, dwo, dw = mlp(mesh, tok, saved[5], wo, g, rows, urow, (chunks,), False)
        tg, dwqkv, vec, qb = attn_bwd(mesh, sides, t3, mgrad.reshape(t3.shape), w, wo, rows, saved, (), False)
        total = lambda x, ax: lax.psum_scatter(x.astype(F32), BOTH, scatter_dimension=ax, tiled=True)
        gqkv = total(dwqkv.reshape(GROUPS, d, 3, GW).transpose(1, 2, 0, 3).reshape(d, 3 * d), 0)
        go = total(dwo, 0)
        both = total(dw, 1)
        cut = lambda x: jnp.pad(x.reshape(x.shape[0], n, -1).transpose(1, 0, 2), ((0, 0), (0, 0), (0, LANES - x.shape[1] // n)))
        gs = total(jnp.concatenate([cut((vec + small2)[:7]), cut(qb[:1]), cut(dub), jnp.zeros((n, 7, LANES), F32)], axis=1), 0)[0]
    gup = both[:, :, :CHUNK].transpose(1, 0, 2).reshape(r, ff)
    gdT = both[:, :, CHUNK:].transpose(1, 0, 2).reshape(r, ff)
    return (out, tg.reshape(-1, d), gs[0:2, :r], gqkv, gs[7, :nb * r], go, gs[2, :r], gs[3, :r], gs[4:6, :r], gup, gs[8, :nu * r], gdT.T, gs[6, :r])


def solution(mesh):
    row, col, one = P(BOTH, None), P(None, BOTH), P(BOTH)
    return jax.shard_map(
        functools.partial(on_device, mesh), mesh=mesh,
        in_specs=(row, row, row, col, row, one, row, one, one, col, row, one, col, one),
        out_specs=(row, row, col, row, one, row, one, one, col, row, one, col, one),
        check_vma=False,
    )
```

```python
import functools
import jax
import jax.numpy as jnp
from jax import lax
from jax.experimental import pallas as pl
from jax.experimental.pallas import tpu as pltpu
from jax.sharding import PartitionSpec as P

HEADS = 12
HD = 64
HALF = HD // 2
GROUP = 4
GROUPS = HEADS // GROUP
GW = GROUP * HD
CHUNK = 512
FIRST = 3
EARLY = 4
ENDS = ((0,), (1, 2))
PLACES = 32
EPS = 1e-06
SCALE = 0.125
GELU_A = 0.7978845608028654
GELU_B = GELU_A * 0.044715
MASKED = -1e30
LANES = 128
BOTH = ("dp", "fsdp")
F32 = jnp.float32
BF16 = jnp.bfloat16
ANY = pl.BlockSpec(memory_space=pl.ANY)
SD = jax.ShapeDtypeStruct


def dot(a, b, ca, cb):
    return lax.dot_general(a, b, (((ca,), (cb,)), ((), ())), preferred_element_type=F32)


class Grid:
    def __init__(self, dp, fsdp):
        self.P, self.Z = dp // 2, fsdp
        i = lax.axis_index("dp")
        self.core, z = i % 2, lax.axis_index("fsdp")
        ring = self.turn(i // 2)
        self.places = {d: self.turn((ring + d + self.P) % self.P) for d in (-1, 0, 1, 2)}
        self.zs = {k: (z + k + fsdp) % fsdp for k in range(1 - fsdp, fsdp)}

    def turn(self, p):
        return p + (p // 2) * (5 - 2 * p)

    def place(self, d):
        return self.places[2 if d == -2 else d]

    def at(self, d=0, core=None, k=0):
        core = self.core if core is None else core
        return (self.place(d) * 2 + core, self.zs[k])

    def block(self, d=0, k=0):
        return self.place(d), self.core, self.zs[k]

    def line(self, d=0):
        return self.place(d), self.core

    def sibling(self):
        return self.at(core=1 - self.core)


def partners(g, wide):
    if wide:
        return [g.sibling()] + [g.at(d, k=k) for d, k in others(g)]
    return [g.at(1), g.at(-1), g.sibling()] + [g.at(k=k) for k in range(1, g.Z)]


def others(g):
    return [(d, k) for d in (0, 1, -1, 2) for k in range(g.Z) if (d, k) != (0, 0)]


def greet(g, wide=False):
    barrier = pltpu.get_barrier_semaphore()
    for w in partners(g, wide):
        pl.semaphore_signal(barrier, inc=1, device_id=w, device_id_type=pl.DeviceIdType.MESH)


def met(g, wide=False):
    pl.semaphore_wait(pltpu.get_barrier_semaphore(), len(partners(g, wide)))


def remote(src, dst, sems, i, who):
    return pltpu.make_async_remote_copy(src_ref=src, dst_ref=dst, send_sem=sems.at[0, i], recv_sem=sems.at[1, i],
                                        device_id=who, device_id_type=pl.DeviceIdType.MESH)


def halves(cols):
    cut = max(cols // 256, 1) * 128
    return pl.ds(0, cut), pl.ds(cut, cols - cut)


class Gather:
    def __init__(self, g, full, sems):
        self.g, self.full, self.sems = g, full, sems
        cols = full.shape[4]
        self.A, self.B = halves(cols)
        self.whole = cols < 256

    @staticmethod
    def scratch(Z):
        return [pltpu.SemaphoreType.DMA((2, Z - 1 + 5))]

    def lined(self, k):
        own = self.full.at[self.g.block()]
        return remote(own, own, self.sems, k - 1, self.g.at(k=k))

    def col(self, d, part=None):
        ref = self.full.at[self.g.line(d)]
        return ref if part is None else ref.at[:, :, part]

    def far_parts(self):
        return ((-1, 1, self.A), ) if self.whole else ((-1, 1, self.A), (1, -1, self.B))

    def copies(self):
        g = self.g

        def copy(i, ref, who):
            return remote(ref, ref, self.sems, g.Z - 1 + i, who)
        out = {0: copy(0, self.col(0), g.at(1)), 1: copy(1, self.col(0), g.at(-1)), 4: copy(4, self.full.at[:, g.core], g.sibling())}
        for i, (d, to, part) in enumerate(self.far_parts()):
            out[2 + i] = copy(2 + i, self.col(d, part), g.at(to))
        return out

    def arrive(self, i, ref):
        remote(ref, ref, self.sems, i, self.g.sibling()).wait_recv()

    def L(self):
        for k in range(1, self.g.Z):
            self.lined(k).start()

    def N(self):
        g = self.g
        for k in range(1, g.Z):
            self.arrive(k - 1, self.full.at[g.block(k=-k)])
        c = self.copies()
        c[0].start()
        c[1].start()

    def F(self):
        c, n = self.copies(), self.g.Z - 1
        self.arrive(n, self.col(-1))
        c[2].start()
        self.arrive(n + 1, self.col(1))
        if not self.whole:
            c[3].start()

    def T(self):
        n = self.g.Z - 1
        for i, (d, to, part) in enumerate(self.far_parts()):
            self.arrive(n + 2 + i, self.col(2 * d, part))
        self.copies()[4].start()

    def E(self):
        g = self.g
        self.arrive(g.Z - 1 + 4, self.full.at[:, 1 - g.core])
        for k in range(1, g.Z):
            self.lined(k).wait_send()
        for c in self.copies().values():
            c.wait_send()


class Scatter:
    def __init__(self, g, part, write, bufs, sems):
        self.g, self.part, self.write, self.sems = g, part, write, sems
        self.sib, self.ra, self.rb, self.rl, self.rr, self.rz = bufs
        cols = part.shape[4]
        self.A, self.B = halves(cols)
        self.whole = cols < 256

    @staticmethod
    def scratch(Z, rows, cols, dtype):
        a, b = halves(cols)
        shapes = [(4, Z, rows, cols), (Z, rows, a.size), (Z, rows, max(b.size, LANES)), (Z, rows, cols), (Z, rows, cols), (max(Z - 1, 1), rows, cols)]
        return [pltpu.VMEM(s, dtype) for s in shapes] + [pltpu.SemaphoreType.DMA((2, 5 + Z - 1))]

    def cores(self):
        g = self.g
        return remote(self.part.at[:, 1 - g.core], self.sib, self.sems, 0, g.sibling())

    def far(self):
        g = self.g
        src = self.part.at[g.line(2)]
        a = [remote(src.at[:, :, self.A], self.ra, self.sems, 1, g.at(1))]
        return a if self.whole else a + [remote(src.at[:, :, self.B], self.rb, self.sems, 2, g.at(-1))]

    def near(self):
        g = self.g
        return [remote(self.part.at[g.line(1)], self.rl, self.sems, 3, g.at(1)), remote(self.part.at[g.line(-1)], self.rr, self.sems, 4, g.at(-1))]

    def lines(self):
        g = self.g
        return [remote(self.part.at[g.block(k=k)], self.rz.at[k - 1], self.sems, 4 + k, g.at(k=k)) for k in range(1, g.Z)]

    def add(self, d, got=(), part=slice(None)):
        place, core = self.g.line(d)
        s = self.part[place, core, :, :, part].astype(F32) + self.sib[place, :, :, part].astype(F32)
        for t in got:
            s += t[...].astype(F32)
        self.part[place, core, :, :, part] = s.astype(self.part.dtype)

    def B_(self):
        self.cores().start()

    def F(self):
        self.cores().wait_recv()
        self.add(2)
        for c in self.far():
            c.start()

    def N(self):
        for c in self.far():
            c.wait_recv()
        if self.whole:
            self.add(1, [self.ra])
            self.add(-1)
        else:
            self.add(1, [self.ra], self.A)
            self.add(1, (), self.B)
            self.add(-1, [self.rb], self.B)
            self.add(-1, (), self.A)
        for c in self.near():
            c.start()

    def O(self):
        for c in self.near():
            c.wait_recv()
        self.add(0, [self.rl, self.rr])
        for c in self.lines():
            c.start()

    def E(self):
        for c in self.lines():
            c.wait_recv()
        s = self.part[self.g.block()].astype(F32)
        for k in range(1, self.g.Z):
            s += self.rz[k - 1].astype(F32)
        self.write(s)
        for c in [self.cores()] + self.far() + self.near() + self.lines():
            c.wait_send()


class Direct:
    def __init__(self, g, part, out, bufs, sems):
        self.g, self.part, self.out, self.sems = g, part, out, sems
        self.sib, self.got = bufs

    @staticmethod
    def scratch(Z, rows, cols, dtype):
        return [pltpu.VMEM((4, Z, rows, cols), dtype), pltpu.VMEM((4 * Z - 1, rows, cols), dtype), pltpu.SemaphoreType.DMA((2, 4 * Z))]

    def cores(self):
        g = self.g
        return remote(self.part.at[:, 1 - g.core], self.sib, self.sems, 0, g.sibling())

    def sends(self):
        g = self.g
        return [remote(self.part.at[g.block(d, k)], self.got.at[i], self.sems, 1 + i, g.at(d, k=k)) for i, (d, k) in enumerate(others(g))]

    def B_(self):
        self.cores().start()

    def O(self):
        self.cores().wait_recv()
        self.part[:, self.g.core] = self.part[:, self.g.core] + self.sib[...]
        for c in self.sends():
            c.start()

    def E(self):
        s = self.part[self.g.block()]
        for i, c in enumerate(self.sends()):
            c.wait_recv()
            s += self.got[i]
        self.out[...] = s
        for c in [self.cores()] + self.sends():
            c.wait_send()


def talk(schedule, step, point, points):
    for at, calls in schedule.items():
        if at % points == point:
            @pl.when(step == at // points)
            def _():
                for call in calls:
                    call()


def places(sides_ref, slot, rows):
    a, b, c = sides_ref[slot, 0], sides_ref[slot, 1], sides_ref[slot, 2]
    e1 = a * a
    e2 = e1 + b * b
    e3 = e2 + c * c
    r = lax.broadcasted_iota(jnp.int32, (1, rows), 1)
    in2, in3, out = r >= e1, r >= e2, r >= e3
    seg = in2.astype(jnp.int32) + in3.astype(jnp.int32) + out.astype(jnp.int32)
    start = jnp.where(in3, e2, jnp.where(in2, e1, 0))
    side = jnp.where(in3, c, jnp.where(in2, b, a))
    side = jnp.maximum(side, 1).astype(F32)
    offset = (r - start).astype(F32)
    height = jnp.floor((offset + 0.5) / side)
    across = offset - height * side
    return seg, jnp.where(out, 0.0, height), jnp.where(out, 0.0, across)


def stats(x):
    mean = jnp.mean(x, axis=-1, keepdims=True)
    cen = x - mean
    var = jnp.mean(cen * cen, axis=-1, keepdims=True)
    rstd = lax.rsqrt(var + EPS)
    return cen * rstd, rstd


def ln_back(dn, gain, xhat, rstd):
    e = dn * gain
    m1 = jnp.mean(e, axis=-1, keepdims=True)
    m2 = jnp.mean(e * xhat, axis=-1, keepdims=True)
    return rstd * (e - m1 - xhat * m2)


def flat(w):
    return w.reshape(-1, w.shape[-1])


def unflat(w, like):
    return w.reshape(*like, -1, w.shape[1])


VECTORS = ("attn_norm", "out_bias", "frequencies", "mlp_norm", "down_bias", "qkv_bias", "up_bias")


def vectors(small, r, nb, nu):
    n = small.shape[0]
    rows = jnp.concatenate([small[i, 0:8, :r] for i in range(n)], axis=1)
    qkv = jnp.concatenate([small[i, 0:8, :nb * r] for i in range(n)], axis=1)
    up = jnp.concatenate([small[i, 8:16, :nu * r] for i in range(n)], axis=1)
    return rows, qkv, up


def spread(rows, qkv, up, n, store):
    r, rq, ru = rows.shape[1] // n, qkv.shape[1] // n, up.shape[1] // n
    wide = lambda x: jnp.concatenate([x, jnp.zeros((x.shape[0], LANES - x.shape[1]), F32)], axis=1)
    for i in range(n):
        store(i, jnp.concatenate([wide(rows[0:7, i * r:(i + 1) * r]), wide(qkv[:, i * rq:(i + 1) * rq]), wide(up[:, i * ru:(i + 1) * ru]),
                                  jnp.zeros((7, LANES), F32)], axis=0))


def attn_fwd_kernel(plan, *refs):
    sides, tok, *refs = refs
    quad, slot = pl.program_id(0), pl.program_id(1)
    step = quad * pl.num_programs(1) + slot
    schedule = {}
    if plan:
        dp, fsdp, r, nb, nu = plan
        wqkv, wo, up, dnT, *refs = refs
        small, refs = refs[:len(VECTORS)], refs[len(VECTORS):]
        qT, kT, vT, eT, linv, oT, cosT, sinT, rows, urow, wqkv_all, wo_all, chunks, *refs = refs
        n1, trig, w, bcol, fcol, small_all, local, *sems = refs
        g = Grid(dp, fsdp)
        own = g.block()
        mines = []

        def mine(src, dst):
            mines.append(pltpu.make_async_copy(src, dst, local.at[len(mines)]))
        mine(wo, wo_all.at[own])
        for i in range(GROUPS):
            for j in range(3):
                mine(wqkv.at[:, pl.ds((j * GROUPS + i) * GW, GW)], w.at[(i, *own)].at[:, pl.ds(j * GW, GW)])
        for f in range(FIRST):
            for j, src in enumerate((up, dnT)):
                mine(src.at[:, pl.ds(f * CHUNK, CHUNK)], chunks.at[(f, *own)].at[:, pl.ds(j * CHUNK, CHUNK)])
        saves = [pltpu.make_async_copy(w.at[i], wqkv_all.at[i], local.at[len(mines) + i]) for i in range(GROUPS)]
        wholes = [small_all, *(w.at[0, :, :, :, :, pl.ds(js[0] * GW, len(js) * GW)] for js in ENDS), *(w.at[i] for i in range(1, GROUPS)), wo_all,
                  *(chunks.at[f] for f in range(FIRST))]
        s, qa, *rest = [Gather(g, a, b) for a, b in zip(wholes, sems)]
        q, o, c = rest[:GROUPS], rest[GROUPS], rest[GROUPS + 1:]

        def ready(a, b):
            for m in mines[a:b]:
                m.wait()

        def begin():
            for m in mines:
                m.start()
            greet(g)
            wide = [jnp.concatenate([x[...].astype(F32), jnp.zeros((x.shape[0], LANES - x.shape[1]), F32)], axis=1) for x in small]
            small_all[own] = jnp.concatenate(wide + [jnp.zeros((7, LANES), F32)], axis=0).astype(BF16)

        def then():
            ready(1, 4)
            met(g)
            s.L()
            qa.L()
            q[0].L()
            ready(4, 1 + 3 * GROUPS)
            for call in (s.N, qa.N, q[0].N, q[1].L, s.F, qa.F, q[0].F, s.T, qa.T, q[0].T, q[1].N, q[2].L, s.E):
                call()
            sm = small_all[...].astype(F32).reshape(-1, 16, LANES)
            vec, qkv, upb = vectors(sm, r, nb, nu)
            rows[...] = vec
            urow[...] = upb
            bcol[...] = qkv.T[:, 7:8]
            fcol[...] = vec.T[:, 3:4]

        def last():
            for call in (qa.E, q[0].E, saves[0].start):
                call()

        chunk = lambda f: functools.partial(ready, 1 + 3 * GROUPS + 2 * f, 3 + 3 * GROUPS + 2 * f)
        schedule = {
            0: [chunk(0), c[0].L],
            1: [chunk(2), c[2].L, q[2].N],
            2: [q[1].F, chunk(1), c[1].L, c[0].N, functools.partial(ready, 0, 1), o.L],
            3: [q[2].F, q[1].T],
            4: [q[1].E, saves[1].start, c[2].N],
            5: [c[1].N],
            6: [c[0].F, o.N, q[2].T],
            7: [q[2].E, saves[2].start],
            8: [c[1].F],
            9: [c[0].T, c[2].F],
            10: [o.F],
            11: [c[1].T, c[2].T, c[0].E, o.T],
        }
        finish = [c[1].E, c[2].E, o.E, *(x.wait for x in saves)]
        weight = lambda: flat(w[quad])
    else:
        w, rows, bcol, fcol, qT, kT, vT, eT, linv, oT, cosT, sinT, n1, trig = refs
        weight = lambda: flat(w[0])
    t = tok.shape[1]

    @pl.when(step == 0)
    def _():
        if plan:
            begin()
        for i in range(tok.shape[0]):
            n1[i] = stats(tok[i].astype(F32))[0]
        if plan:
            then()
        for i in range(tok.shape[0]):
            n1[i] = n1[i] * rows[0:1, :] + rows[1:2, :]
        if plan:
            last()

    talk(schedule, step, 0, 2)
    seg, height, across = places(sides, slot, t)

    @pl.when(slot == 0)
    def _():
        lane = lax.broadcasted_iota(jnp.int32, (GW // 2, LANES), 1).astype(F32)
        low = pl.ds(pl.multiple_of(quad * (GW // 2), GW // 2), GW // 2)
        high = pl.ds(pl.multiple_of(fcol.shape[0] // 2 + quad * (GW // 2), GW // 2), GW // 2)
        angle = jnp.where(lane < PLACES, fcol[low] * lane, fcol[high] * (lane - PLACES))
        rest = jnp.concatenate([jnp.cos(angle), jnp.sin(angle)], axis=0)[:, :2 * PLACES]
        parts = []
        for _ in range(3):
            parts.append(rest.astype(BF16))
            rest = rest - parts[-1].astype(F32)
        trig[...] = jnp.concatenate(parts + [jnp.zeros_like(parts[0])], axis=1)

    k256 = lax.broadcasted_iota(jnp.int32, (8 * PLACES, t), 0) % (2 * PLACES)
    pick = lambda v: jnp.where(k256 == v, 1.0, 0.0).astype(BF16)
    by_height = dot(trig[...], pick(height.astype(jnp.int32)), 1, 0)
    by_across = dot(trig[...], pick(across.astype(jnp.int32) + PLACES), 1, 0)
    ch, sh, ca, sa = by_height[:GW // 2], by_height[GW // 2:], by_across[:GW // 2], by_across[GW // 2:]
    cos = ch * ca - sh * sa
    sin = sh * ca + ch * sa
    cosT[0] = cos
    sinT[0] = sin
    j16 = lax.broadcasted_iota(jnp.int32, (16, t), 0)
    hit = j16 == seg
    k_aug = jnp.where(hit, 1.0, 0.0).astype(BF16)
    q_aug = jnp.where(hit | (j16 > 3), 0.0, MASKED).astype(BF16)
    n = n1[slot].astype(BF16)
    x = dot(weight(), n, 0, 1)
    nd = bcol.shape[0] // 3
    bias = jnp.concatenate([bcol[pl.ds(pl.multiple_of(j * nd + quad * GW, GW), GW)] for j in range(3)], axis=0)
    x = x + bias
    xq, xk, xv = x[:GW], x[GW:2 * GW], x[2 * GW:].astype(BF16)
    vT[0] = xv
    qs, ks = [], []
    for h in range(GROUP):
        c_, s_ = cos[h * HALF:(h + 1) * HALF], sin[h * HALF:(h + 1) * HALF]
        lo, mi, hi = h * HD, h * HD + HALF, (h + 1) * HD
        q_ = jnp.concatenate([(xq[lo:mi] * c_ - xq[mi:hi] * s_) * SCALE, (xq[lo:mi] * s_ + xq[mi:hi] * c_) * SCALE], axis=0).astype(BF16)
        k_ = jnp.concatenate([xk[lo:mi] * c_ - xk[mi:hi] * s_, xk[lo:mi] * s_ + xk[mi:hi] * c_], axis=0).astype(BF16)
        qT[0, lo:hi] = q_
        kT[0, lo:hi] = k_
        qs.append(jnp.concatenate([q_, q_aug], axis=0))
        ks.append(jnp.concatenate([k_, k_aug], axis=0))
    sT = dot(ks[0], qs[0], 0, 0)
    for h in range(GROUP):
        if h == GROUP // 2:
            talk(schedule, step, 1, 2)
        now = sT
        if h + 1 < GROUP:
            sT = dot(ks[h + 1], qs[h + 1], 0, 0)
        lo, hi = h * HD, (h + 1) * HD
        m = jnp.max(now, axis=0, keepdims=True)
        e = jnp.exp(now - m)
        inv = 1.0 / jnp.sum(e, axis=0, keepdims=True)
        e = e.astype(BF16)
        eT[h] = e
        linv[0, h:h + 1] = inv
        oT[0, lo:hi] = (dot(xv[lo:hi], e, 1, 0) * inv).astype(BF16)
    linv[0, GROUP:] = jnp.zeros_like(linv[0, GROUP:])
    if plan:
        talk({0: finish}, step - 2 * GROUPS + 1, 0, 1)


def attn_fwd(mesh, sides, tok, args, hand):
    slots, t, d = tok.shape
    fixed = lambda s: pl.BlockSpec(s, lambda i, j: (0,) * len(s))
    tr = pl.BlockSpec((1, GW, t), lambda i, j: (j, i, 0))
    trh = pl.BlockSpec((1, GW // 2, t), lambda i, j: (j, i, 0))
    specs = [tr, tr, tr, pl.BlockSpec((GROUP, t, t), lambda i, j: (j * GROUPS + i, 0, 0)),
             pl.BlockSpec((1, 8, t), lambda i, j: (j * GROUPS + i, 0, 0)), tr, trh, trh]
    shapes = [SD((slots, d, t), BF16)] * 3 + [SD((slots * HEADS, t, t), BF16), SD((slots * GROUPS, 8, t), F32), SD((slots, d, t), BF16)]
    shapes += [SD((slots, d // 2, t), F32)] * 2
    scratch = [pltpu.VMEM((slots, t, d), F32), pltpu.VMEM((GW, 8 * PLACES), BF16)]
    plan, params = None, {}
    if hand:
        dp, fsdp = mesh.shape["dp"], mesh.shape["fsdp"]
        wqkv, wo, up, dnT, *small = args
        r = wqkv.shape[0]
        nb, nu = wqkv.shape[1] // d, up.shape[1] // d
        plan = dp, fsdp, r, nb, nu
        in_specs = [ANY] * 4 + [fixed(x.shape) for x in small]
        specs += [fixed((8, d)), fixed((8, up.shape[1])), ANY, ANY, ANY]
        n = dp // 2, 2, fsdp
        shapes += [SD((8, d), F32), SD((8, up.shape[1]), F32), SD((GROUPS, *n, r, 3 * GW), BF16), SD((*n, r, d), BF16), SD((FIRST, *n, r, 2 * CHUNK), BF16)]
        scratch += [pltpu.VMEM((GROUPS, *n, r, 3 * GW), BF16), pltpu.VMEM((nb * d, 1), F32), pltpu.VMEM((d, 1), F32), pltpu.VMEM((*n, 16, LANES), BF16),
                    pltpu.SemaphoreType.DMA((1 + 4 * GROUPS + 2 * FIRST,))]
        scratch += Gather.scratch(fsdp) * (3 + GROUPS + FIRST)
        params = dict(collective_id=0, has_side_effects=True)
    else:
        w, rows, bcol, fcol = args
        in_specs = [pl.BlockSpec((1, d, 3 * GW), lambda i, j: (i, 0, 0)), fixed(rows.shape), fixed(bcol.shape), fixed(fcol.shape)]
    return pl.pallas_call(
        functools.partial(attn_fwd_kernel, plan),
        grid=(GROUPS, slots),
        in_specs=[pl.BlockSpec(memory_space=pltpu.SMEM), fixed(tok.shape), *in_specs],
        out_specs=specs, out_shape=shapes, scratch_shapes=scratch,
        compiler_params=pltpu.CompilerParams(vmem_limit_bytes=60 * 2**20, **params),
        name="attn_fwd",
    )(sides, tok, *args)


def mlp_kernel(plan, *refs):
    tok, oT, wo, g_, rows, ub, *refs = refs
    f, last = pl.program_id(0), pl.num_programs(0) - 1
    schedule = {}
    if plan:
        dp, fsdp, count = plan
        chunks, up, dnT, out, mgrad, small, dub, dwo, late, early, *refs = refs
        w, local, n2, act, hg, oacc, dacc, *refs = refs
        g = Grid(dp, fsdp)
        mines = [pltpu.make_async_copy(src.at[:, pl.ds((FIRST + i) * CHUNK, CHUNK)], w.at[(FIRST + i, *g.block())].at[:, pl.ds(j * CHUNK, CHUNK)],
                                       local.at[2 * i + j])
                 for i in range(count - FIRST) for j, src in enumerate((up, dnT))]
        loads = [pltpu.make_async_copy(chunks.at[i], w.at[i], local.at[len(mines) + i]) for i in range(FIRST)]
        outs = [pltpu.make_async_copy(w.at[i], late.at[i - EARLY], local.at[len(mines) + i]) for i in range(EARLY, count)]
        c = {FIRST + i: Gather(g, w.at[FIRST + i], refs[i]) for i in range(count - FIRST)}
        refs = refs[count - FIRST:]

        def keep(i):
            def write(s):
                early[i] = s
            return write
        rs = [Scatter(g, w.at[i], keep(i), refs[7 * i:7 * i + 6], refs[7 * i + 6]) for i in range(EARLY)]

        def begin():
            for m in loads + mines:
                m.start()
            greet(g)

        def then():
            for m in mines:
                m.wait()
            met(g)
            c[3].L()
            loads[0].wait()
        schedule = {
            0: [c[4].L],
            2: [c[5].L],
            4: [loads[1].wait, rs[0].B_, c[3].N],
            5: [c[4].N],
            6: [rs[0].F],
            7: [c[3].F],
            8: [loads[2].wait, rs[1].B_, c[5].N],
            9: [rs[1].F],
            10: [c[3].T, c[4].F],
            12: [c[3].E, rs[2].B_, c[5].F],
            13: [c[4].T, rs[2].F, rs[0].N],
            14: [c[5].T],
            15: [rs[1].N],
            16: [c[4].E, rs[3].B_],
            17: [rs[0].O, rs[3].F],
            18: [rs[2].N],
            19: [rs[1].O],
            20: [c[5].E, rs[3].N, outs[0].start],
            21: [rs[2].O, rs[0].E],
            23: [rs[3].O, rs[1].E],
        }
        finish = [outs[1].start], [rs[2].E, rs[3].E, *(x.wait for x in outs)]
        weight = lambda: w[f]
    else:
        w, out, mgrad, small, dub, dwo, dw, n2, act, hg, oacc, dacc = refs
        weight = lambda: w[0]
    mid = mgrad

    @pl.when(f == 0)
    def _():
        if plan:
            begin()
        slots = oT.shape[0]
        branch = jnp.concatenate([dot(oT[i], flat(wo[...]), 0, 0) for i in range(slots)], axis=0)
        x = tok[...].astype(F32) + branch + rows[2:3, :]
        mid[...] = x
        xhat, _ = stats(x)
        n2[...] = (xhat * rows[4:5, :] + rows[5:6, :]).astype(BF16)
        oacc[...] = x + rows[6:7, :]
        if plan:
            then()

    talk(schedule, f, 0, 4)
    v = dot(n2[...], flat(weight()[..., :CHUNK]), 1, 0) + ub[0:1, :]
    ga = dot(g_[...], flat(weight()[..., CHUNK:]), 1, 0)
    v2 = v * v
    t = jnp.tanh(v * (GELU_A + GELU_B * v2))
    p = 0.5 * t + 0.5
    act[...] = (v * p).astype(BF16)
    slope = p + (0.5 * v) * (1.0 - t * t) * (GELU_A + (3.0 * GELU_B) * v2)
    low = (slope * ga).astype(BF16)
    hg[...] = low
    dub[...] = jnp.sum(low.astype(F32), axis=0, keepdims=True)
    talk(schedule, f, 1, 4)
    oacc[...] += dot(act[...], flat(weight()[..., CHUNK:]), 1, 1)
    dn = dot(hg[...], flat(weight()[..., :CHUNK]), 1, 1)

    @pl.when(f == 0)
    def _():
        dacc[...] = dn

    @pl.when(f > 0)
    def _():
        dacc[...] += dn

    talk(schedule, f, 2, 4)
    for point, cols, a, b in ((3, slice(0, CHUNK), n2, hg), (None, slice(CHUNK, None), g_, act)):
        grad = dot(a[...], b[...], 0, 0)
        if plan:
            w[f, :, :, :, :, cols] = unflat(grad, w.shape[1:4]).astype(BF16)
        else:
            dw[0, :, cols] = grad.astype(BF16)
        if point:
            talk(schedule, f, point, 4)

    @pl.when(f == last)
    def _():
        if plan:
            for call in finish[0]:
                call()
        out[...] = oacc[...].astype(BF16)
        xhat, rstd = stats(mid[...])
        dn = dacc[...]
        gf = g_[...].astype(F32)
        mg = gf + ln_back(dn, rows[4:5, :], xhat, rstd)
        mgrad[...] = mg
        low = mg.astype(BF16)
        small[4:5, :] = jnp.sum(dn * xhat, axis=0, keepdims=True)
        small[5:6, :] = jnp.sum(dn, axis=0, keepdims=True)
        small[6:7, :] = jnp.sum(gf, axis=0, keepdims=True)
        small[2:3, :] = jnp.sum(low.astype(F32), axis=0, keepdims=True)
        small[0:2, :] = jnp.zeros_like(small[0:2, :])
        small[3:4, :] = jnp.zeros_like(small[3:4, :])
        small[7:8, :] = jnp.zeros_like(small[7:8, :])
        slots, t = oT.shape[0], oT.shape[2]
        go = dot(oT[0], mg[:t].astype(BF16), 1, 0)
        for i in range(1, slots):
            go += dot(oT[i], mg[i * t:(i + 1) * t].astype(BF16), 1, 0)
        dwo[...] = (unflat(go, dwo.shape[:3]) if plan else go).astype(BF16)
        if plan:
            for call in finish[1]:
                call()


def mlp(mesh, tok, oT, wo, g, rows, urow, args, hand):
    t, d = tok.shape
    ff = urow.shape[1]
    count = ff // CHUNK
    fixed = lambda s: pl.BlockSpec(s, lambda f: (0,) * len(s), pipeline_mode=pl.Buffered(1))
    col = lambda h: pl.BlockSpec((h, CHUNK), lambda f: (0, f))
    specs = [fixed((t, d)), fixed((t, d)), fixed((8, d)), col(1), fixed(wo.shape)]
    shapes = [SD((t, d), BF16), SD((t, d), F32), SD((8, d), F32), SD((1, ff), F32), SD(wo.shape, BF16)]
    scratch = [pltpu.VMEM((t, d), BF16), pltpu.VMEM((t, CHUNK), BF16), pltpu.VMEM((t, CHUNK), BF16), pltpu.VMEM((t, d), F32), pltpu.VMEM((t, d), F32)]
    plan, params = None, {}
    if hand:
        dp, fsdp = mesh.shape["dp"], mesh.shape["fsdp"]
        chunks, up, dnT = args
        *n, r, w2 = chunks.shape[1:]
        plan = dp, fsdp, count
        in_specs = [ANY] * 3
        specs += [ANY, fixed((EARLY, r, w2))]
        shapes += [SD((count - EARLY, *n, r, w2), BF16), SD((EARLY, r, w2), F32)]
        scratch = [pltpu.VMEM((count, *n, r, w2), BF16), pltpu.SemaphoreType.DMA((2 * (count - FIRST) + count,)), *scratch]
        scratch += Gather.scratch(fsdp) * (count - FIRST) + Scatter.scratch(fsdp, r, w2, BF16) * EARLY
        params = dict(collective_id=1, has_side_effects=True)
    else:
        wide = pl.BlockSpec((1, d, 2 * CHUNK), lambda f: (f, 0, 0))
        in_specs = [wide]
        specs += [wide]
        shapes += [SD((count, d, 2 * CHUNK), BF16)]
    return pl.pallas_call(
        functools.partial(mlp_kernel, plan),
        grid=(count,),
        in_specs=[fixed((t, d)), fixed(oT.shape), fixed(wo.shape), fixed((t, d)), fixed((8, d)), col(8), *in_specs],
        out_specs=specs, out_shape=shapes, scratch_shapes=scratch,
        compiler_params=pltpu.CompilerParams(vmem_limit_bytes=62 * 2**20, **params),
        name="mlp",
    )(tok, oT, wo, g, rows, urow, *args)


def attn_bwd_kernel(plan, *refs):
    sides, tok, mgrad, w, wo, rows, qT, kT, vT, eT, linv, oT, cosT, sinT, *refs = refs
    quad, slot = pl.program_id(0), pl.program_id(1)
    lastq, lasts = pl.num_programs(0) - 1, pl.num_programs(1) - 1
    step = quad * pl.num_programs(1) + slot
    schedule = {}
    tail = [[]] * 3
    if plan:
        dp, fsdp = plan
        small2, dub, dwo, late, tgrad, gqkv, go, gs, gl, *refs = refs
        n1, dacc, mg, vec, qb, px, po, pq, ps, local, *refs = refs
        g = Grid(dp, fsdp)
        count = late.shape[0]
        loads = [pltpu.make_async_copy(late.at[i], px.at[i], local.at[i]) for i in range(count)] + [pltpu.make_async_copy(dwo, po, local.at[count])]
        units = []

        def unit(part, write):
            nonlocal refs
            units.append(Scatter(g, part, write, refs[:6], refs[6]))
            refs = refs[7:]
            return units[-1]

        def into(ref, i=None):
            def write(s):
                if i is None:
                    ref[...] = s
                else:
                    ref[i] = s
            return write
        x = [unit(px.at[i], into(gl, i)) for i in range(count)]
        o = unit(po, into(go))

        def quads(i, js):
            def write(s):
                for j in js:
                    gqkv[:, (j * GROUPS + i) * GW:(j * GROUPS + i + 1) * GW] = s[:, (j - js[0]) * GW:(j - js[0] + 1) * GW]
            return write
        q = [unit(pq.at[i], quads(i, (0, 1, 2))) for i in range(GROUPS - 1)]
        q += [unit(pq.at[GROUPS - 1, :, :, :, :, pl.ds(js[0] * GW, len(js) * GW)], quads(GROUPS - 1, js)) for js in ENDS]
        sm = Direct(g, ps, gs, refs[:2], refs[2])

        def begin():
            for m in loads:
                m.start()
            greet(g, True)

        def then():
            met(g, True)
            loads[-1].wait()
            o.B_()

        schedule = {
            0: [loads[0].wait, x[0].B_],
            2: [loads[1].wait, x[1].B_],
            3: [x[0].F, o.F],
            6: [q[0].B_],
            7: [x[0].N],
            8: [q[0].F, o.N],
            9: [x[1].F],
            12: [q[1].B_, o.O],
            13: [x[1].N],
            14: [q[1].F],
            15: [q[0].N, x[0].O],
            16: [q[1].N],
            17: [x[1].O, q[0].O],
        }
        tail = [[q[2].B_, q[3].B_], [q[2].F, q[3].F, q[1].O, o.E],
                [sm.B_, q[2].N, q[3].N, x[0].E, sm.O, x[1].E, q[0].E, q[1].E, q[2].O, q[3].O, sm.E, q[2].E, q[3].E]]
        weight = lambda: flat(w[0])
    else:
        tgrad, dwqkv, vec, qb, n1, dacc, mg = refs
        weight = lambda: flat(w[0])
    t = tok.shape[1]

    @pl.when(step == 0)
    def _():
        if plan:
            begin()
        for i in range(tok.shape[0]):
            xhat, _ = stats(tok[i].astype(F32))
            n1[i] = (xhat * rows[0:1, :] + rows[1:2, :]).astype(BF16)
        vec[...] = small2[...] if plan else jnp.zeros_like(vec)
        qb[...] = jnp.zeros_like(qb)
        if plan:
            then()

    talk(schedule, step, 0, 3)
    _, height, across = places(sides, slot, t)
    ml = mgrad[slot].astype(BF16)
    wo_q = pl.ds(pl.multiple_of(quad * GW, GW), GW)
    dO = dot(wo[wo_q], ml, 1, 1)
    dqs, dks, dvs, angs = [], [], [], []
    for h in range(GROUP):
        if h == GROUP // 2:
            talk(schedule, step, 1, 3)
        lo, mi, hi = h * HD, h * HD + HALF, (h + 1) * HD
        c_, s_ = cosT[0, h * HALF:(h + 1) * HALF], sinT[0, h * HALF:(h + 1) * HALF]
        dof = dO[lo:hi] * linv[0, h:h + 1]
        do = dof.astype(BF16)
        dd = jnp.sum(dof * oT[0, lo:hi].astype(F32), axis=0, keepdims=True)
        dp_ = dot(vT[0, lo:hi], do, 0, 0)
        e = eT[h]
        ds = (e.astype(F32) * (dp_ - dd)).astype(BF16)
        dvs.append(dot(do, e, 1, 1))
        dk = dot(qT[0, lo:hi], ds, 1, 1)
        dq = dot(kT[0, lo:hi], ds, 1, 0)
        k = kT[0, lo:hi].astype(F32)
        q_ = qT[0, lo:hi].astype(F32)
        angs.append(dq[HALF:] * q_[:HALF] - dq[:HALF] * q_[HALF:] + dk[HALF:] * k[:HALF] - dk[:HALF] * k[HALF:])
        dq = dq * SCALE
        dqs += [dq[:HALF] * c_ + dq[HALF:] * s_, dq[HALF:] * c_ - dq[:HALF] * s_]
        dks += [dk[:HALF] * c_ + dk[HALF:] * s_, dk[HALF:] * c_ - dk[:HALF] * s_]
    m = jnp.concatenate(dqs + dks + dvs, axis=0).astype(BF16)
    mg[slot] = m
    ang = jnp.concatenate(angs, axis=0)
    j8 = lax.broadcasted_iota(jnp.int32, (8, t), 0)
    where = jnp.where(j8 == 0, height, jnp.where(j8 == 1, across, 0.0)).astype(BF16)
    big = ang.astype(BF16)
    fr = dot(where, big, 1, 1) + dot(where, (ang - big.astype(F32)).astype(BF16), 1, 1)
    d = vec.shape[1]
    for a in range(2):
        at = pl.ds(pl.multiple_of(a * (d // 2) + quad * (GW // 2), GW // 2), GW // 2)
        vec[3:4, at] += fr[a:a + 1]
    bias = dot(jnp.ones((8, t), BF16), m, 1, 1)[0:1]
    for j in range(3):
        at = pl.ds(pl.multiple_of(j * d + quad * GW, GW), GW)
        qb[0:1, at] += bias[:, j * GW:(j + 1) * GW]
    talk(schedule, step, 2, 3)

    @pl.when(slot == lasts)
    def _():
        gw = dot(n1[0], mg[0], 0, 1)
        for i in range(1, n1.shape[0]):
            gw += dot(n1[i], mg[i], 0, 1)
        if plan:
            pq[quad] = unflat(gw, pq.shape[1:4]).astype(BF16)
        else:
            dwqkv[0] = gw.astype(BF16)

    if plan:
        @pl.when((quad == lastq) & (slot == lasts))
        def _():
            for call in tail[0]:
                call()

    def gradient(i):
        return dot(mg[i], weight(), 0, 1)

    @pl.when(quad == 0)
    def _():
        dacc[slot] = gradient(slot)

    @pl.when((quad > 0) & (quad < lastq))
    def _():
        dacc[slot] += gradient(slot)

    @pl.when((quad == lastq) & (slot == lasts))
    def _():
        def end(i, carry):
            xhat, rstd = stats(tok[i].astype(F32))
            dn = dacc[i] + gradient(i)
            tgrad[i] = (mgrad[i] + ln_back(dn, rows[0:1, :], xhat, rstd)).astype(BF16)
            vec[0:1, :] += jnp.sum(dn * xhat, axis=0, keepdims=True)
            vec[1:2, :] += jnp.sum(dn, axis=0, keepdims=True)

            @pl.when(i == 0)
            def _():
                for call in tail[1]:
                    call()
            return carry
        lax.fori_loop(0, tok.shape[0], end, 0)
        if plan:
            cs, zs = ps.shape[1:3]

            def store(i, x):
                ps[i // (cs * zs), i // zs % cs, i % zs] = x
            spread(vec[...], qb[0:1, :], dub[...], dp * fsdp, store)
        for call in tail[2]:
            call()


def attn_bwd(mesh, sides, tok, mgrad, w, wo, rows, saved, args, hand):
    slots, t, d = tok.shape
    fixed = lambda s: pl.BlockSpec(s, lambda i, j: (0,) * len(s), pipeline_mode=pl.Buffered(1))
    tr = pl.BlockSpec((1, GW, t), lambda i, j: (j, i, 0))
    trh = pl.BlockSpec((1, GW // 2, t), lambda i, j: (j, i, 0))
    block = lambda s: pl.BlockSpec((1, *s[1:]), lambda i, j: (i,) + (0,) * (len(s) - 1))
    specs = [fixed(tok.shape)]
    shapes = [SD(tok.shape, BF16)]
    scratch = [pltpu.VMEM((slots, t, d), BF16), pltpu.VMEM((slots, t, d), F32), pltpu.VMEM((slots, 3 * GW, t), BF16)]
    vec, qb = (8, d), (8, 3 * d)
    plan, params = None, {}
    if hand:
        dp, fsdp = mesh.shape["dp"], mesh.shape["fsdp"]
        small2, dub, dwo, late = args
        *n, r, _ = dwo.shape
        plan = dp, fsdp
        in_specs = [fixed(small2.shape), fixed(dub.shape), ANY, ANY]
        outs = [(r, 3 * d), (r, d), (16, LANES), (late.shape[0], *late.shape[4:])]
        specs += [fixed(s) for s in outs]
        shapes += [SD(s, F32) for s in outs]
        parts = [*[late.shape[1:]] * late.shape[0], dwo.shape, *[(*n, r, 3 * GW)] * (GROUPS - 1), *[(*n, r, len(js) * GW) for js in ENDS]]
        scratch += [pltpu.VMEM(vec, F32), pltpu.VMEM(qb, F32), pltpu.VMEM(late.shape, BF16), pltpu.VMEM(dwo.shape, BF16),
                    pltpu.VMEM((GROUPS, *n, r, 3 * GW), BF16), pltpu.VMEM((*n, 16, LANES), F32), pltpu.SemaphoreType.DMA((late.shape[0] + 1,))]
        scratch += [y for s in parts for y in Scatter.scratch(fsdp, s[3], s[4], BF16)] + Direct.scratch(fsdp, 16, LANES, F32)
        params = dict(collective_id=2, has_side_effects=True)
    else:
        in_specs = []
        specs += [block((GROUPS, d, 3 * GW)), fixed(vec), fixed(qb)]
        shapes += [SD((GROUPS, d, 3 * GW), BF16), SD(vec, F32), SD(qb, F32)]
    return pl.pallas_call(
        functools.partial(attn_bwd_kernel, plan),
        grid=(GROUPS, slots),
        in_specs=[pl.BlockSpec(memory_space=pltpu.SMEM), fixed(tok.shape), fixed(tok.shape), block(w.shape), fixed((d, d)), fixed((8, d)),
                  tr, tr, tr, pl.BlockSpec((GROUP, t, t), lambda i, j: (j * GROUPS + i, 0, 0)), pl.BlockSpec((1, 8, t), lambda i, j: (j * GROUPS + i, 0, 0)),
                  tr, trh, trh, *in_specs],
        out_specs=specs, out_shape=shapes, scratch_shapes=scratch,
        compiler_params=pltpu.CompilerParams(vmem_limit_bytes=62 * 2**20, **params),
        name="attn_bwd",
    )(sides, tok, mgrad, w, wo, rows, *saved, *args)


def lay_out_kernel(r, widths, gqkv, go, gs, early, late, an_o, qkv_o, bq_o, o_o, bo_o, f_o, mn_o, up_o, bu_o, dT_o, bd_o):
    qkv_o[...] = gqkv[...]
    o_o[...] = go[...]
    for f, ref in enumerate([early.at[i] for i in range(early.shape[0])] + [late.at[i] for i in range(late.shape[0])]):
        up_o[:, f * CHUNK:(f + 1) * CHUNK] = ref[:, :CHUNK]
        dT_o[:, f * CHUNK:(f + 1) * CHUNK] = ref[:, CHUNK:]
    nb, nu = widths
    an_o[...] = gs[0:2, :r]
    bo_o[...] = gs[2:3, :r]
    f_o[...] = gs[3:4, :r]
    mn_o[...] = gs[4:6, :r]
    bd_o[...] = gs[6:7, :r]
    bq_o[...] = gs[7:8, :nb]
    bu_o[...] = gs[8:9, :nu]


def lay_out(gqkv, go, gs, early, late, nb, nu):
    r, d = go.shape
    ff = (early.shape[0] + late.shape[0]) * CHUNK
    one = lambda w: SD((1, w), F32)
    vm = pl.BlockSpec(memory_space=pltpu.VMEM)
    shapes = [SD((2, r), F32), SD(gqkv.shape, F32), one(nb), SD(go.shape, F32), one(r), one(r), SD((2, r), F32),
              SD((r, ff), F32), one(nu), SD((r, ff), F32), one(r)]
    res = pl.pallas_call(
        functools.partial(lay_out_kernel, r, (nb, nu)),
        in_specs=[vm] * 5, out_specs=[vm] * 11, out_shape=shapes, name="lay_out",
    )(gqkv, go, gs, early, late)
    res = list(res)
    res[9] = res[9].T
    return tuple(x.reshape(-1) if x.shape[0] == 1 else x for x in res)


def on_device(mesh, tok, sides, g, attn_norm, wqkv, bqkv, wo, bo, freq, mlp_norm, up, ub, down, db):
    n = mesh.shape["dp"] * mesh.shape["fsdp"]
    slots = sides.shape[0]
    d = tok.shape[1]
    t = tok.shape[0] // slots
    r = wqkv.shape[0]
    ff = up.shape[1]
    nb, nu = bqkv.shape[0] // r, ub.shape[0] // r
    count = ff // CHUNK
    hand = mesh.shape["dp"] == 8 and r % 8 == 0 and count == 6
    dnT = down.T
    small = [x.reshape(-1, x.shape[-1]) for x in (attn_norm, bo, freq, mlp_norm, db, bqkv, ub)]
    t3 = tok.reshape(slots, t, d)
    if hand:
        *saved, rows, urow, wqkv, wo, chunks = attn_fwd(mesh, sides, t3, (wqkv, wo, up, dnT, *small), True)
        out, mgrad, small2, dub, dwo, late, early = mlp(mesh, tok, saved[5], wo, g, rows, urow, (chunks, up, dnT), True)
        tg, gqkv, go, gs, gl = attn_bwd(mesh, sides, t3, mgrad.reshape(t3.shape), wqkv, wo.reshape(d, d), rows, saved, (small2, dub, dwo, late), True)
        return (out, tg.reshape(-1, d)) + lay_out(gqkv, go, gs, early, gl, nb * r, nu * r)
    else:
        whole = lambda x: lax.all_gather(x, BOTH, axis=0, tiled=True)
        wqkv, wo, up, dnT = (whole(x) for x in (wqkv, wo, up, dnT))
        small = jnp.concatenate([jnp.pad(x, ((0, 0), (0, LANES - x.shape[1]))) for x in small] + [jnp.zeros((7, LANES), BF16)], axis=0)
        small = lax.all_gather(small, BOTH, axis=0).astype(F32)
        wide = lambda i, k: small[:, i, :k * r].reshape(1, k * d)
        rows = small[:, :8, :r].transpose(1, 0, 2).reshape(8, d)
        urow = jnp.broadcast_to(wide(8, nu), (8, nu * d))
        w = wqkv.reshape(d, 3, GROUPS, GW).transpose(2, 0, 1, 3).reshape(GROUPS, d, 3 * GW)
        saved = attn_fwd(mesh, sides, t3, (w, rows, wide(7, nb).T, rows[3:4].T), False)
        chunks = jnp.stack([up.reshape(d, count, CHUNK), dnT.reshape(d, count, CHUNK)], axis=2).transpose(1, 0, 2, 3).reshape(count, d, 2 * CHUNK)
        out, mgrad, small2, dub, dwo, dw = mlp(mesh, tok, saved[5], wo, g, rows, urow, (chunks,), False)
        tg, dwqkv, vec, qb = attn_bwd(mesh, sides, t3, mgrad.reshape(t3.shape), w, wo, rows, saved, (), False)
        total = lambda x, ax: lax.psum_scatter(x.astype(F32), BOTH, scatter_dimension=ax, tiled=True)
        gqkv = total(dwqkv.reshape(GROUPS, d, 3, GW).transpose(1, 2, 0, 3).reshape(d, 3 * d), 0)
        go = total(dwo, 0)
        both = total(dw, 1)
        cut = lambda x: jnp.pad(x.reshape(x.shape[0], n, -1).transpose(1, 0, 2), ((0, 0), (0, 0), (0, LANES - x.shape[1] // n)))
        gs = total(jnp.concatenate([cut((vec + small2)[:7]), cut(qb[:1]), cut(dub), jnp.zeros((n, 7, LANES), F32)], axis=1), 0)[0]
    gup = both[:, :, :CHUNK].transpose(1, 0, 2).reshape(r, ff)
    gdT = both[:, :, CHUNK:].transpose(1, 0, 2).reshape(r, ff)
    return (out, tg.reshape(-1, d), gs[0:2, :r], gqkv, gs[7, :nb * r], go, gs[2, :r], gs[3, :r], gs[4:6, :r], gup, gs[8, :nu * r], gdT.T, gs[6, :r])


def solution(mesh):
    row, col, one = P(BOTH, None), P(None, BOTH), P(BOTH)
    return jax.shard_map(
        functools.partial(on_device, mesh), mesh=mesh,
        in_specs=(row, row, row, col, row, one, row, one, one, col, row, one, col, one),
        out_specs=(row, row, col, row, one, row, one, one, col, row, one, col, one),
        check_vma=False,
    )
```
